32 devices in a mesh: row: 4 (over y, x), col: 8 (over z, core).
Axes of the slice: x: 2, y: 2, z: 4, core: 2. Of those that a mesh axis runs over, the one named last changes fastest.
Arguments:
- row_emb: float32 [16, 512, 256], P('row', 'col'), may hold values from -1.8 to 1.8
- col_emb: float32 [32, 512, 256], P('col', 'row'), may hold values from -1.8 to 1.8
- row_marg: bfloat16 [16, 512], P('row', 'col'), may hold values from 0.5 to 3
- col_marg: bfloat16 [32, 512], P('col', 'row'), may hold values from 0.5 to 3
- tile_list: int32 [4, 8, 8, 2], P('row', 'col'), may hold values from 0 to 31, as said below
- tile_count: int32 [4, 8], P('row', 'col'), may hold values from 1 to 8, as said below
- tile_data: int32 [4, 8, 8, 512, 512], P('row', 'col'), may hold values from 0 to 215
Outputs:
- row_new: float32 [16, 512, 256], P('row', 'col')
- col_new: float32 [32, 512, 256], P('col', 'row')
The draws below stay inside these ranges and needn't reach their ends.
Inputs may be any that keep to these rules, and one draw needn't show every extreme that they name: `tile_list`: the slots of device (r, c) name distinct tiles with row block in r * 4 to (r + 1) * 4 - 1 and column block in c * 4 to (c + 1) * 4 - 1; slots at or past the device's tile_count are not used. `tile_count`: some device uses all 8 slots.
All inputs are finite; a program needn't handle non-finite values.
Results may differ from the reference program's by a relative error of at most 0.012.
Values may be sent and summed in bfloat16 or wider, within the bound.
No kernel may reach another device: no remote copies, remote signals or barrier semaphores. Data moves between devices by JAX's collectives and lax.ppermute only.
A program may use at most 64 MiB of HBM per device.

```python
import jax
import jax.numpy as jnp
from jax import lax

K = 256
B = 512
RB_DEV = 4
CB_DEV = 4
SLOTS = 8
NRB = 16
NCB = 32


def tile_plan(key):
    base = jax.random.fold_in(key, 7)
    n_row = NRB // RB_DEV
    n_col = NCB // CB_DEV
    devices = n_row * n_col
    keys = jax.random.split(base, devices)
    orders = jax.vmap(lambda k: jax.random.permutation(k, RB_DEV * CB_DEV))(keys)[:, :SLOTS]
    device_ids = jnp.arange(devices, dtype=jnp.int32)
    row_start = device_ids // n_col * RB_DEV
    col_start = device_ids % n_col * CB_DEV
    global_rows = row_start[:, None] + orders // CB_DEV
    global_cols = col_start[:, None] + orders % CB_DEV
    listing = jnp.stack([global_rows, global_cols], -1).astype(jnp.int32).reshape(n_row, n_col, SLOTS, 2)
    first = jax.random.randint(jax.random.fold_in(base, 1), (devices,), 1, SLOTS + 1)
    second = jax.random.randint(jax.random.fold_in(base, 2), (devices,), 1, SLOTS + 1)
    loads = jnp.maximum(first * second // SLOTS, 1)
    busiest = jax.random.randint(jax.random.fold_in(base, 3), (), 0, devices)
    loads = jnp.where(device_ids == busiest, SLOTS, loads).astype(jnp.int32).reshape(n_row, n_col)
    return (listing, loads)


def draw_tile_list(key, part):
    return tile_plan(key)[0]


def draw_tile_count(key, part):
    return tile_plan(key)[1]


def draw_tile_data(key, part):
    n_row = NRB // RB_DEV
    n_col = NCB // CB_DEV
    raw = jax.random.randint(jax.random.fold_in(key, 11), (n_row, n_col, SLOTS, B, B), 0, 1024)
    return jnp.maximum(raw * raw // 4096 - 40, 0).astype(jnp.int32)


def levels(key, dims, cuts, smallest, high):
    factor_of, own = 1.0, jax.random.fold_in(key, 6)
    for axis_at, shards_of in cuts:
        draws = jnp.exp(jax.random.uniform(jax.random.fold_in(own, axis_at), (shards_of,), jnp.float32, smallest / len(cuts), high / len(cuts)))
        factor_of = factor_of * jnp.repeat(draws, dims[axis_at] // shards_of).reshape([-1 if axis == axis_at else 1 for axis in range(len(dims))])
    return factor_of


def normal_values(stream_key, extent, scale, most, cuts=(), held_as=jnp.bfloat16):
    loudness = levels(stream_key, extent, cuts, -0.22, 0.18) if cuts else 1.0
    result = jax.random.normal(stream_key, extent, jnp.float32) * scale * loudness
    return jnp.minimum(jnp.maximum(result, -most), most).astype(held_as)


def setup_inputs(seed: int = 0) -> dict:
    key_list = jax.random.split(jax.random.key(seed), 8)
    return {
        "row_emb": normal_values(key_list[0], (NRB, B, K), 0.3, 1.8, ((0, 4), (1, 8)), jnp.float32),
        "col_emb": normal_values(key_list[1], (NCB, B, K), 0.3, 1.8, ((0, 8), (1, 4)), jnp.float32),
        "row_marg": jnp.clip(0.5 + 2.5 * jax.random.uniform(key_list[2], (NRB, B), jnp.float32) ** levels(key_list[2], (NRB, B), ((0, 4), (1, 8)), -0.2, 0.2), 0.5, 3.0).astype(jnp.bfloat16),
        "col_marg": jnp.clip(0.5 + 2.5 * jax.random.uniform(key_list[3], (NCB, B), jnp.float32) ** levels(key_list[3], (NCB, B), ((0, 8), (1, 4)), -0.2, 0.2), 0.5, 3.0).astype(jnp.bfloat16),
        "tile_list": draw_tile_list(jax.random.fold_in(key_list[7], 71), 0),
        "tile_count": draw_tile_count(jax.random.fold_in(key_list[7], 71), 0),
        "tile_data": draw_tile_data(jax.random.fold_in(key_list[7], 71), 0),
    }


def tile_signal(scores, counts, marg_left, marg_right):
    level = counts.astype(jnp.float32)
    diff = scores - (jnp.log(jnp.maximum(level, 1.0)) - marg_left[:, None] - marg_right[None, :])
    weight = 0.1 + 0.25 * jnp.sqrt(level)
    return jnp.where(level > 0.0, weight * diff, jax.nn.sigmoid(diff))

def substep(row_emb, col_emb, row_marg, col_marg, tile_list, tile_count, tile_data):
    row_panel = row_emb.astype(jnp.bfloat16)
    col_panel = col_emb.astype(jnp.bfloat16)
    row_margf = row_marg.astype(jnp.float32)
    col_margf = col_marg.astype(jnp.float32)
    flat_list = tile_list.reshape(-1, 2)
    flat_data = tile_data.reshape(-1, B, B)
    slot_ids = jnp.arange(SLOTS, dtype=jnp.int32)
    usable = (slot_ids[None, None, :] < tile_count[:, :, None]).reshape(-1)

    def one_tile(carry, item):
        grad_row, grad_col = carry
        pair, counts, valid = item
        i = pair[0].astype(jnp.int32)
        j = pair[1].astype(jnp.int32)
        row_piece = lax.dynamic_index_in_dim(row_panel, i, 0, keepdims=False)
        col_piece = lax.dynamic_index_in_dim(col_panel, j, 0, keepdims=False)
        scores = lax.dot_general(row_piece, col_piece, (((1,), (1,)), ((), ())), preferred_element_type=jnp.float32)
        marg_left = lax.dynamic_index_in_dim(row_margf, i, 0, keepdims=False)
        marg_right = lax.dynamic_index_in_dim(col_margf, j, 0, keepdims=False)
        signal = tile_signal(scores, counts, marg_left, marg_right).astype(jnp.bfloat16)
        row_term = jnp.dot(signal, col_piece, preferred_element_type=jnp.float32)
        col_term = lax.dot_general(signal, row_piece, (((0,), (0,)), ((), ())), preferred_element_type=jnp.float32)
        row_term = jnp.where(valid, row_term, jnp.zeros_like(row_term))
        col_term = jnp.where(valid, col_term, jnp.zeros_like(col_term))
        return ((grad_row.at[i].add(row_term), grad_col.at[j].add(col_term)), None)
    start = (jnp.zeros(row_emb.shape, jnp.float32), jnp.zeros(col_emb.shape, jnp.float32))
    (grad_row, grad_col), _ = lax.scan(one_tile, start, (flat_list, flat_data, usable))
    return (row_emb - 0.0004 * grad_row, col_emb - 0.0004 * grad_col)

def reference(row_emb, col_emb, row_marg, col_marg, tile_list, tile_count, tile_data):
    for substep_index in range(2):
        row_emb, col_emb = substep(row_emb, col_emb, row_marg, col_marg, tile_list, tile_count, tile_data)
    return (row_emb, col_emb)
```

```python
import functools

import jax
import jax.numpy as jnp
from jax import lax
from jax.experimental import pallas as pl
from jax.experimental.pallas import tpu as pltpu
from jax.sharding import PartitionSpec as P

RATE = 0.0004
MARG_ROWS = 16
MARG_LANES = 128
ANY = pl.BlockSpec(memory_space=pl.ANY)
VMEM = pl.BlockSpec(memory_space=pltpu.VMEM)
SMEM = pl.BlockSpec(memory_space=pltpu.SMEM)


def pack_kernel(row_emb, row_marg, col_emb, col_marg, row_out, col_out):
    for emb, marg, out in ((row_emb, row_marg, row_out), (col_emb, col_marg, col_out)):
        blocks, part, width = emb.shape
        out[: blocks * part, :] = emb[...].astype(jnp.bfloat16).reshape(blocks * part, width)
        out[blocks * part :, :] = jnp.zeros((MARG_ROWS, width), jnp.bfloat16)
        for b in range(blocks):
            out[blocks * part + b : blocks * part + b + 1, :part] = marg[b : b + 1, :]


def pack(row_emb, row_marg, col_emb, col_marg):
    outs = [
        jax.ShapeDtypeStruct((e.shape[0] * e.shape[1] + MARG_ROWS, e.shape[2]), jnp.bfloat16)
        for e in (row_emb, col_emb)
    ]
    return pl.pallas_call(
        pack_kernel,
        out_shape=outs,
        in_specs=[VMEM] * 4,
        out_specs=[VMEM] * 2,
        cost_estimate=pl.CostEstimate(flops=0, bytes_accessed=2 << 20, transcendentals=0),
    )(row_emb, row_marg, col_emb, col_marg)


def marg_table(pieces, owners, part, size):
    table = jnp.zeros((MARG_ROWS, size), jnp.float32)
    for n, owner in enumerate(owners):
        k = lax.broadcasted_iota(jnp.int32, (MARG_LANES, size), 0)
        at = lax.broadcasted_iota(jnp.int32, (MARG_LANES, size), 1)
        place = ((at == k + owner * part) & (k < part)).astype(jnp.bfloat16)
        table += jnp.dot(pieces[n, :, :MARG_LANES], place, preferred_element_type=jnp.float32)
    return table


def work_kernel(n_row, n_col, row_owner, col_owner, row_base, col_base, *refs):
    refs = list(refs)
    take = lambda n: [refs.pop(0) for _ in range(n)]
    listing, used, tiles = take(3)
    row_in, col_in, row_tail, col_tail = take(n_row), take(n_col), take(n_row), take(n_col)
    keep, swap, col_out = take(1)[0], take(1)[0], take(n_col)
    row_panel, col_panel, row_margs, col_margs, left, right, grad_row, grad_col, tile_buf, signal = take(10)
    row_sem, col_sem, tile_sem = take(3)

    row_blocks, size, width = row_panel.shape
    col_blocks = col_panel.shape[0]
    row_part, col_part = size // n_row, size // n_col
    me_row, me_col = lax.axis_index("row"), lax.axis_index("col")
    row_owners = [me_col ^ k for k in row_owner]
    col_owners = [me_row ^ k for k in col_owner]
    row_zero, col_zero = me_row * row_blocks, me_col * col_blocks
    count = used[0]

    def tile_copy(slot):
        at = lax.rem(slot, 2)
        return pltpu.make_async_copy(tiles.at[slot], tile_buf.at[at], tile_sem.at[at])

    tile_copy(0).start()

    copies = []
    for pieces, tails, owners, panel, margs, part, sem in (
        (row_in, row_tail, row_owners, row_panel, row_margs, row_part, row_sem),
        (col_in, col_tail, col_owners, col_panel, col_margs, col_part, col_sem),
    ):
        blocks = panel.shape[0]
        for n, owner in enumerate(owners):
            start = pl.multiple_of(owner * part, part)
            for b in range(blocks):
                copies.append(
                    pltpu.make_async_copy(
                        pieces[n].at[pl.ds(b * part, part)],
                        panel.at[b, pl.ds(start, part)],
                        sem.at[n, b],
                    )
                )
            copies.append(
                pltpu.make_async_copy(
                    tails[n].at[pl.ds(blocks * part, MARG_ROWS)], margs.at[n], sem.at[n, blocks]
                )
            )
    for copy in copies:
        copy.start()
    grad_row[...] = jnp.zeros_like(grad_row)
    grad_col[...] = jnp.zeros_like(grad_col)
    for copy in copies:
        copy.wait()

    row_table = marg_table(row_margs, row_owners, row_part, size).astype(jnp.bfloat16)
    for b in range(row_blocks):
        pick = (lax.broadcasted_iota(jnp.int32, (MARG_ROWS, 128), 0) == b).astype(jnp.bfloat16)
        left[b] = lax.dot_general(
            row_table, pick, (((0,), (0,)), ((), ())), preferred_element_type=jnp.float32
        )
    col_table = marg_table(col_margs, col_owners, col_part, size)
    for b in range(col_blocks):
        right[b] = jnp.broadcast_to(col_table[b : b + 1, :], right.shape[1:])

    chunk = 256

    def one_tile(slot, carry):
        at = lax.rem(slot, 2)

        @pl.when(slot + 1 < count)
        def _():
            tile_copy(slot + 1).start()

        tile_copy(slot).wait()
        i = listing[2 * slot] - row_zero
        j = listing[2 * slot + 1] - col_zero
        col_piece = col_panel[j]
        marg_right = right[j, 0:1, :]
        for begin in range(0, size, chunk):
            rows = slice(begin, begin + chunk)
            scores = lax.dot_general(
                row_panel[i, rows, :],
                col_piece,
                (((1,), (1,)), ((), ())),
                preferred_element_type=jnp.float32,
            )
            counts = tile_buf[at, rows, :].astype(jnp.float32)
            level = jnp.maximum(counts, 1.0)
            marg_left = jnp.concatenate([left[i, rows, :]] * (size // 128), axis=1)
            diff = scores + marg_left + marg_right - jnp.log(level)
            weight = 0.1 + 0.25 * (level * lax.rsqrt(level))
            flat = 0.5 * jnp.tanh(0.5 * diff) + 0.5
            signal[rows, :] = jnp.where(counts > 0.0, weight * diff, flat).astype(jnp.bfloat16)
        grad_row[i] += jnp.dot(signal[...], col_piece, preferred_element_type=jnp.float32)
        grad_col[j] += lax.dot_general(
            signal[...], row_panel[i], (((0,), (0,)), ((), ())), preferred_element_type=jnp.float32
        )
        return carry

    lax.fori_loop(0, count, one_tile, 0)

    half = n_row // 2
    for n in range(n_row):
        start = pl.multiple_of(row_owners[n] * row_part, row_part)
        piece = grad_row[:, pl.ds(start, row_part), :]
        if n < half:
            keep[n] = piece
        else:
            swap[n - half] = piece.astype(jnp.bfloat16)
    for n in range(n_col):
        start = pl.multiple_of(col_owners[n] * col_part, col_part)
        col_out[n][...] = grad_col[:, pl.ds(start, col_part), :].astype(col_out[n].dtype)


def work(listing, used, tiles, row_in, col_in, row_tail, col_tail, row_owner, col_owner, dims):
    row_blocks, col_blocks, size, width = dims
    n_row, n_col = len(row_owner), len(col_owner)
    row_part, col_part = size // n_row, size // n_col
    half = n_row // 2
    f32, bf16 = jnp.float32, jnp.bfloat16
    shape = jax.ShapeDtypeStruct
    outs = [
        shape((half, row_blocks, row_part, width), f32),
        shape((half, row_blocks, row_part, width), bf16),
        shape((col_blocks, col_part, width), f32),
    ] + [shape((col_blocks, col_part, width), bf16)] * (n_col - 1)
    kernel = functools.partial(work_kernel, n_row, n_col, row_owner, col_owner, None, None)
    res = pl.pallas_call(
        kernel,
        out_shape=outs,
        in_specs=[SMEM, SMEM] + [ANY] * (1 + 2 * n_row + 2 * n_col),
        out_specs=[VMEM] * len(outs),
        scratch_shapes=[
            pltpu.VMEM((row_blocks, size, width), bf16),
            pltpu.VMEM((col_blocks, size, width), bf16),
            pltpu.VMEM((n_row, MARG_ROWS, width), bf16),
            pltpu.VMEM((n_col, MARG_ROWS, width), bf16),
            pltpu.VMEM((row_blocks, size, 128), f32),
            pltpu.VMEM((col_blocks, 8, size), f32),
            pltpu.VMEM((row_blocks, size, width), f32),
            pltpu.VMEM((col_blocks, size, width), f32),
            pltpu.VMEM((2, size, size), jnp.int32),
            pltpu.VMEM((size, size), bf16),
            pltpu.SemaphoreType.DMA((n_row, row_blocks + 1)),
            pltpu.SemaphoreType.DMA((n_col, col_blocks + 1)),
            pltpu.SemaphoreType.DMA((2,)),
        ],
        compiler_params=pltpu.CompilerParams(vmem_limit_bytes=40 << 20),
        cost_estimate=pl.CostEstimate(
            flops=8 * 6 * size * size * width, bytes_accessed=16 << 20, transcendentals=0
        ),
    )(listing, used, tiles, *row_in, *col_in, *row_tail, *col_tail)
    return res[0], res[1], res[2:]


def merge_kernel(keep, got, *outs):
    for n, out in enumerate(outs):
        out[...] = (keep[n] + got[n].astype(jnp.float32)).astype(out.dtype)


def merge(keep, got):
    n, *piece = keep.shape
    outs = [jax.ShapeDtypeStruct(tuple(piece), jnp.float32)]
    outs += [jax.ShapeDtypeStruct(tuple(piece), jnp.bfloat16)] * (n - 1)
    return pl.pallas_call(
        merge_kernel,
        out_shape=outs,
        in_specs=[VMEM] * 2,
        out_specs=[VMEM] * len(outs),
        cost_estimate=pl.CostEstimate(flops=0, bytes_accessed=2 << 20, transcendentals=0),
    )(keep, got)


def update_kernel(n_parts, emb, *refs):
    parts, outs = refs[:n_parts], refs[n_parts:]
    total = parts[0][...].astype(jnp.float32)
    for part in parts[1:]:
        total += part[...].astype(jnp.float32)
    new = emb[...] - RATE * total
    outs[0][...] = new
    if len(outs) > 1:
        outs[1][...] = new.astype(jnp.bfloat16).reshape(outs[1].shape)


def update(emb, parts, last):
    blocks, part, width = emb.shape
    outs = [jax.ShapeDtypeStruct(emb.shape, jnp.float32)]
    if not last:
        outs.append(jax.ShapeDtypeStruct((blocks * part, width), jnp.bfloat16))
    res = pl.pallas_call(
        functools.partial(update_kernel, len(parts)),
        out_shape=outs,
        in_specs=[VMEM] * (1 + len(parts)),
        out_specs=[VMEM] * len(outs),
        cost_estimate=pl.CostEstimate(flops=0, bytes_accessed=2 << 20, transcendentals=0),
    )(emb, *parts)
    return res if not last else (res[0], None)


def send(x, axis, count, mask):
    return lax.ppermute(x, axis, [(k, k ^ mask) for k in range(count)])


def shards(n_row_dev, n_col_dev, row_emb, col_emb, row_marg, col_marg, tile_list, tile_count, tile_data):
    listing = tile_list[0, 0].reshape(-1)
    used = tile_count[0]
    tiles = tile_data[0, 0]
    dims = (row_emb.shape[0], col_emb.shape[0], tiles.shape[-1], row_emb.shape[-1])
    half = n_col_dev // 2
    row_owner = [2 * k for k in range(half)] + [2 * k + 1 for k in range(half)]
    col_owner = list(range(n_row_dev))
    row_pay, col_pay = pack(row_emb, row_marg, col_emb, col_marg)
    row_tail = col_tail = None
    for substep in range(2):
        col_in = [col_pay] + [send(col_pay, "row", n_row_dev, k) for k in col_owner[1:]]
        row_in = [row_pay] + [send(row_pay, "col", n_col_dev, 2 * k) for k in range(1, half)]
        row_in += [send(piece, "col", n_col_dev, 1) for piece in row_in]
        if substep == 0:
            row_tail, col_tail = row_in, col_in
        keep, swap, col_out = work(
            listing, used, tiles, row_in, col_in, row_tail, col_tail, row_owner, col_owner, dims
        )
        got = send(swap, "col", n_col_dev, 1)
        col_parts = [col_out[0]] + [send(col_out[k], "row", n_row_dev, k) for k in col_owner[1:]]
        merged = merge(keep, got)
        row_parts = [merged[0]] + [send(merged[k], "col", n_col_dev, 2 * k) for k in range(1, half)]
        col_emb, col_pay = update(col_emb, col_parts, substep == 1)
        row_emb, row_pay = update(row_emb, row_parts, substep == 1)
    return (row_emb, col_emb)


def solution(mesh):
    placed = (
        P("row", "col", None),
        P("col", "row", None),
        P("row", "col"),
        P("col", "row"),
        P("row", "col", None, None),
        P("row", "col"),
        P("row", "col", None, None, None),
    )
    return jax.shard_map(
        functools.partial(shards, mesh.shape["row"], mesh.shape["col"]),
        mesh=mesh,
        in_specs=placed,
        out_specs=(P("row", "col", None), P("col", "row", None)),
        check_vma=False,
    )
```

```python
import functools

import jax
import jax.numpy as jnp
from jax import lax
from jax.experimental import pallas as pl
from jax.experimental.pallas import tpu as pltpu
from jax.sharding import PartitionSpec as P

RATE = 0.0004
MARG_ROWS = 16
MARG_LANES = 128
ANY = pl.BlockSpec(memory_space=pl.ANY)
HBM = pl.BlockSpec(memory_space=pltpu.HBM)
VMEM = pl.BlockSpec(memory_space=pltpu.VMEM)
SMEM = pl.BlockSpec(memory_space=pltpu.SMEM)
SMALL = 12 << 20
LARGE = 32 << 20
f32, bf16 = jnp.float32, jnp.bfloat16
shape = jax.ShapeDtypeStruct


def cost(flops, moved):
    return pl.CostEstimate(flops=flops, bytes_accessed=moved, transcendentals=0)


def pack_kernel(row_emb, row_marg, col_emb, col_marg, row_out, col_out):
    for emb, marg, out in ((row_emb, row_marg, row_out), (col_emb, col_marg, col_out)):
        blocks, part, width = emb.shape
        out[: blocks * part, :] = emb[...].astype(bf16).reshape(blocks * part, width)
        out[blocks * part :, :] = jnp.zeros((MARG_ROWS, width), bf16)
        for b in range(blocks):
            out[blocks * part + b : blocks * part + b + 1, :part] = marg[b : b + 1, :]


def pack(row_emb, row_marg, col_emb, col_marg):
    outs = [
        shape((e.shape[0] * e.shape[1] + MARG_ROWS, e.shape[2]), bf16) for e in (row_emb, col_emb)
    ]
    return pl.pallas_call(
        pack_kernel,
        out_shape=outs,
        in_specs=[VMEM] * 4,
        out_specs=[VMEM] * 2,
        compiler_params=pltpu.CompilerParams(vmem_limit_bytes=SMALL),
        cost_estimate=cost(0, 2 << 20),
    )(row_emb, row_marg, col_emb, col_marg)


def levels_kernel(used, tiles, logs, weights, tile_buf, log_buf, weight_buf, in_sem, out_sem):
    count = used[0]
    size = tile_buf.shape[-1]
    chunk = 64

    def load(slot):
        at = lax.rem(slot, 2)
        return pltpu.make_async_copy(tiles.at[slot], tile_buf.at[at], in_sem.at[at])

    def stores(slot):
        at = lax.rem(slot, 2)
        return (
            pltpu.make_async_copy(log_buf.at[at], logs.at[slot], out_sem.at[at, 0]),
            pltpu.make_async_copy(weight_buf.at[at], weights.at[slot], out_sem.at[at, 1]),
        )

    load(0).start()

    def one_tile(slot, carry):
        at = lax.rem(slot, 2)

        @pl.when(slot + 1 < count)
        def _():
            load(slot + 1).start()

        load(slot).wait()

        @pl.when(slot >= 2)
        def _():
            for copy in stores(slot - 2):
                copy.wait()

        def one_chunk(n, carry):
            rows = pl.ds(pl.multiple_of(n * chunk, chunk), chunk)
            counts = tile_buf[at, rows, :].astype(f32)
            level = jnp.maximum(counts, 1.0)
            log_buf[at, rows, :] = jnp.log(level)
            weight = 0.1 + 0.25 * (level * lax.rsqrt(level))
            weight_buf[at, rows, :] = jnp.where(counts > 0.0, weight, 0.0)
            return carry

        lax.fori_loop(0, size // chunk, one_chunk, 0)
        for copy in stores(slot):
            copy.start()
        return carry

    lax.fori_loop(0, count, one_tile, 0)

    @pl.when(count >= 2)
    def _():
        for copy in stores(count - 2):
            copy.wait()

    for copy in stores(count - 1):
        copy.wait()


def levels(used, tiles):
    slots, size, _ = tiles.shape
    return pl.pallas_call(
        levels_kernel,
        out_shape=[shape(tiles.shape, f32)] * 2,
        in_specs=[SMEM, HBM],
        out_specs=[HBM] * 2,
        scratch_shapes=[
            pltpu.VMEM((2, size, size), jnp.int32),
            pltpu.VMEM((2, size, size), f32),
            pltpu.VMEM((2, size, size), f32),
            pltpu.SemaphoreType.DMA((2,)),
            pltpu.SemaphoreType.DMA((2, 2)),
        ],
        compiler_params=pltpu.CompilerParams(vmem_limit_bytes=SMALL),
        cost_estimate=cost(0, 24 << 20),
    )(used, tiles)


def marg_table(pieces, owners, part, size):
    table = jnp.zeros((MARG_ROWS, size), f32)
    for piece, owner in zip(pieces, owners):
        tail = piece[piece.shape[0] - MARG_ROWS :, :MARG_LANES]
        k = lax.broadcasted_iota(jnp.int32, (MARG_LANES, size), 0)
        at = lax.broadcasted_iota(jnp.int32, (MARG_LANES, size), 1)
        place = ((at == k + owner * part) & (k < part)).astype(bf16)
        table += jnp.dot(tail, place, preferred_element_type=f32)
    return table


def work_kernel(first, n_row, n_col, row_owner, col_owner, *refs):
    refs = list(refs)

    def take(n):
        return [refs.pop(0) for _ in range(n)]

    listing, used, logs, weights = take(4)
    row_in, col_in = take(n_row), take(n_col)
    if not first:
        left, right = take(2)
    keep, swap = take(2)
    col_out = take(n_col)
    if first:
        left, right = take(2)
    row_panel, col_panel, grad_row, grad_col, log_buf, weight_buf, signal, sem = take(8)

    row_blocks, size, width = row_panel.shape
    col_blocks = col_panel.shape[0]
    row_part, col_part = size // n_row, size // n_col
    me_row, me_col = lax.axis_index("row"), lax.axis_index("col")
    row_owners = [me_col ^ k for k in row_owner]
    col_owners = [me_row ^ k for k in col_owner]
    row_zero, col_zero = me_row * row_blocks, me_col * col_blocks
    count = used[0]

    def loads(slot):
        at = lax.rem(slot, 2)
        return (
            pltpu.make_async_copy(logs.at[slot], log_buf.at[at], sem.at[at, 0]),
            pltpu.make_async_copy(weights.at[slot], weight_buf.at[at], sem.at[at, 1]),
        )

    for copy in loads(0):
        copy.start()

    for pieces, owners, panel, part in (
        (row_in, row_owners, row_panel, row_part),
        (col_in, col_owners, col_panel, col_part),
    ):
        for piece, owner in zip(pieces, owners):
            start = pl.multiple_of(owner * part, part)
            for b in range(panel.shape[0]):
                panel[b, pl.ds(start, part), :] = piece[b * part : (b + 1) * part, :]
    grad_row[...] = jnp.zeros_like(grad_row)
    grad_col[...] = jnp.zeros_like(grad_col)

    if first:
        row_table = marg_table(row_in, row_owners, row_part, size).astype(bf16)
        for b in range(row_blocks):
            pick = (lax.broadcasted_iota(jnp.int32, (MARG_ROWS, 128), 0) == b).astype(bf16)
            left[b] = lax.dot_general(
                row_table, pick, (((0,), (0,)), ((), ())), preferred_element_type=f32
            )
        col_table = marg_table(col_in, col_owners, col_part, size)
        for b in range(col_blocks):
            right[b] = jnp.broadcast_to(col_table[b : b + 1, :], right.shape[1:])

    chunk = 256

    def one_tile(slot, carry):
        at = lax.rem(slot, 2)

        @pl.when(slot + 1 < count)
        def _():
            for copy in loads(slot + 1):
                copy.start()

        for copy in loads(slot):
            copy.wait()
        i = listing[0, slot] - row_zero
        j = listing[1, slot] - col_zero
        col_piece = col_panel[j]
        marg_right = right[j, 0:1, :]
        for begin in range(0, size, chunk):
            rows = slice(begin, begin + chunk)
            scores = lax.dot_general(
                row_panel[i, rows, :],
                col_piece,
                (((1,), (1,)), ((), ())),
                preferred_element_type=f32,
            )
            marg_left = jnp.concatenate([left[i, rows, :]] * (size // 128), axis=1)
            diff = scores + marg_left + marg_right - log_buf[at, rows, :]
            weight = weight_buf[at, rows, :]
            flat = 0.5 * jnp.tanh(0.5 * diff) + 0.5
            signal[rows, :] = jnp.where(weight > 0.0, weight * diff, flat).astype(bf16)
        grad_row[i] += jnp.dot(signal[...], col_piece, preferred_element_type=f32)
        grad_col[j] += lax.dot_general(
            signal[...], row_panel[i], (((0,), (0,)), ((), ())), preferred_element_type=f32
        )
        return carry

    lax.fori_loop(0, count, one_tile, 0)

    half = n_row // 2
    for n in range(n_row):
        start = pl.multiple_of(row_owners[n] * row_part, row_part)
        piece = grad_row[:, pl.ds(start, row_part), :]
        if n < half:
            keep[n] = piece
        else:
            swap[n - half] = piece.astype(bf16)
    for n in range(n_col):
        start = pl.multiple_of(col_owners[n] * col_part, col_part)
        col_out[n][...] = grad_col[:, pl.ds(start, col_part), :].astype(col_out[n].dtype)


def work(listing, used, logs, weights, row_in, col_in, tables, row_owner, col_owner, dims):
    row_blocks, col_blocks, size, width = dims
    first = tables is None
    n_row, n_col = len(row_owner), len(col_owner)
    row_part, col_part = size // n_row, size // n_col
    half = n_row // 2
    outs = [
        shape((half, row_blocks, row_part, width), f32),
        shape((half, row_blocks, row_part, width), bf16),
        shape((col_blocks, col_part, width), f32),
    ] + [shape((col_blocks, col_part, width), bf16)] * (n_col - 1)
    if first:
        outs += [shape((row_blocks, size, 128), f32), shape((col_blocks, 8, size), f32)]
    args = [listing, used, logs, weights, *row_in, *col_in] + ([] if first else list(tables))
    res = pl.pallas_call(
        functools.partial(work_kernel, first, n_row, n_col, row_owner, col_owner),
        out_shape=outs,
        in_specs=[SMEM, SMEM, HBM, HBM] + [VMEM] * (len(args) - 4),
        out_specs=[VMEM] * len(outs),
        scratch_shapes=[
            pltpu.VMEM((row_blocks, size, width), bf16),
            pltpu.VMEM((col_blocks, size, width), bf16),
            pltpu.VMEM((row_blocks, size, width), f32),
            pltpu.VMEM((col_blocks, size, width), f32),
            pltpu.VMEM((2, size, size), f32),
            pltpu.VMEM((2, size, size), f32),
            pltpu.VMEM((size, size), bf16),
            pltpu.SemaphoreType.DMA((2, 2)),
        ],
        compiler_params=pltpu.CompilerParams(vmem_limit_bytes=LARGE),
        cost_estimate=cost(8 * 6 * size * size * width, 16 << 20),
    )(*args)
    return res[0], res[1], res[2 : 2 + n_col], res[2 + n_col :]


def merge_kernel(keep, got, *outs):
    for n, out in enumerate(outs):
        out[...] = (keep[n] + got[n].astype(f32)).astype(out.dtype)


def merge(keep, got):
    n, *piece = keep.shape
    outs = [shape(tuple(piece), f32)] + [shape(tuple(piece), bf16)] * (n - 1)
    return pl.pallas_call(
        merge_kernel,
        out_shape=outs,
        in_specs=[VMEM] * 2,
        out_specs=[VMEM] * len(outs),
        compiler_params=pltpu.CompilerParams(vmem_limit_bytes=SMALL),
        cost_estimate=cost(0, 2 << 20),
    )(keep, got)


def update_kernel(n_parts, emb, *refs):
    parts, outs = refs[:n_parts], refs[n_parts + 1 :]
    total = parts[0][...].astype(f32)
    for part in parts[1:]:
        total += part[...].astype(f32)
    new = emb[...] - RATE * total
    outs[0][...] = new
    if len(outs) > 1:
        outs[1][...] = new.astype(bf16).reshape(outs[1].shape)


def update(emb, parts, after, last):
    blocks, part, width = emb.shape
    outs = [shape(emb.shape, f32)]
    if not last:
        outs.append(shape((blocks * part, width), bf16))
    res = pl.pallas_call(
        functools.partial(update_kernel, len(parts)),
        out_shape=outs,
        in_specs=[VMEM] * (1 + len(parts)) + [ANY],
        out_specs=[VMEM] * len(outs),
        compiler_params=pltpu.CompilerParams(vmem_limit_bytes=SMALL),
        cost_estimate=cost(0, 2 << 20),
    )(emb, *parts, after)
    return res if not last else (res[0], None)


def send(x, axis, count, mask):
    return lax.ppermute(x, axis, [(k, k ^ mask) for k in range(count)])


def shards(n_row_dev, n_col_dev, row_emb, col_emb, row_marg, col_marg, tile_list, tile_count, tile_data):
    listing = tile_list[0, 0].T
    used = tile_count[0]
    tiles = tile_data[0, 0]
    dims = (row_emb.shape[0], col_emb.shape[0], tiles.shape[-1], row_emb.shape[-1])
    half = n_col_dev // 2
    row_owner = [2 * k for k in range(half)] + [2 * k + 1 for k in range(half)]
    col_owner = list(range(n_row_dev))
    row_pay, col_pay = pack(row_emb, row_marg, col_emb, col_marg)
    logs, weights = levels(used, tiles)
    tables = None
    for substep in range(2):
        col_in = [col_pay] + [send(col_pay, "row", n_row_dev, k) for k in col_owner[1:]]
        row_in = [row_pay] + [send(row_pay, "col", n_col_dev, 2 * k) for k in range(1, half)]
        row_in += [send(piece, "col", n_col_dev, 1) for piece in row_in]
        keep, swap, col_out, made = work(
            listing, used, logs, weights, row_in, col_in, tables, row_owner, col_owner, dims
        )
        tables = tables or made
        got = send(swap, "col", n_col_dev, 1)
        col_parts = [col_out[0]] + [send(col_out[k], "row", n_row_dev, k) for k in col_owner[1:]]
        merged = merge(keep, got)
        row_parts = [merged[0]] + [send(merged[k], "col", n_col_dev, 2 * k) for k in range(1, half)]
        col_emb, col_pay = update(col_emb, col_parts, merged[0], substep == 1)
        row_emb, row_pay = update(row_emb, row_parts, col_emb, substep == 1)
    return (row_emb, col_emb)


def solution(mesh):
    placed = (
        P("row", "col", None),
        P("col", "row", None),
        P("row", "col"),
        P("col", "row"),
        P("row", "col", None, None),
        P("row", "col"),
        P("row", "col", None, None, None),
    )
    return jax.shard_map(
        functools.partial(shards, mesh.shape["row"], mesh.shape["col"]),
        mesh=mesh,
        in_specs=placed,
        out_specs=(P("row", "col", None), P("col", "row", None)),
        check_vma=False,
    )
```

```python
import functools

import jax
import jax.numpy as jnp
from jax import lax
from jax.experimental import pallas as pl
from jax.experimental.pallas import tpu as pltpu
from jax.sharding import PartitionSpec as P

RATE = 0.0004
MARG_ROWS = 16
MARG_LANES = 128
ANY = pl.BlockSpec(memory_space=pl.ANY)
HBM = pl.BlockSpec(memory_space=pltpu.HBM)
VMEM = pl.BlockSpec(memory_space=pltpu.VMEM)
SMEM = pl.BlockSpec(memory_space=pltpu.SMEM)
SMALL = 12 << 20
LARGE = 32 << 20
f32, bf16 = jnp.float32, jnp.bfloat16
shape = jax.ShapeDtypeStruct


def cost(flops, moved):
    return pl.CostEstimate(flops=flops, bytes_accessed=moved, transcendentals=0)


def pack_kernel(emb, marg, out):
    blocks, part, width = emb.shape
    out[: blocks * part, :] = emb[...].astype(bf16).reshape(blocks * part, width)
    out[blocks * part :, :] = jnp.zeros((MARG_ROWS, width), bf16)
    for b in range(blocks):
        out[blocks * part + b : blocks * part + b + 1, :part] = marg[b : b + 1, :]


def pack(emb, marg):
    blocks, part, width = emb.shape
    return pl.pallas_call(
        pack_kernel,
        out_shape=shape((blocks * part + MARG_ROWS, width), bf16),
        in_specs=[VMEM] * 2,
        out_specs=VMEM,
        compiler_params=pltpu.CompilerParams(vmem_limit_bytes=SMALL),
        cost_estimate=cost(0, 1 << 20),
    )(emb, marg)


def levels_kernel(begin, used, tiles, logs, weights, tile_buf, sem):
    end = jnp.minimum(used[0] - begin, logs.shape[0])
    size = tile_buf.shape[-1]
    chunk = 64

    def load(slot):
        at = lax.rem(slot, 2)
        return pltpu.make_async_copy(tiles.at[begin + slot], tile_buf.at[at], sem.at[at])

    @pl.when(end > 0)
    def _():
        load(0).start()

    def one_tile(slot, carry):
        at = lax.rem(slot, 2)

        @pl.when(slot + 1 < end)
        def _():
            load(slot + 1).start()

        load(slot).wait()

        def one_chunk(n, carry):
            rows = pl.ds(pl.multiple_of(n * chunk, chunk), chunk)
            counts = tile_buf[at, rows, :].astype(f32)
            level = jnp.maximum(counts, 1.0)
            logs[slot, rows, :] = jnp.log(level)
            weight = 0.1 + 0.25 * (level * lax.rsqrt(level))
            weights[slot, rows, :] = jnp.where(counts > 0.0, weight, 0.0)
            return carry

        lax.fori_loop(0, size // chunk, one_chunk, 0)
        return carry

    lax.fori_loop(0, end, one_tile, 0)


def levels(begin, slots, used, tiles):
    size = tiles.shape[-1]
    return pl.pallas_call(
        functools.partial(levels_kernel, begin),
        out_shape=[shape((slots, size, size), f32)] * 2,
        in_specs=[SMEM, HBM],
        out_specs=[VMEM] * 2,
        scratch_shapes=[pltpu.VMEM((2, size, size), jnp.int32), pltpu.SemaphoreType.DMA((2,))],
        compiler_params=pltpu.CompilerParams(vmem_limit_bytes=SMALL),
        cost_estimate=cost(0, 12 << 20),
    )(used, tiles)


def join_kernel(n_parts, *refs):
    out = refs[-1]
    for n in range(n_parts):
        out[n] = refs[n][...]


def join(parts, afters):
    return pl.pallas_call(
        functools.partial(join_kernel, len(parts)),
        out_shape=shape((len(parts), *parts[0].shape), parts[0].dtype),
        in_specs=[VMEM] * len(parts) + [ANY] * len(afters),
        out_specs=VMEM,
        compiler_params=pltpu.CompilerParams(vmem_limit_bytes=SMALL),
        cost_estimate=cost(0, 1 << 20),
    )(*parts, *afters)


def marg_table(pieces, owners, part, size):
    table = jnp.zeros((MARG_ROWS, size), f32)
    for piece, owner in zip(pieces, owners):
        tail = piece[piece.shape[0] - MARG_ROWS :, :MARG_LANES]
        k = lax.broadcasted_iota(jnp.int32, (MARG_LANES, size), 0)
        at = lax.broadcasted_iota(jnp.int32, (MARG_LANES, size), 1)
        place = ((at == k + owner * part) & (k < part)).astype(bf16)
        table += jnp.dot(tail, place, preferred_element_type=f32)
    return table


def work_kernel(first, n_row, n_col, row_owner, col_owner, *refs):
    refs = list(refs)

    def take(n):
        return [refs.pop(0) for _ in range(n)]

    listing, used, logs_a, weights_a, logs_b, weights_b, row_near, row_far = take(8)
    col_in = take(n_col)
    if not first:
        left, right = take(2)
    keep, swap = take(2)
    col_out = take(n_col)
    if first:
        left, right = take(2)
    row_panel, row_turned, col_panel, grad_row, grad_turned, grad_col = take(6)

    row_blocks, size, width = row_panel.shape
    col_blocks = col_panel.shape[0]
    row_part, col_part = size // n_row, size // n_col
    half = n_row // 2
    me_row, me_col = lax.axis_index("row"), lax.axis_index("col")
    row_owners = [me_col ^ k for k in row_owner]
    col_owners = [me_row ^ k for k in col_owner]
    row_zero, col_zero = me_row * row_blocks, me_col * col_blocks
    count = used[0]
    row_in = [side.at[n] for side in (row_near, row_far) for n in range(half)]

    for pieces, owners, panel, part in (
        (row_in, row_owners, row_panel, row_part),
        (col_in, col_owners, col_panel, col_part),
    ):
        for piece, owner in zip(pieces, owners):
            start = pl.multiple_of(owner * part, part)
            for b in range(panel.shape[0]):
                panel[b, pl.ds(start, part), :] = piece[b * part : (b + 1) * part, :]
    for b in range(row_blocks):
        row_turned[b] = row_panel[b].T
    grad_row[...] = jnp.zeros_like(grad_row)
    grad_turned[...] = jnp.zeros_like(grad_turned)

    if first:
        row_table = marg_table(row_in, row_owners, row_part, size).astype(bf16)
        for b in range(row_blocks):
            pick = (lax.broadcasted_iota(jnp.int32, (MARG_ROWS, 128), 0) == b).astype(bf16)
            left[b] = lax.dot_general(
                row_table, pick, (((0,), (0,)), ((), ())), preferred_element_type=f32
            )
        col_table = marg_table(col_in, col_owners, col_part, size)
        for b in range(col_blocks):
            right[b] = jnp.broadcast_to(col_table[b : b + 1, :], right.shape[1:])

    chunk = 256
    split = logs_a.shape[0]

    def tile_of(logs, weights, begin):
        def one_tile(slot, carry):
            i = listing[0, slot] - row_zero
            j = listing[1, slot] - col_zero
            col_piece = col_panel[j]
            marg_right = right[j, 0:1, :]
            turned = None
            for first_row in range(0, size, chunk):
                rows = slice(first_row, first_row + chunk)
                scores = lax.dot_general(
                    row_panel[i, rows, :],
                    col_piece,
                    (((1,), (1,)), ((), ())),
                    preferred_element_type=f32,
                )
                marg_left = jnp.concatenate([left[i, rows, :]] * (size // 128), axis=1)
                diff = scores + marg_left + marg_right - logs[slot - begin, rows, :]
                weight = weights[slot - begin, rows, :]
                flat = 0.5 * jnp.tanh(0.5 * diff) + 0.5
                signal = jnp.where(weight > 0.0, weight * diff, flat).astype(bf16)
                grad_row[i, rows, :] += jnp.dot(signal, col_piece, preferred_element_type=f32)
                term = jnp.dot(row_turned[i, :, rows], signal, preferred_element_type=f32)
                turned = term if turned is None else turned + term
            grad_turned[j] += turned
            return carry

        return one_tile

    lax.fori_loop(0, jnp.minimum(count, split), tile_of(logs_a, weights_a, 0), 0)
    lax.fori_loop(split, count, tile_of(logs_b, weights_b, split), 0)

    for n in range(n_row):
        place, sibling = row_owner[n] >> 1, row_owner[n] & 1
        start = pl.multiple_of(row_owners[n] * row_part, row_part)
        piece = grad_row[:, pl.ds(start, row_part), :]
        if sibling:
            swap[place] = piece.astype(bf16)
        else:
            keep[place] = piece
    for b in range(col_blocks):
        grad_col[b] = grad_turned[b].astype(bf16).T
    for n in range(n_col):
        start = pl.multiple_of(col_owners[n] * col_part, col_part)
        col_out[n][...] = grad_col[:, pl.ds(start, col_part), :]


def work(listing, used, tabs, row_near, row_far, col_in, tables, row_owner, col_owner, dims):
    row_blocks, col_blocks, size, width = dims
    first = tables is None
    n_row, n_col = len(row_owner), len(col_owner)
    row_part, col_part = size // n_row, size // n_col
    half = n_row // 2
    outs = [
        shape((half, row_blocks, row_part, width), f32),
        shape((half, row_blocks, row_part, width), bf16),
    ] + [shape((col_blocks, col_part, width), bf16)] * n_col
    if first:
        outs += [shape((row_blocks, size, 128), f32), shape((col_blocks, 8, size), f32)]
    args = [listing, used, *tabs, row_near, row_far, *col_in] + ([] if first else list(tables))
    res = pl.pallas_call(
        functools.partial(work_kernel, first, n_row, n_col, row_owner, col_owner),
        out_shape=outs,
        in_specs=[SMEM, SMEM] + [VMEM] * (len(args) - 2),
        out_specs=[VMEM] * len(outs),
        scratch_shapes=[
            pltpu.VMEM((row_blocks, size, width), bf16),
            pltpu.VMEM((row_blocks, width, size), bf16),
            pltpu.VMEM((col_blocks, size, width), bf16),
            pltpu.VMEM((row_blocks, size, width), f32),
            pltpu.VMEM((col_blocks, width, size), f32),
            pltpu.VMEM((col_blocks, size, width), bf16),
        ],
        compiler_params=pltpu.CompilerParams(vmem_limit_bytes=LARGE),
        cost_estimate=cost(8 * 6 * size * size * width, 16 << 20),
    )(*args)
    return res[0], res[1], res[2 : 2 + n_col], res[2 + n_col :]


def merge_kernel(keep, got, keep_out, send_out):
    for n in range(keep_out.shape[0]):
        keep_out[n] = keep[2 * n] + got[2 * n].astype(f32)
        send_out[n] = (keep[2 * n + 1] + got[2 * n + 1].astype(f32)).astype(bf16)


def merge(keep, got):
    n, *piece = keep.shape
    return pl.pallas_call(
        merge_kernel,
        out_shape=[shape((n // 2, *piece), f32), shape((n // 2, *piece), bf16)],
        in_specs=[VMEM] * 2,
        out_specs=[VMEM] * 2,
        compiler_params=pltpu.CompilerParams(vmem_limit_bytes=SMALL),
        cost_estimate=cost(0, 2 << 20),
    )(keep, got)


def update_kernel(n_parts, emb, *refs):
    parts, outs = refs[:n_parts], refs[n_parts + 1 :]
    total = parts[0][...].astype(f32)
    for part in parts[1:]:
        total += part[...].astype(f32)
    new = emb[...] - RATE * total.reshape(emb.shape)
    outs[0][...] = new
    if len(outs) > 1:
        outs[1][...] = new.astype(bf16).reshape(outs[1].shape)


def update(emb, parts, after, last):
    blocks, part, width = emb.shape
    outs = [shape(emb.shape, f32)]
    if not last:
        outs.append(shape((blocks * part, width), bf16))
    res = pl.pallas_call(
        functools.partial(update_kernel, len(parts)),
        out_shape=outs,
        in_specs=[VMEM] * (1 + len(parts)) + [ANY],
        out_specs=[VMEM] * len(outs),
        compiler_params=pltpu.CompilerParams(vmem_limit_bytes=SMALL),
        cost_estimate=cost(0, 2 << 20),
    )(emb, *parts, after)
    return res if not last else (res[0], None)


def send(x, axis, count, mask):
    return lax.ppermute(x, axis, [(k, k ^ mask) for k in range(count)])


def shards(n_row_dev, n_col_dev, row_emb, col_emb, row_marg, col_marg, tile_list, tile_count, tile_data):
    listing = tile_list[0, 0].T
    used = tile_count[0]
    tiles = tile_data[0, 0]
    dims = (row_emb.shape[0], col_emb.shape[0], tiles.shape[-1], row_emb.shape[-1])
    half = n_col_dev // 2
    masks = [1 << b for b in range(1, n_col_dev.bit_length() - 1)]
    row_owner = [2 * k for k in range(half)] + [2 * k + 1 for k in range(half)]
    col_owner = list(range(n_row_dev))
    slots = tiles.shape[0]
    col_pay = pack(col_emb, col_marg)
    row_pay = pack(row_emb, row_marg)
    tabs = [levels(0, slots // 2, used, tiles), levels(slots // 2, slots - slots // 2, used, tiles)]
    afters = [tabs[0][0], tabs[1][0]]
    tabs = [*tabs[0], *tabs[1]]
    tables = None
    for substep in range(2):
        row_near = [row_pay] + [send(row_pay, "col", n_col_dev, 2 * k) for k in range(1, half)]
        col_in = [col_pay] + [send(col_pay, "row", n_row_dev, k) for k in col_owner[1:]]
        row_near = join(row_near, col_in[1:] + (afters if substep == 0 else []))
        row_far = send(row_near, "col", n_col_dev, 1)
        keep, swap, col_out, made = work(
            listing, used, tabs, row_near, row_far, col_in, tables, row_owner, col_owner, dims
        )
        tables = tables or made
        col_parts = [col_out[0]] + [send(col_out[k], "row", n_row_dev, k) for k in col_owner[1:]]
        got = send(swap, "col", n_col_dev, 1)
        for mask in masks:
            keep, leaving = merge(keep, got)
            got = send(leaving, "col", n_col_dev, mask)
        col_emb, col_pay = update(col_emb, col_parts, leaving, substep == 1)
        row_emb, row_pay = update(row_emb, [keep, got], col_pay if substep == 0 else keep, substep == 1)
    return (row_emb, col_emb)


def solution(mesh):
    placed = (
        P("row", "col", None),
        P("col", "row", None),
        P("row", "col"),
        P("col", "row"),
        P("row", "col", None, None),
        P("row", "col"),
        P("row", "col", None, None, None),
    )
    return jax.shard_map(
        functools.partial(shards, mesh.shape["row"], mesh.shape["col"]),
        mesh=mesh,
        in_specs=placed,
        out_specs=(P("row", "col", None), P("col", "row", None)),
        check_vma=False,
    )
```

```python
import functools

import jax
import jax.numpy as jnp
from jax import lax
from jax.experimental import pallas as pl
from jax.experimental.pallas import tpu as pltpu
from jax.sharding import PartitionSpec as P

RATE = 0.0004
MARG_ROWS = 16
MARG_LANES = 128
ANY = pl.BlockSpec(memory_space=pl.ANY)
HBM = pl.BlockSpec(memory_space=pltpu.HBM)
VMEM = pl.BlockSpec(memory_space=pltpu.VMEM)
SMEM = pl.BlockSpec(memory_space=pltpu.SMEM)
SMALL = 12 << 20
LARGE = 32 << 20
LEVELS = 35 << 20
PACK = 62 << 20
f32, bf16 = jnp.float32, jnp.bfloat16
shape = jax.ShapeDtypeStruct


def cost(flops, moved):
    return pl.CostEstimate(flops=flops, bytes_accessed=moved, transcendentals=0)


def pack_kernel(row_emb, row_marg, col_emb, col_marg, row_out, col_out, *scratch):
    bufs, sem = scratch[:4], scratch[4]
    copies = [
        pltpu.make_async_copy(src, dst, sem.at[n])
        for n, (src, dst) in enumerate(zip((row_emb, row_marg, col_emb, col_marg), bufs))
    ]
    for copy in copies:
        copy.start()
    for n, out in enumerate((row_out, col_out)):
        copies[2 * n].wait()
        copies[2 * n + 1].wait()
        emb, marg = bufs[2 * n], bufs[2 * n + 1]
        blocks, part, width = emb.shape
        out[: blocks * part, :] = emb[...].astype(bf16).reshape(blocks * part, width)
        out[blocks * part :, :] = jnp.zeros((MARG_ROWS, width), bf16)
        for b in range(blocks):
            out[blocks * part + b : blocks * part + b + 1, :part] = marg[b : b + 1, :]


def pack(row_emb, row_marg, col_emb, col_marg):
    args = (row_emb, row_marg, col_emb, col_marg)
    return pl.pallas_call(
        pack_kernel,
        out_shape=[
            shape((e.shape[0] * e.shape[1] + MARG_ROWS, e.shape[2]), bf16) for e in args[::2]
        ],
        in_specs=[ANY] * 4,
        out_specs=[VMEM] * 2,
        scratch_shapes=[pltpu.VMEM(x.shape, x.dtype) for x in args]
        + [pltpu.SemaphoreType.DMA((4,))],
        compiler_params=pltpu.CompilerParams(vmem_limit_bytes=PACK),
        cost_estimate=cost(0, 1 << 20),
    )(*args)


def levels_kernel(used, tiles, logs, weights, token, tile_buf, sem):
    end = used[0]
    size = tile_buf.shape[-1]
    chunk = 64

    def load(slot):
        at = lax.rem(slot, 2)
        return pltpu.make_async_copy(tiles.at[slot], tile_buf.at[at], sem.at[at])

    load(0).start()
    token[...] = jnp.zeros_like(token)

    def one_tile(slot, carry):
        at = lax.rem(slot, 2)

        @pl.when(slot + 1 < end)
        def _():
            load(slot + 1).start()

        load(slot).wait()

        def one_chunk(n, carry):
            rows = pl.ds(pl.multiple_of(n * chunk, chunk), chunk)
            counts = tile_buf[at, rows, :].astype(f32)
            level = jnp.maximum(counts, 1.0)
            logs[slot, rows, :] = jnp.log(level)
            weight = 0.1 + 0.25 * (level * lax.rsqrt(level))
            weights[slot, rows, :] = jnp.where(counts > 0.0, weight, 0.0)
            return carry

        lax.fori_loop(0, size // chunk, one_chunk, 0)
        return carry

    lax.fori_loop(0, end, one_tile, 0)


def levels(used, tiles):
    size = tiles.shape[-1]
    return pl.pallas_call(
        levels_kernel,
        out_shape=[shape(tiles.shape, f32)] * 2 + [shape((8, 128), f32)],
        in_specs=[SMEM, HBM],
        out_specs=[VMEM] * 3,
        scratch_shapes=[pltpu.VMEM((2, size, size), jnp.int32), pltpu.SemaphoreType.DMA((2,))],
        compiler_params=pltpu.CompilerParams(vmem_limit_bytes=LEVELS),
        cost_estimate=cost(0, 24 << 20),
    )(used, tiles)


def join_kernel(n_parts, *refs):
    out = refs[-1]
    for n in range(n_parts):
        out[n] = refs[n][...]


def join(parts, afters):
    return pl.pallas_call(
        functools.partial(join_kernel, len(parts)),
        out_shape=shape((len(parts), *parts[0].shape), parts[0].dtype),
        in_specs=[VMEM] * len(parts) + [ANY] * len(afters),
        out_specs=VMEM,
        compiler_params=pltpu.CompilerParams(vmem_limit_bytes=SMALL),
        cost_estimate=cost(0, 1 << 20),
    )(*parts, *afters)


def marg_table(pieces, owners, part, size):
    table = jnp.zeros((MARG_ROWS, size), f32)
    for piece, owner in zip(pieces, owners):
        tail = piece[piece.shape[0] - MARG_ROWS :, :MARG_LANES]
        k = lax.broadcasted_iota(jnp.int32, (MARG_LANES, size), 0)
        at = lax.broadcasted_iota(jnp.int32, (MARG_LANES, size), 1)
        place = ((at == k + owner * part) & (k < part)).astype(bf16)
        table += jnp.dot(tail, place, preferred_element_type=f32)
    return table


def work_kernel(first, n_row, n_col, row_owner, col_owner, *refs):
    refs = list(refs)

    def take(n):
        return [refs.pop(0) for _ in range(n)]

    listing, used, logs, weights, row_near, row_far = take(6)
    col_in = take(n_col)
    if not first:
        left, right = take(2)
    keep, swap = take(2)
    col_out = take(n_col)
    if first:
        left, right = take(2)
    row_panel, row_turned, col_panel, grad_row, grad_turned, grad_col, scores, signal = take(8)

    row_blocks, size, width = row_panel.shape
    col_blocks = col_panel.shape[0]
    row_part, col_part = size // n_row, size // n_col
    half = n_row // 2
    me_row, me_col = lax.axis_index("row"), lax.axis_index("col")
    row_owners = [me_col ^ k for k in row_owner]
    col_owners = [me_row ^ k for k in col_owner]
    row_zero, col_zero = me_row * row_blocks, me_col * col_blocks
    count = used[0]
    row_in = [side.at[n] for side in (row_near, row_far) for n in range(half)]

    for pieces, owners, panel, part in (
        (row_in, row_owners, row_panel, row_part),
        (col_in, col_owners, col_panel, col_part),
    ):
        for piece, owner in zip(pieces, owners):
            start = pl.multiple_of(owner * part, part)
            for b in range(panel.shape[0]):
                panel[b, pl.ds(start, part), :] = piece[b * part : (b + 1) * part, :]
    for b in range(row_blocks):
        row_turned[b] = row_panel[b].T
    grad_row[...] = jnp.zeros_like(grad_row)
    grad_turned[...] = jnp.zeros_like(grad_turned)

    if first:
        row_table = marg_table(row_in, row_owners, row_part, size).astype(bf16)
        for b in range(row_blocks):
            pick = (lax.broadcasted_iota(jnp.int32, (MARG_ROWS, 128), 0) == b).astype(bf16)
            left[b] = lax.dot_general(
                row_table, pick, (((0,), (0,)), ((), ())), preferred_element_type=f32
            )
        col_table = marg_table(col_in, col_owners, col_part, size)
        for b in range(col_blocks):
            right[b] = jnp.broadcast_to(col_table[b : b + 1, :], right.shape[1:])

    chunks = [slice(at, at + 256) for at in range(0, size, 256)]

    def place(slot):
        return listing[0, slot] - row_zero, listing[1, slot] - col_zero

    def make_scores(slot, rows):
        i, j = place(slot)
        scores[rows, :] = lax.dot_general(
            row_panel[i, rows, :], col_panel[j], (((1,), (1,)), ((), ())), preferred_element_type=f32
        )

    def make_signal(slot, rows):
        i, j = place(slot)
        marg_left = jnp.concatenate([left[i, rows, :]] * (size // 128), axis=1)
        diff = scores[rows, :] + marg_left + right[j, 0:1, :] - logs[slot, rows, :]
        weight = weights[slot, rows, :]
        flat = 0.5 * jnp.tanh(0.5 * diff) + 0.5
        signal[rows, :] = jnp.where(weight > 0.0, weight * diff, flat).astype(bf16)

    def add_grads(slot, rows):
        i, j = place(slot)
        piece = signal[rows, :]
        grad_row[i, rows, :] += jnp.dot(piece, col_panel[j], preferred_element_type=f32)
        grad_turned[j] += jnp.dot(row_turned[i, :, rows], piece, preferred_element_type=f32)

    def one_tile(slot, carry):
        for rows in chunks:
            add_grads(slot - 1, rows)
            make_signal(slot, rows)
            make_scores(jnp.minimum(slot + 1, count - 1), rows)
        return carry

    for rows in chunks:
        make_scores(0, rows)
    for rows in chunks:
        make_signal(0, rows)
        make_scores(jnp.minimum(1, count - 1), rows)
    lax.fori_loop(1, count, one_tile, 0)
    for rows in chunks:
        add_grads(count - 1, rows)

    for n in range(n_row):
        place, sibling = row_owner[n] >> 1, row_owner[n] & 1
        start = pl.multiple_of(row_owners[n] * row_part, row_part)
        piece = grad_row[:, pl.ds(start, row_part), :]
        if sibling:
            swap[place] = piece.astype(bf16)
        else:
            keep[place] = piece
    for b in range(col_blocks):
        grad_col[b] = grad_turned[b].astype(bf16).T
    for n in range(n_col):
        start = pl.multiple_of(col_owners[n] * col_part, col_part)
        col_out[n][...] = grad_col[:, pl.ds(start, col_part), :]


def work(listing, used, tabs, row_near, row_far, col_in, tables, row_owner, col_owner, dims):
    row_blocks, col_blocks, size, width = dims
    first = tables is None
    n_row, n_col = len(row_owner), len(col_owner)
    row_part, col_part = size // n_row, size // n_col
    half = n_row // 2
    outs = [
        shape((half, row_blocks, row_part, width), f32),
        shape((half, row_blocks, row_part, width), bf16),
    ] + [shape((col_blocks, col_part, width), bf16)] * n_col
    if first:
        outs += [shape((row_blocks, size, 128), f32), shape((col_blocks, 8, size), f32)]
    args = [listing, used, *tabs, row_near, row_far, *col_in] + ([] if first else list(tables))
    res = pl.pallas_call(
        functools.partial(work_kernel, first, n_row, n_col, row_owner, col_owner),
        out_shape=outs,
        in_specs=[SMEM, SMEM] + [VMEM] * (len(args) - 2),
        out_specs=[VMEM] * len(outs),
        scratch_shapes=[
            pltpu.VMEM((row_blocks, size, width), bf16),
            pltpu.VMEM((row_blocks, width, size), bf16),
            pltpu.VMEM((col_blocks, size, width), bf16),
            pltpu.VMEM((row_blocks, size, width), f32),
            pltpu.VMEM((col_blocks, width, size), f32),
            pltpu.VMEM((col_blocks, size, width), bf16),
            pltpu.VMEM((size, size), f32),
            pltpu.VMEM((size, size), bf16),
        ],
        compiler_params=pltpu.CompilerParams(vmem_limit_bytes=LARGE),
        cost_estimate=cost(8 * 6 * size * size * width, 16 << 20),
    )(*args)
    return res[0], res[1], res[2 : 2 + n_col], res[2 + n_col :]


def merge_kernel(keep, got, *outs):
    for n, out in enumerate(outs):
        out[...] = (keep[n] + got[n].astype(f32)).astype(out.dtype)


def merge(keep, got):
    n, *piece = keep.shape
    outs = [shape(tuple(piece), f32)] + [shape(tuple(piece), bf16)] * (n - 1)
    return pl.pallas_call(
        merge_kernel,
        out_shape=outs,
        in_specs=[VMEM] * 2,
        out_specs=[VMEM] * len(outs),
        compiler_params=pltpu.CompilerParams(vmem_limit_bytes=SMALL),
        cost_estimate=cost(0, 2 << 20),
    )(keep, got)


def update_kernel(n_row, n_col, row_emb, col_emb, *refs):
    row_parts, col_parts, outs = refs[:n_row], refs[n_row : n_row + n_col], refs[n_row + n_col :]
    for n, (emb, parts) in enumerate(((row_emb, row_parts), (col_emb, col_parts))):
        total = parts[0][...].astype(f32)
        for part in parts[1:]:
            total += part[...].astype(f32)
        new = emb[...] - RATE * total
        outs[n][...] = new
        if len(outs) > 2:
            outs[2 + n][...] = new.astype(bf16).reshape(outs[2 + n].shape)


def update(row_emb, col_emb, row_parts, col_parts, last):
    embs = (row_emb, col_emb)
    outs = [shape(e.shape, f32) for e in embs]
    if not last:
        outs += [shape((e.shape[0] * e.shape[1], e.shape[2]), bf16) for e in embs]
    return pl.pallas_call(
        functools.partial(update_kernel, len(row_parts), len(col_parts)),
        out_shape=outs,
        in_specs=[VMEM] * (2 + len(row_parts) + len(col_parts)),
        out_specs=[VMEM] * len(outs),
        compiler_params=pltpu.CompilerParams(vmem_limit_bytes=SMALL),
        cost_estimate=cost(0, 2 << 20),
    )(row_emb, col_emb, *row_parts, *col_parts)


def send(x, axis, count, mask):
    return lax.ppermute(x, axis, [(k, k ^ mask) for k in range(count)])


def shards(n_row_dev, n_col_dev, row_emb, col_emb, row_marg, col_marg, tile_list, tile_count, tile_data):
    listing = tile_list[0, 0].T
    used = tile_count[0]
    tiles = tile_data[0, 0]
    dims = (row_emb.shape[0], col_emb.shape[0], tiles.shape[-1], row_emb.shape[-1])
    half = n_col_dev // 2
    row_owner = [2 * k for k in range(half)] + [2 * k + 1 for k in range(half)]
    col_owner = list(range(n_row_dev))
    row_pay, col_pay = pack(row_emb, row_marg, col_emb, col_marg)
    *tabs, made_tabs = levels(used, tiles)
    tables = None
    for substep in range(2):
        row_near = [row_pay] + [send(row_pay, "col", n_col_dev, 2 * k) for k in range(1, half)]
        col_in = [col_pay] + [send(col_pay, "row", n_row_dev, k) for k in col_owner[1:]]
        row_near = join(row_near, col_in[1:] + ([made_tabs] if substep == 0 else []))
        row_far = send(row_near, "col", n_col_dev, 1)
        keep, swap, col_out, made = work(
            listing, used, tabs, row_near, row_far, col_in, tables, row_owner, col_owner, dims
        )
        tables = tables or made
        col_parts = [col_out[0]] + [send(col_out[k], "row", n_row_dev, k) for k in col_owner[1:]]
        merged = merge(keep, send(swap, "col", n_col_dev, 1))
        row_parts = [merged[0]] + [send(merged[k], "col", n_col_dev, 2 * k) for k in range(1, half)]
        if substep == 0:
            row_emb, col_emb, row_pay, col_pay = update(row_emb, col_emb, row_parts, col_parts, False)
    return tuple(update(row_emb, col_emb, row_parts, col_parts, True))


def solution(mesh):
    placed = (
        P("row", "col", None),
        P("col", "row", None),
        P("row", "col"),
        P("col", "row"),
        P("row", "col", None, None),
        P("row", "col"),
        P("row", "col", None, None, None),
    )
    return jax.shard_map(
        functools.partial(shards, mesh.shape["row"], mesh.shape["col"]),
        mesh=mesh,
        in_specs=placed,
        out_specs=(P("row", "col", None), P("col", "row", None)),
        check_vma=False,
    )
```

```python
import functools

import jax
import jax.numpy as jnp
from jax import lax
from jax.experimental import pallas as pl
from jax.experimental.pallas import tpu as pltpu
from jax.sharding import PartitionSpec as P

RATE = 0.0004
MARG_ROWS = 16
MARG_LANES = 128
ANY = pl.BlockSpec(memory_space=pl.ANY)
HBM = pl.BlockSpec(memory_space=pltpu.HBM)
VMEM = pl.BlockSpec(memory_space=pltpu.VMEM)
SMEM = pl.BlockSpec(memory_space=pltpu.SMEM)
SMALL = 12 << 20
LARGE = 32 << 20
LEVELS = 35 << 20
PACK = 62 << 20
f32, bf16 = jnp.float32, jnp.bfloat16
shape = jax.ShapeDtypeStruct


def cost(flops, moved):
    return pl.CostEstimate(flops=flops, bytes_accessed=moved, transcendentals=0)


def pack_kernel(row_emb, row_marg, col_emb, col_marg, row_out, col_out, *scratch):
    bufs, sem = scratch[:4], scratch[4]
    copies = [
        pltpu.make_async_copy(src, dst, sem.at[n])
        for n, (src, dst) in enumerate(zip((row_emb, row_marg, col_emb, col_marg), bufs))
    ]
    for copy in copies:
        copy.start()
    for n, out in enumerate((row_out, col_out)):
        copies[2 * n].wait()
        copies[2 * n + 1].wait()
        emb, marg = bufs[2 * n], bufs[2 * n + 1]
        blocks, part, width = emb.shape
        rounded = emb[...].astype(bf16).reshape(blocks * part, width)
        for n in range(out.shape[0]):
            out[n, : blocks * part, :] = rounded
            out[n, blocks * part :, :] = jnp.zeros((MARG_ROWS, width), bf16)
            for b in range(blocks):
                out[n, blocks * part + b : blocks * part + b + 1, :part] = marg[b : b + 1, :]


def pack(row_emb, row_marg, col_emb, col_marg, copies):
    args = (row_emb, row_marg, col_emb, col_marg)
    return pl.pallas_call(
        pack_kernel,
        out_shape=[
            shape((n, e.shape[0] * e.shape[1] + MARG_ROWS, e.shape[2]), bf16)
            for e, n in zip(args[::2], copies)
        ],
        in_specs=[ANY] * 4,
        out_specs=[VMEM] * 2,
        scratch_shapes=[pltpu.VMEM(x.shape, x.dtype) for x in args]
        + [pltpu.SemaphoreType.DMA((4,))],
        compiler_params=pltpu.CompilerParams(vmem_limit_bytes=PACK),
        cost_estimate=cost(0, 1 << 20),
    )(*args)


def levels_kernel(used, tiles, logs, weights, tile_buf, sem):
    count = used[0]
    slots, size, _ = tile_buf.shape
    chunk = 64

    def load(slot):
        return pltpu.make_async_copy(tiles.at[slot], tile_buf.at[slot], sem.at[slot])

    for slot in range(slots):

        @pl.when(slot < count)
        def _():
            load(slot).start()

    def one_tile(slot, carry):
        load(slot).wait()

        def one_chunk(n, carry):
            rows = pl.ds(pl.multiple_of(n * chunk, chunk), chunk)
            counts = tile_buf[slot, rows, :].astype(f32)
            level = jnp.maximum(counts, 1.0)
            logs[slot, rows, :] = jnp.log(level)
            weight = 0.1 + 0.25 * (level * lax.rsqrt(level))
            weights[slot, rows, :] = jnp.where(counts > 0.0, weight, 0.0)
            return carry

        lax.fori_loop(0, size // chunk, one_chunk, 0)
        return carry

    lax.fori_loop(0, count, one_tile, 0)


def levels(used, tiles):
    return pl.pallas_call(
        levels_kernel,
        out_shape=[shape(tiles.shape, f32)] * 2,
        in_specs=[SMEM, HBM],
        out_specs=[VMEM] * 2,
        scratch_shapes=[
            pltpu.VMEM(tiles.shape, jnp.int32),
            pltpu.SemaphoreType.DMA((tiles.shape[0],)),
        ],
        compiler_params=pltpu.CompilerParams(vmem_limit_bytes=LEVELS),
        cost_estimate=cost(0, 24 << 20),
    )(used, tiles)


def marg_table(pieces, owners, part, size):
    table = jnp.zeros((MARG_ROWS, size), f32)
    for piece, owner in zip(pieces, owners):
        tail = piece[piece.shape[0] - MARG_ROWS :, :MARG_LANES]
        k = lax.broadcasted_iota(jnp.int32, (MARG_LANES, size), 0)
        at = lax.broadcasted_iota(jnp.int32, (MARG_LANES, size), 1)
        place = ((at == k + owner * part) & (k < part)).astype(bf16)
        table += jnp.dot(tail, place, preferred_element_type=f32)
    return table


def work_kernel(first, n_row, n_col, *refs):
    refs = list(refs)

    def take(n):
        return [refs.pop(0) for _ in range(n)]

    listing, used, logs, weights, row_near, row_far, col_in = take(7)
    if not first:
        left, right = take(2)
    keep, swap, col_out = take(3)
    if first:
        left, right = take(2)
    row_panel, row_turned, col_panel, grad_row, grad_turned, grad_col, scores, signal = take(8)

    row_blocks, size, width = row_panel.shape
    col_blocks = col_panel.shape[0]
    row_part, col_part = size // n_row, size // n_col
    half = n_row // 2
    me_row, me_col = lax.axis_index("row"), lax.axis_index("col")
    core = lax.rem(me_col, 2)
    row_owners = [2 * n + core for n in range(half)] + [2 * n + 1 - core for n in range(half)]
    col_owners = list(range(n_col))
    row_zero, col_zero = me_row * row_blocks, me_col * col_blocks
    count = used[0]
    row_in = [side.at[n] for side in (row_near, row_far) for n in range(half)]
    col_in = [col_in.at[n] for n in range(n_col)]

    for pieces, owners, panel, part in (
        (row_in, row_owners, row_panel, row_part),
        (col_in, col_owners, col_panel, col_part),
    ):
        for piece, owner in zip(pieces, owners):
            start = owner * part if isinstance(owner, int) else pl.multiple_of(owner * part, part)
            for b in range(panel.shape[0]):
                panel[b, pl.ds(start, part), :] = piece[b * part : (b + 1) * part, :]
    for b in range(row_blocks):
        row_turned[b] = row_panel[b].T
    grad_row[...] = jnp.zeros_like(grad_row)
    grad_turned[...] = jnp.zeros_like(grad_turned)

    if first:
        row_table = marg_table(row_in, row_owners, row_part, size).astype(bf16)
        for b in range(row_blocks):
            pick = (lax.broadcasted_iota(jnp.int32, (MARG_ROWS, 128), 0) == b).astype(bf16)
            left[b] = lax.dot_general(
                row_table, pick, (((0,), (0,)), ((), ())), preferred_element_type=f32
            )
        col_table = marg_table(col_in, col_owners, col_part, size)
        for b in range(col_blocks):
            right[b] = jnp.broadcast_to(col_table[b : b + 1, :], right.shape[1:])

    chunks = [slice(at, at + 256) for at in range(0, size, 256)]

    def place(slot):
        return listing[0, slot] - row_zero, listing[1, slot] - col_zero

    def make_scores(slot, rows):
        i, j = place(slot)
        scores[rows, :] = lax.dot_general(
            row_panel[i, rows, :], col_panel[j], (((1,), (1,)), ((), ())), preferred_element_type=f32
        )

    def make_signal(slot, rows):
        i, j = place(slot)
        marg_left = jnp.concatenate([left[i, rows, :]] * (size // 128), axis=1)
        diff = scores[rows, :] + marg_left + right[j, 0:1, :] - logs[slot, rows, :]
        weight = weights[slot, rows, :]
        flat = 0.5 * jnp.tanh(0.5 * diff) + 0.5
        signal[rows, :] = jnp.where(weight > 0.0, weight * diff, flat).astype(bf16)

    def add_grads(slot, rows):
        i, j = place(slot)
        piece = signal[rows, :]
        grad_row[i, rows, :] += jnp.dot(piece, col_panel[j], preferred_element_type=f32)
        grad_turned[j] += jnp.dot(row_turned[i, :, rows], piece, preferred_element_type=f32)

    def one_tile(slot, carry):
        for rows in chunks:
            add_grads(slot - 1, rows)
            make_signal(slot, rows)
            make_scores(jnp.minimum(slot + 1, count - 1), rows)
        return carry

    for rows in chunks:
        make_scores(0, rows)
    for rows in chunks:
        make_signal(0, rows)
        make_scores(jnp.minimum(1, count - 1), rows)
    lax.fori_loop(1, count, one_tile, 0)
    for rows in chunks:
        add_grads(count - 1, rows)

    for n in range(n_row):
        start = pl.multiple_of(row_owners[n] * row_part, row_part)
        piece = grad_row[:, pl.ds(start, row_part), :]
        if n < half:
            keep[n] = piece
        else:
            swap[n - half] = piece.astype(bf16)
    for b in range(col_blocks):
        grad_col[b] = grad_turned[b].astype(bf16).T
    for n in range(n_col):
        col_out[n] = grad_col[:, n * col_part : (n + 1) * col_part, :]


def work(listing, used, tabs, row_near, row_far, col_in, tables, n_row, n_col, dims):
    row_blocks, col_blocks, size, width = dims
    first = tables is None
    row_part, col_part = size // n_row, size // n_col
    half = n_row // 2
    outs = [
        shape((half, row_blocks, row_part, width), f32),
        shape((half, row_blocks, row_part, width), bf16),
        shape((n_col, col_blocks, col_part, width), bf16),
    ]
    if first:
        outs += [shape((row_blocks, size, 128), f32), shape((col_blocks, 8, size), f32)]
    args = [listing, used, *tabs, row_near, row_far, col_in] + ([] if first else list(tables))
    res = pl.pallas_call(
        functools.partial(work_kernel, first, n_row, n_col),
        out_shape=outs,
        in_specs=[SMEM, SMEM] + [VMEM] * (len(args) - 2),
        out_specs=[VMEM] * len(outs),
        scratch_shapes=[
            pltpu.VMEM((row_blocks, size, width), bf16),
            pltpu.VMEM((row_blocks, width, size), bf16),
            pltpu.VMEM((col_blocks, size, width), bf16),
            pltpu.VMEM((row_blocks, size, width), f32),
            pltpu.VMEM((col_blocks, width, size), f32),
            pltpu.VMEM((col_blocks, size, width), bf16),
            pltpu.VMEM((size, size), f32),
            pltpu.VMEM((size, size), bf16),
        ],
        compiler_params=pltpu.CompilerParams(vmem_limit_bytes=LARGE),
        cost_estimate=cost(8 * 6 * size * size * width, 16 << 20),
    )(*args)
    return res[0], res[1], res[2], res[3:]


def merge_kernel(keep, got, out):
    out[...] = (keep[...] + got[...].astype(f32)).astype(out.dtype)


def merge(keep, got):
    return pl.pallas_call(
        merge_kernel,
        out_shape=shape(keep.shape, bf16),
        in_specs=[VMEM] * 2,
        out_specs=VMEM,
        compiler_params=pltpu.CompilerParams(vmem_limit_bytes=SMALL),
        cost_estimate=cost(0, 2 << 20),
    )(keep, got)


def update_kernel(row_emb, col_emb, row_parts, col_parts, *outs):
    for n, (emb, parts) in enumerate(((row_emb, row_parts), (col_emb, col_parts))):
        total = parts[0].astype(f32)
        for k in range(1, parts.shape[0]):
            total += parts[k].astype(f32)
        new = emb[...] - RATE * total
        outs[n][...] = new
        if len(outs) > 2:
            copies = outs[2 + n]
            rounded = new.astype(bf16).reshape(copies.shape[1:])
            for k in range(copies.shape[0]):
                copies[k] = rounded


def update(row_emb, col_emb, row_parts, col_parts, last):
    embs = (row_emb, col_emb)
    outs = [shape(e.shape, f32) for e in embs]
    if not last:
        outs += [
            shape((p.shape[0], e.shape[0] * e.shape[1], e.shape[2]), bf16)
            for e, p in zip(embs, (row_parts, col_parts))
        ]
    return pl.pallas_call(
        update_kernel,
        out_shape=outs,
        in_specs=[VMEM] * 4,
        out_specs=[VMEM] * len(outs),
        compiler_params=pltpu.CompilerParams(vmem_limit_bytes=SMALL),
        cost_estimate=cost(0, 2 << 20),
    )(row_emb, col_emb, row_parts, col_parts)


def shards(n_row_dev, n_col_dev, row_emb, col_emb, row_marg, col_marg, tile_list, tile_count, tile_data):
    listing = tile_list[0, 0].T
    used = tile_count[0]
    tiles = tile_data[0, 0]
    dims = (row_emb.shape[0], col_emb.shape[0], tiles.shape[-1], row_emb.shape[-1])
    half = n_col_dev // 2
    kinds = [[2 * k + core for k in range(half)] for core in range(2)]

    def along_col(x):
        return lax.all_to_all(x, "col", 0, 0, axis_index_groups=kinds)

    def along_row(x):
        return lax.all_to_all(x, "row", 0, 0)

    def across(x):
        return lax.ppermute(x, "col", [(k, k ^ 1) for k in range(n_col_dev)])

    row_pay, col_pay = pack(row_emb, row_marg, col_emb, col_marg, (half, n_row_dev))
    tabs = levels(used, tiles)
    tables = None
    for substep in range(2):
        row_near, col_in = along_col(row_pay), along_row(col_pay)
        keep, swap, col_out, made = work(
            listing, used, tabs, row_near, across(row_near), col_in, tables, n_col_dev, n_row_dev, dims
        )
        tables = tables or made
        col_parts = along_row(col_out)
        row_parts = along_col(merge(keep, across(swap)))
        if substep == 0:
            row_emb, col_emb, row_pay, col_pay = update(row_emb, col_emb, row_parts, col_parts, False)
    return tuple(update(row_emb, col_emb, row_parts, col_parts, True))


def solution(mesh):
    placed = (
        P("row", "col", None),
        P("col", "row", None),
        P("row", "col"),
        P("col", "row"),
        P("row", "col", None, None),
        P("row", "col"),
        P("row", "col", None, None, None),
    )
    return jax.shard_map(
        functools.partial(shards, mesh.shape["row"], mesh.shape["col"]),
        mesh=mesh,
        in_specs=placed,
        out_specs=(P("row", "col", None), P("col", "row", None)),
        check_vma=False,
    )
```

```python
import functools

import jax
import jax.numpy as jnp
from jax import lax
from jax.experimental import pallas as pl
from jax.experimental.pallas import tpu as pltpu
from jax.sharding import PartitionSpec as P

RATE = 0.0004
MARG_ROWS = 16
MARG_LANES = 128
ANY = pl.BlockSpec(memory_space=pl.ANY)
HBM = pl.BlockSpec(memory_space=pltpu.HBM)
VMEM = pl.BlockSpec(memory_space=pltpu.VMEM)
SMEM = pl.BlockSpec(memory_space=pltpu.SMEM)
SMALL = 12 << 20
LARGE = 32 << 20
LEVELS = 35 << 20
PACK = 62 << 20
f32, bf16 = jnp.float32, jnp.bfloat16
shape = jax.ShapeDtypeStruct


def cost(flops, moved):
    return pl.CostEstimate(flops=flops, bytes_accessed=moved, transcendentals=0)


def pack_kernel(row_emb, row_marg, col_emb, col_marg, row_out, col_out, *scratch):
    bufs, sem = scratch[:4], scratch[4]
    copies = [
        pltpu.make_async_copy(src, dst, sem.at[n])
        for n, (src, dst) in enumerate(zip((row_emb, row_marg, col_emb, col_marg), bufs))
    ]
    for copy in copies:
        copy.start()
    for n, out in enumerate((row_out, col_out)):
        copies[2 * n].wait()
        copies[2 * n + 1].wait()
        emb, marg = bufs[2 * n], bufs[2 * n + 1]
        blocks, part, width = emb.shape
        out[: blocks * part, :] = emb[...].astype(bf16).reshape(blocks * part, width)
        out[blocks * part :, :] = jnp.zeros((MARG_ROWS, width), bf16)
        for b in range(blocks):
            out[blocks * part + b : blocks * part + b + 1, :part] = marg[b : b + 1, :]


def pack(row_emb, row_marg, col_emb, col_marg):
    args = (row_emb, row_marg, col_emb, col_marg)
    return pl.pallas_call(
        pack_kernel,
        out_shape=[
            shape((e.shape[0] * e.shape[1] + MARG_ROWS, e.shape[2]), bf16) for e in args[::2]
        ],
        in_specs=[ANY] * 4,
        out_specs=[VMEM] * 2,
        scratch_shapes=[pltpu.VMEM(x.shape, x.dtype) for x in args]
        + [pltpu.SemaphoreType.DMA((4,))],
        compiler_params=pltpu.CompilerParams(vmem_limit_bytes=PACK),
        cost_estimate=cost(0, 1 << 20),
    )(*args)


def levels_kernel(used, tiles, logs, weights, token, tile_buf, sem):
    count = used[0]
    slots, size, _ = tile_buf.shape
    chunk = 64

    def load(slot):
        return pltpu.make_async_copy(tiles.at[slot], tile_buf.at[slot], sem.at[slot])

    for slot in range(slots):

        @pl.when(slot < count)
        def _():
            load(slot).start()

    token[...] = jnp.zeros_like(token)

    def one_tile(slot, carry):
        load(slot).wait()

        def one_chunk(n, carry):
            rows = pl.ds(pl.multiple_of(n * chunk, chunk), chunk)
            counts = tile_buf[slot, rows, :].astype(f32)
            level = jnp.maximum(counts, 1.0)
            logs[slot, rows, :] = jnp.log(level)
            weight = 0.1 + 0.25 * (level * lax.rsqrt(level))
            weights[slot, rows, :] = jnp.where(counts > 0.0, weight, 0.0)
            return carry

        lax.fori_loop(0, size // chunk, one_chunk, 0)
        return carry

    lax.fori_loop(0, count, one_tile, 0)


def levels(used, tiles):
    return pl.pallas_call(
        levels_kernel,
        out_shape=[shape(tiles.shape, f32)] * 2 + [shape((8, 128), f32)],
        in_specs=[SMEM, HBM],
        out_specs=[VMEM] * 3,
        scratch_shapes=[
            pltpu.VMEM(tiles.shape, jnp.int32),
            pltpu.SemaphoreType.DMA((tiles.shape[0],)),
        ],
        compiler_params=pltpu.CompilerParams(vmem_limit_bytes=LEVELS),
        cost_estimate=cost(0, 24 << 20),
    )(used, tiles)


def join_kernel(n_parts, *refs):
    out = refs[-1]
    for n in range(n_parts):
        out[n] = refs[n][...]


def join(parts, afters):
    return pl.pallas_call(
        functools.partial(join_kernel, len(parts)),
        out_shape=shape((len(parts), *parts[0].shape), parts[0].dtype),
        in_specs=[VMEM] * len(parts) + [ANY] * len(afters),
        out_specs=VMEM,
        compiler_params=pltpu.CompilerParams(vmem_limit_bytes=SMALL),
        cost_estimate=cost(0, 1 << 20),
    )(*parts, *afters)


def marg_table(pieces, owners, part, size):
    table = jnp.zeros((MARG_ROWS, size), f32)
    for piece, owner in zip(pieces, owners):
        tail = piece[piece.shape[0] - MARG_ROWS :, :MARG_LANES]
        k = lax.broadcasted_iota(jnp.int32, (MARG_LANES, size), 0)
        at = lax.broadcasted_iota(jnp.int32, (MARG_LANES, size), 1)
        place = ((at == k + owner * part) & (k < part)).astype(bf16)
        table += jnp.dot(tail, place, preferred_element_type=f32)
    return table


def work_kernel(first, n_row, n_col, row_owner, col_owner, *refs):
    refs = list(refs)

    def take(n):
        return [refs.pop(0) for _ in range(n)]

    listing, used, logs, weights, row_near, row_far = take(6)
    col_in = take(n_col)
    if not first:
        left, right = take(2)
    keep, swap = take(2)
    col_out = take(n_col)
    if first:
        left, right = take(2)
    row_panel, row_turned, col_panel, grad_row, grad_turned, grad_col, scores, signal = take(8)

    row_blocks, size, width = row_panel.shape
    col_blocks = col_panel.shape[0]
    row_part, col_part = size // n_row, size // n_col
    half = n_row // 2
    me_row, me_col = lax.axis_index("row"), lax.axis_index("col")
    row_owners = [me_col ^ k for k in row_owner]
    col_owners = [me_row ^ k for k in col_owner]
    row_zero, col_zero = me_row * row_blocks, me_col * col_blocks
    count = used[0]
    row_in = [side.at[n] for side in (row_near, row_far) for n in range(half)]

    for pieces, owners, panel, part in (
        (row_in, row_owners, row_panel, row_part),
        (col_in, col_owners, col_panel, col_part),
    ):
        for piece, owner in zip(pieces, owners):
            start = pl.multiple_of(owner * part, part)
            for b in range(panel.shape[0]):
                panel[b, pl.ds(start, part), :] = piece[b * part : (b + 1) * part, :]
    for b in range(row_blocks):
        row_turned[b] = row_panel[b].T
    grad_row[...] = jnp.zeros_like(grad_row)
    grad_turned[...] = jnp.zeros_like(grad_turned)

    if first:
        row_table = marg_table(row_in, row_owners, row_part, size).astype(bf16)
        for b in range(row_blocks):
            pick = (lax.broadcasted_iota(jnp.int32, (MARG_ROWS, 128), 0) == b).astype(bf16)
            left[b] = lax.dot_general(
                row_table, pick, (((0,), (0,)), ((), ())), preferred_element_type=f32
            )
        col_table = marg_table(col_in, col_owners, col_part, size)
        for b in range(col_blocks):
            right[b] = jnp.broadcast_to(col_table[b : b + 1, :], right.shape[1:])

    chunks = [slice(at, at + 256) for at in range(0, size, 256)]

    def place(slot):
        return listing[0, slot] - row_zero, listing[1, slot] - col_zero

    def make_scores(slot, rows):
        i, j = place(slot)
        scores[rows, :] = lax.dot_general(
            row_panel[i, rows, :], col_panel[j], (((1,), (1,)), ((), ())), preferred_element_type=f32
        )

    def make_signal(slot, rows):
        i, j = place(slot)
        marg_left = jnp.concatenate([left[i, rows, :]] * (size // 128), axis=1)
        diff = scores[rows, :] + marg_left + right[j, 0:1, :] - logs[slot, rows, :]
        weight = weights[slot, rows, :]
        flat = 0.5 * jnp.tanh(0.5 * diff) + 0.5
        signal[rows, :] = jnp.where(weight > 0.0, weight * diff, flat).astype(bf16)

    def add_grads(slot, rows):
        i, j = place(slot)
        piece = signal[rows, :]
        grad_row[i, rows, :] += jnp.dot(piece, col_panel[j], preferred_element_type=f32)
        grad_turned[j] += jnp.dot(row_turned[i, :, rows], piece, preferred_element_type=f32)

    def one_tile(slot, carry):
        for rows in chunks:
            add_grads(slot - 1, rows)
            make_signal(slot, rows)
            make_scores(jnp.minimum(slot + 1, count - 1), rows)
        return carry

    for rows in chunks:
        make_scores(0, rows)
    for rows in chunks:
        make_signal(0, rows)
        make_scores(jnp.minimum(1, count - 1), rows)
    lax.fori_loop(1, count, one_tile, 0)
    for rows in chunks:
        add_grads(count - 1, rows)

    for n in range(n_row):
        place, sibling = row_owner[n] >> 1, row_owner[n] & 1
        start = pl.multiple_of(row_owners[n] * row_part, row_part)
        piece = grad_row[:, pl.ds(start, row_part), :]
        if sibling:
            swap[place] = piece.astype(bf16)
        else:
            keep[place] = piece
    for b in range(col_blocks):
        grad_col[b] = grad_turned[b].astype(bf16).T
    for n in range(n_col):
        start = pl.multiple_of(col_owners[n] * col_part, col_part)
        col_out[n][...] = grad_col[:, pl.ds(start, col_part), :]


def work(listing, used, tabs, row_near, row_far, col_in, tables, row_owner, col_owner, dims):
    row_blocks, col_blocks, size, width = dims
    first = tables is None
    n_row, n_col = len(row_owner), len(col_owner)
    row_part, col_part = size // n_row, size // n_col
    half = n_row // 2
    outs = [
        shape((half, row_blocks, row_part, width), f32),
        shape((half, row_blocks, row_part, width), bf16),
    ] + [shape((col_blocks, col_part, width), bf16)] * n_col
    if first:
        outs += [shape((row_blocks, size, 128), f32), shape((col_blocks, 8, size), f32)]
    args = [listing, used, *tabs, row_near, row_far, *col_in] + ([] if first else list(tables))
    res = pl.pallas_call(
        functools.partial(work_kernel, first, n_row, n_col, row_owner, col_owner),
        out_shape=outs,
        in_specs=[SMEM, SMEM] + [VMEM] * (len(args) - 2),
        out_specs=[VMEM] * len(outs),
        scratch_shapes=[
            pltpu.VMEM((row_blocks, size, width), bf16),
            pltpu.VMEM((row_blocks, width, size), bf16),
            pltpu.VMEM((col_blocks, size, width), bf16),
            pltpu.VMEM((row_blocks, size, width), f32),
            pltpu.VMEM((col_blocks, width, size), f32),
            pltpu.VMEM((col_blocks, size, width), bf16),
            pltpu.VMEM((size, size), f32),
            pltpu.VMEM((size, size), bf16),
        ],
        compiler_params=pltpu.CompilerParams(vmem_limit_bytes=LARGE),
        cost_estimate=cost(8 * 6 * size * size * width, 16 << 20),
    )(*args)
    return res[0], res[1], res[2 : 2 + n_col], res[2 + n_col :]


def merge_kernel(kept, keep, got, *outs):
    for n, out in enumerate(outs):
        out[...] = (keep[n] + got[n].astype(f32)).astype(out.dtype)


def merge(keep, got, kept):
    n, *piece = keep.shape
    return pl.pallas_call(
        functools.partial(merge_kernel, kept),
        out_shape=[shape(tuple(piece), f32 if k in kept else bf16) for k in range(n)],
        in_specs=[VMEM] * 2,
        out_specs=[VMEM] * n,
        compiler_params=pltpu.CompilerParams(vmem_limit_bytes=SMALL),
        cost_estimate=cost(0, 2 << 20),
    )(keep, got)


def add_kernel(*refs):
    total = refs[0][...]
    for ref in refs[1:-1]:
        total += ref[...].astype(f32)
    refs[-1][...] = total.astype(bf16)


def add(own, parts):
    return pl.pallas_call(
        add_kernel,
        out_shape=shape(own.shape, bf16),
        in_specs=[VMEM] * (1 + len(parts)),
        out_specs=VMEM,
        compiler_params=pltpu.CompilerParams(vmem_limit_bytes=SMALL),
        cost_estimate=cost(0, 1 << 20),
    )(own, *parts)


def update_kernel(n_row, n_col, row_emb, col_emb, *refs):
    row_parts, col_parts, outs = refs[:n_row], refs[n_row : n_row + n_col], refs[n_row + n_col :]
    for n, (emb, parts) in enumerate(((row_emb, row_parts), (col_emb, col_parts))):
        total = parts[0][...].astype(f32)
        for part in parts[1:]:
            total += part[...].astype(f32)
        new = emb[...] - RATE * total
        outs[n][...] = new
        if len(outs) > 2:
            outs[2 + n][...] = new.astype(bf16).reshape(outs[2 + n].shape)


def update(row_emb, col_emb, row_parts, col_parts, last):
    embs = (row_emb, col_emb)
    outs = [shape(e.shape, f32) for e in embs]
    if not last:
        outs += [shape((e.shape[0] * e.shape[1], e.shape[2]), bf16) for e in embs]
    return pl.pallas_call(
        functools.partial(update_kernel, len(row_parts), len(col_parts)),
        out_shape=outs,
        in_specs=[VMEM] * (2 + len(row_parts) + len(col_parts)),
        out_specs=[VMEM] * len(outs),
        compiler_params=pltpu.CompilerParams(vmem_limit_bytes=SMALL),
        cost_estimate=cost(0, 2 << 20),
    )(row_emb, col_emb, *row_parts, *col_parts)


def send(x, axis, count, mask):
    return lax.ppermute(x, axis, [(k, k ^ mask) for k in range(count)])


def shards(n_row_dev, n_col_dev, row_emb, col_emb, row_marg, col_marg, tile_list, tile_count, tile_data):
    listing = tile_list[0, 0].T
    used = tile_count[0]
    tiles = tile_data[0, 0]
    dims = (row_emb.shape[0], col_emb.shape[0], tiles.shape[-1], row_emb.shape[-1])
    half = n_col_dev // 2
    far = half // 2
    near = range(1, far)
    row_owner = [2 * k for k in range(half)] + [2 * k + 1 for k in range(half)]
    col_owner = list(range(n_row_dev))

    def hop(x, distance):
        return send(x, "col", n_col_dev, 2 * distance)

    row_pay, col_pay = pack(row_emb, row_marg, col_emb, col_marg)
    *tabs, made_tabs = levels(used, tiles)
    tables = None
    for substep in range(2):
        crossed = hop(row_pay, far)
        row_near = [row_pay] + [hop(row_pay, k) for k in near] + [crossed] + [hop(crossed, k) for k in near]
        col_in = [col_pay] + [send(col_pay, "row", n_row_dev, k) for k in col_owner[1:]]
        row_near = join(row_near, col_in[1:] + ([made_tabs] if substep == 0 else []))
        row_far = send(row_near, "col", n_col_dev, 1)
        keep, swap, col_out, made = work(
            listing, used, tabs, row_near, row_far, col_in, tables, row_owner, col_owner, dims
        )
        tables = tables or made
        merged = merge(keep, send(swap, "col", n_col_dev, 1), (0, far))
        crossing = add(merged[far], [hop(merged[far + k], k) for k in near])
        col_parts = [col_out[0]] + [send(col_out[k], "row", n_row_dev, k) for k in col_owner[1:]]
        row_parts = [merged[0], hop(crossing, far)] + [hop(merged[k], k) for k in near]
        if substep == 0:
            row_emb, col_emb, row_pay, col_pay = update(row_emb, col_emb, row_parts, col_parts, False)
    return tuple(update(row_emb, col_emb, row_parts, col_parts, True))


def solution(mesh):
    placed = (
        P("row", "col", None),
        P("col", "row", None),
        P("row", "col"),
        P("col", "row"),
        P("row", "col", None, None),
        P("row", "col"),
        P("row", "col", None, None, None),
    )
    return jax.shard_map(
        functools.partial(shards, mesh.shape["row"], mesh.shape["col"]),
        mesh=mesh,
        in_specs=placed,
        out_specs=(P("row", "col", None), P("col", "row", None)),
        check_vma=False,
    )
```

```python
import functools

import jax
import jax.numpy as jnp
from jax import lax
from jax.experimental import pallas as pl
from jax.experimental.pallas import tpu as pltpu
from jax.sharding import PartitionSpec as P

RATE = 0.0004
MARG_ROWS = 16
MARG_LANES = 128
ANY = pl.BlockSpec(memory_space=pl.ANY)
HBM = pl.BlockSpec(memory_space=pltpu.HBM)
VMEM = pl.BlockSpec(memory_space=pltpu.VMEM)
SMEM = pl.BlockSpec(memory_space=pltpu.SMEM)
SMALL = 12 << 20
LARGE = 14 << 20
LEVELS = 35 << 20
PACK = 62 << 20
WORK_BYTES = 1 << 20
f32, bf16 = jnp.float32, jnp.bfloat16
shape = jax.ShapeDtypeStruct


def cost(flops, moved):
    return pl.CostEstimate(flops=flops, bytes_accessed=moved, transcendentals=0)


def pack_kernel(row_emb, row_marg, col_emb, col_marg, row_out, col_out, *scratch):
    bufs, sem = scratch[:4], scratch[4]
    copies = [
        pltpu.make_async_copy(src, dst, sem.at[n])
        for n, (src, dst) in enumerate(zip((row_emb, row_marg, col_emb, col_marg), bufs))
    ]
    for copy in copies:
        copy.start()
    for n, out in enumerate((row_out, col_out)):
        copies[2 * n].wait()
        copies[2 * n + 1].wait()
        emb, marg = bufs[2 * n], bufs[2 * n + 1]
        blocks, part, width = emb.shape
        out[: blocks * part, :] = emb[...].astype(bf16).reshape(blocks * part, width)
        out[blocks * part :, :] = jnp.zeros((MARG_ROWS, width), bf16)
        for b in range(blocks):
            out[blocks * part + b : blocks * part + b + 1, :part] = marg[b : b + 1, :]


def pack(row_emb, row_marg, col_emb, col_marg):
    args = (row_emb, row_marg, col_emb, col_marg)
    return pl.pallas_call(
        pack_kernel,
        out_shape=[
            shape((e.shape[0] * e.shape[1] + MARG_ROWS, e.shape[2]), bf16) for e in args[::2]
        ],
        in_specs=[ANY] * 4,
        out_specs=[VMEM] * 2,
        scratch_shapes=[pltpu.VMEM(x.shape, x.dtype) for x in args]
        + [pltpu.SemaphoreType.DMA((4,))],
        compiler_params=pltpu.CompilerParams(vmem_limit_bytes=PACK),
        cost_estimate=cost(0, 1 << 20),
    )(*args)


def levels_kernel(used, tiles, logs, weights, token, tile_buf, sem):
    count = used[0]
    slots, size, _ = tile_buf.shape
    chunk = 64

    def load(slot):
        return pltpu.make_async_copy(tiles.at[slot], tile_buf.at[slot], sem.at[slot])

    for slot in range(slots):

        @pl.when(slot < count)
        def _():
            load(slot).start()

    token[...] = jnp.zeros_like(token)

    def one_tile(slot, carry):
        load(slot).wait()

        def one_chunk(n, carry):
            rows = pl.ds(pl.multiple_of(n * chunk, chunk), chunk)
            counts = tile_buf[slot, rows, :].astype(f32)
            level = jnp.maximum(counts, 1.0)
            logs[slot, rows, :] = jnp.log(level)
            weight = 0.1 + 0.25 * (level * lax.rsqrt(level))
            weights[slot, rows, :] = jnp.where(counts > 0.0, weight, 0.0)
            return carry

        lax.fori_loop(0, size // chunk, one_chunk, 0)
        return carry

    lax.fori_loop(0, count, one_tile, 0)


def levels(used, tiles):
    return pl.pallas_call(
        levels_kernel,
        out_shape=[shape(tiles.shape, f32)] * 2 + [shape((8, 128), f32)],
        in_specs=[SMEM, HBM],
        out_specs=[VMEM] * 3,
        scratch_shapes=[
            pltpu.VMEM(tiles.shape, jnp.int32),
            pltpu.SemaphoreType.DMA((tiles.shape[0],)),
        ],
        compiler_params=pltpu.CompilerParams(vmem_limit_bytes=LEVELS),
        cost_estimate=cost(0, 24 << 20),
    )(used, tiles)


def join_kernel(n_parts, *refs):
    out = refs[-1]
    for n in range(n_parts):
        out[n] = refs[n][...]


def join(parts, afters):
    return pl.pallas_call(
        functools.partial(join_kernel, len(parts)),
        out_shape=shape((len(parts), *parts[0].shape), parts[0].dtype),
        in_specs=[VMEM] * len(parts) + [ANY] * len(afters),
        out_specs=VMEM,
        compiler_params=pltpu.CompilerParams(vmem_limit_bytes=SMALL),
        cost_estimate=cost(0, 1 << 20),
    )(*parts, *afters)


def marg_table(pieces, starts, part, size):
    table = jnp.zeros((MARG_ROWS, size), f32)
    for piece, start in zip(pieces, starts):
        tail = piece[piece.shape[0] - MARG_ROWS :, :MARG_LANES]
        k = lax.broadcasted_iota(jnp.int32, (MARG_LANES, size), 0)
        at = lax.broadcasted_iota(jnp.int32, (MARG_LANES, size), 1)
        place = ((at == k + start) & (k < part)).astype(bf16)
        table += jnp.dot(tail, place, preferred_element_type=f32)
    return table


def fill(panel, pieces, starts, part):
    for piece, start in zip(pieces, starts):
        for b in range(panel.shape[0]):
            panel[b, pl.ds(start, part), :] = piece[b * part : (b + 1) * part, :]


class Plan:
    def __init__(self, row_owner, col_owner, n_col, first, opening, closing):
        self.row_owner, self.col_owner, self.n_col = row_owner, col_owner, n_col
        self.first, self.opening, self.closing = first, opening, closing


def work_kernel(plan, *refs):
    refs = list(refs)

    def take(n):
        return [refs.pop(0) for _ in range(n)]

    first, opening, closing = plan.first, plan.opening, plan.closing
    n_row, n_group = len(plan.row_owner), len(plan.col_owner)
    half = n_row // 2
    listing, used, logs, weights = take(4)
    if opening:
        row_near, row_far = take(2)
    else:
        row_panel, row_turned, row_before = take(3)
    col_in = take(n_group)
    if not (first and opening):
        (left,) = take(1)
    if not first:
        (right,) = take(1)
    if closing:
        keep, swap = take(2)
    else:
        row_panel, row_turned, grad_row = take(3)
    col_out = take(n_group)
    if first and opening:
        (left,) = take(1)
    if first:
        (right,) = take(1)
    col_panel, grad_turned, grad_col, scores, signal = take(5)
    if closing:
        (grad_row,) = take(1)
    if opening and closing:
        row_panel, row_turned = take(2)

    row_blocks, size, width = row_panel.shape
    col_blocks, columns, _ = col_panel.shape
    row_part, col_part = size // n_row, size // plan.n_col
    me_row, me_col = lax.axis_index("row"), lax.axis_index("col")
    row_starts = [pl.multiple_of((me_col ^ k) * row_part, row_part) for k in plan.row_owner]
    col_starts = [pl.multiple_of((me_row ^ k) * col_part, col_part) for k in plan.col_owner]
    whole = columns == size
    places = col_starts if whole else [n * col_part for n in range(n_group)]
    row_zero, col_zero = me_row * row_blocks, me_col * col_blocks
    count = used[0]

    if opening:
        row_in = [side.at[n] for side in (row_near, row_far) for n in range(half)]
        fill(row_panel, row_in, row_starts, row_part)
        for b in range(row_blocks):
            row_turned[b] = row_panel[b].T
    fill(col_panel, col_in, places, col_part)
    grad_row[...] = jnp.zeros_like(grad_row)
    grad_turned[...] = jnp.zeros_like(grad_turned)

    if first and opening:
        row_table = marg_table(row_in, row_starts, row_part, size).astype(bf16)
        for b in range(row_blocks):
            pick = (lax.broadcasted_iota(jnp.int32, (MARG_ROWS, 128), 0) == b).astype(bf16)
            left[b] = lax.dot_general(
                row_table, pick, (((0,), (0,)), ((), ())), preferred_element_type=f32
            )
    if first:
        col_table = marg_table(col_in, places, col_part, columns)
        for b in range(col_blocks):
            right[b] = jnp.broadcast_to(col_table[b : b + 1, :], right.shape[1:])

    chunks = [slice(at, at + 256) for at in range(0, size, 256)]

    def place(slot):
        return listing[0, slot] - row_zero, listing[1, slot] - col_zero

    def of_tile(ref, slot, rows):
        if whole:
            return ref[slot, rows, :]
        return jnp.concatenate([ref[slot, rows, pl.ds(start, col_part)] for start in col_starts], axis=1)

    def make_scores(slot, rows):
        i, j = place(slot)
        scores[rows, :] = lax.dot_general(
            row_panel[i, rows, :], col_panel[j], (((1,), (1,)), ((), ())), preferred_element_type=f32
        )

    def make_signal(slot, rows):
        i, j = place(slot)
        marg_left = jnp.concatenate([left[i, rows, :]] * (columns // 128), axis=1)
        diff = scores[rows, :] + marg_left + right[j, 0:1, :] - of_tile(logs, slot, rows)
        weight = of_tile(weights, slot, rows)
        flat = 0.5 * jnp.tanh(0.5 * diff) + 0.5
        signal[rows, :] = jnp.where(weight > 0.0, weight * diff, flat).astype(bf16)

    def add_grads(slot, rows):
        i, j = place(slot)
        piece = signal[rows, :]
        grad_row[i, rows, :] += jnp.dot(piece, col_panel[j], preferred_element_type=f32)
        grad_turned[j] += jnp.dot(row_turned[i, :, rows], piece, preferred_element_type=f32)

    def one_tile(slot, carry):
        for rows in chunks:
            add_grads(slot - 1, rows)
            make_signal(slot, rows)
            make_scores(jnp.minimum(slot + 1, count - 1), rows)
        return carry

    for rows in chunks:
        make_scores(0, rows)
    for rows in chunks:
        make_signal(0, rows)
        make_scores(jnp.minimum(1, count - 1), rows)
    lax.fori_loop(1, count, one_tile, 0)
    for rows in chunks:
        add_grads(count - 1, rows)

    if closing:
        for n in range(n_row):
            at, sibling = plan.row_owner[n] >> 1, plan.row_owner[n] & 1
            piece = grad_row[:, pl.ds(row_starts[n], row_part), :]
            if not opening:
                piece += row_before[:, pl.ds(row_starts[n], row_part), :]
            if sibling:
                swap[at] = piece.astype(bf16)
            else:
                keep[at] = piece
    for b in range(col_blocks):
        grad_col[b] = grad_turned[b].astype(bf16).T
    for n in range(n_group):
        col_out[n][...] = grad_col[:, pl.ds(places[n], col_part), :]


def work(plan, listing, used, tabs, rows, col_in, left, right, dims):
    row_blocks, col_blocks, size, width = dims
    first, opening, closing = plan.first, plan.opening, plan.closing
    n_row, n_group = len(plan.row_owner), len(plan.col_owner)
    row_part, col_part = size // n_row, size // plan.n_col
    half, columns = n_row // 2, n_group * col_part
    panel = (row_blocks, size, width)
    turned = (row_blocks, width, size)
    if closing:
        outs = [shape((half, row_blocks, row_part, width), kind) for kind in (f32, bf16)]
    else:
        outs = [shape(panel, bf16), shape(turned, bf16), shape(panel, f32)]
    n_state = len(outs)
    outs += [shape((col_blocks, col_part, width), bf16)] * n_group
    args = [listing, used, *tabs, *rows, *col_in]
    if first and opening:
        outs.append(shape((row_blocks, size, 128), f32))
    else:
        args.append(left)
    if first:
        outs.append(shape((col_blocks, 8, columns), f32))
    else:
        args.append(right)
    scratch = [
        pltpu.VMEM((col_blocks, columns, width), bf16),
        pltpu.VMEM((col_blocks, width, columns), f32),
        pltpu.VMEM((col_blocks, columns, width), bf16),
        pltpu.VMEM((size, columns), f32),
        pltpu.VMEM((size, columns), bf16),
    ]
    if closing:
        scratch.append(pltpu.VMEM(panel, f32))
    if opening and closing:
        scratch += [pltpu.VMEM(panel, bf16), pltpu.VMEM(turned, bf16)]
    res = pl.pallas_call(
        functools.partial(work_kernel, plan),
        out_shape=outs,
        in_specs=[SMEM, SMEM] + [VMEM] * (len(args) - 2),
        out_specs=[VMEM] * len(outs),
        scratch_shapes=scratch,
        compiler_params=pltpu.CompilerParams(vmem_limit_bytes=LARGE),
        cost_estimate=cost(0, WORK_BYTES),
    )(*args)
    state, res = res[:n_state], res[n_state:]
    pieces, res = res[:n_group], res[n_group:]
    if first:
        right = res[-1]
    if first and opening:
        left = res[0]
    return state, pieces, left, right


def merge_kernel(keep, got, *outs):
    for n, out in enumerate(outs):
        out[...] = (keep[n] + got[n].astype(f32)).astype(out.dtype)


def merge(keep, got, kept):
    n, *piece = keep.shape
    return pl.pallas_call(
        merge_kernel,
        out_shape=[shape(tuple(piece), f32 if k in kept else bf16) for k in range(n)],
        in_specs=[VMEM] * 2,
        out_specs=[VMEM] * n,
        compiler_params=pltpu.CompilerParams(vmem_limit_bytes=SMALL),
        cost_estimate=cost(0, 2 << 20),
    )(keep, got)


def add_kernel(*refs):
    total = refs[0][...]
    for ref in refs[1:-1]:
        total += ref[...].astype(f32)
    refs[-1][...] = total.astype(bf16)


def add(own, parts):
    return pl.pallas_call(
        add_kernel,
        out_shape=shape(own.shape, bf16),
        in_specs=[VMEM] * (1 + len(parts)),
        out_specs=VMEM,
        compiler_params=pltpu.CompilerParams(vmem_limit_bytes=SMALL),
        cost_estimate=cost(0, 1 << 20),
    )(own, *parts)


def update_kernel(n_row, n_col, row_emb, col_emb, *refs):
    row_parts, col_parts, outs = refs[:n_row], refs[n_row : n_row + n_col], refs[n_row + n_col :]
    for n, (emb, parts) in enumerate(((row_emb, row_parts), (col_emb, col_parts))):
        total = parts[0][...].astype(f32)
        for part in parts[1:]:
            total += part[...].astype(f32)
        new = emb[...] - RATE * total
        outs[n][...] = new
        if len(outs) > 2:
            outs[2 + n][...] = new.astype(bf16).reshape(outs[2 + n].shape)


def update(row_emb, col_emb, row_parts, col_parts, last):
    embs = (row_emb, col_emb)
    outs = [shape(e.shape, f32) for e in embs]
    if not last:
        outs += [shape((e.shape[0] * e.shape[1], e.shape[2]), bf16) for e in embs]
    return pl.pallas_call(
        functools.partial(update_kernel, len(row_parts), len(col_parts)),
        out_shape=outs,
        in_specs=[VMEM] * (2 + len(row_parts) + len(col_parts)),
        out_specs=[VMEM] * len(outs),
        compiler_params=pltpu.CompilerParams(vmem_limit_bytes=SMALL),
        cost_estimate=cost(0, 2 << 20),
    )(row_emb, col_emb, *row_parts, *col_parts)


def send(x, axis, count, mask):
    return lax.ppermute(x, axis, [(k, k ^ mask) for k in range(count)])


def shards(n_row_dev, n_col_dev, row_emb, col_emb, row_marg, col_marg, tile_list, tile_count, tile_data):
    listing = tile_list[0, 0].T
    used = tile_count[0]
    tiles = tile_data[0, 0]
    dims = (row_emb.shape[0], col_emb.shape[0], tiles.shape[-1], row_emb.shape[-1])
    half = n_col_dev // 2
    far = half // 2
    near = range(1, far)
    row_owner = [2 * k for k in range(half)] + [2 * k + 1 for k in range(half)]
    col_owner = list(range(n_row_dev))

    def hop(x, distance):
        return send(x, "col", n_col_dev, 2 * distance)

    if n_row_dev == 4 and dims[2] // n_row_dev % 128 == 0:
        groups, late = [[0, 1], [2, 3]], [3]
    else:
        groups, late = [list(range(n_row_dev))], []
    calls = len(groups)

    row_pay, col_pay = pack(row_emb, row_marg, col_emb, col_marg)
    *tabs, made_tabs = levels(used, tiles)
    left, right = None, [None] * calls
    for substep in range(2):
        early = {k: send(col_pay, "row", n_row_dev, k) for k in range(1, n_row_dev) if k not in late}
        crossed = hop(row_pay, far)
        row_near = [row_pay] + [hop(row_pay, k) for k in near] + [crossed] + [hop(crossed, k) for k in near]
        row_near = join(row_near, [*early.values()] + ([made_tabs] if substep == 0 else []))
        rows = [row_near, send(row_near, "col", n_col_dev, 1)]
        col_parts = []
        for n, group in enumerate(groups):
            plan = Plan(row_owner, group, n_row_dev, substep == 0, n == 0, n == calls - 1)
            if n == 0:
                col_in = {0: col_pay} | early
            else:
                col_in |= {k: send(col_pay, "row", n_row_dev, k) for k in late}
            rows, made, left, right[n] = work(
                plan, listing, used, tabs, rows, [col_in[k] for k in group], left, right[n], dims
            )
            col_parts += [send(x, "row", n_row_dev, k) if k else x for k, x in zip(group, made)]
        keep, swap = rows
        merged = merge(keep, send(swap, "col", n_col_dev, 1), (0, far))
        crossing = add(merged[far], [hop(merged[far + k], k) for k in near])
        row_parts = [merged[0], hop(crossing, far)] + [hop(merged[k], k) for k in near]
        if substep == 0:
            row_emb, col_emb, row_pay, col_pay = update(row_emb, col_emb, row_parts, col_parts, False)
    return tuple(update(row_emb, col_emb, row_parts, col_parts, True))


def solution(mesh):
    placed = (
        P("row", "col", None),
        P("col", "row", None),
        P("row", "col"),
        P("col", "row"),
        P("row", "col", None, None),
        P("row", "col"),
        P("row", "col", None, None, None),
    )
    return jax.shard_map(
        functools.partial(shards, mesh.shape["row"], mesh.shape["col"]),
        mesh=mesh,
        in_specs=placed,
        out_specs=(P("row", "col", None), P("col", "row", None)),
        check_vma=False,
    )
```

```python
import functools

import jax
import jax.numpy as jnp
from jax import lax
from jax.experimental import pallas as pl
from jax.experimental.pallas import tpu as pltpu
from jax.sharding import PartitionSpec as P

RATE = 0.0004
MARG_ROWS = 16
MARG_LANES = 128
ANY = pl.BlockSpec(memory_space=pl.ANY)
HBM = pl.BlockSpec(memory_space=pltpu.HBM)
VMEM = pl.BlockSpec(memory_space=pltpu.VMEM)
SMEM = pl.BlockSpec(memory_space=pltpu.SMEM)
SMALL = 12 << 20
LARGE = 16 << 20
LEVELS = 31 << 20
PACK = 62 << 20
f32, bf16 = jnp.float32, jnp.bfloat16
shape = jax.ShapeDtypeStruct


def cost(flops, moved):
    return pl.CostEstimate(flops=flops, bytes_accessed=moved, transcendentals=0)


def pack_kernel(row_emb, row_marg, col_emb, col_marg, row_out, col_out, *scratch):
    bufs, sem = scratch[:4], scratch[4]
    copies = [
        pltpu.make_async_copy(src, dst, sem.at[n])
        for n, (src, dst) in enumerate(zip((row_emb, row_marg, col_emb, col_marg), bufs))
    ]
    for copy in copies:
        copy.start()
    for n, out in enumerate((row_out, col_out)):
        copies[2 * n].wait()
        copies[2 * n + 1].wait()
        emb, marg = bufs[2 * n], bufs[2 * n + 1]
        blocks, part, width = emb.shape
        out[: blocks * part, :] = emb[...].astype(bf16).reshape(blocks * part, width)
        out[blocks * part :, :] = jnp.zeros((MARG_ROWS, width), bf16)
        for b in range(blocks):
            out[blocks * part + b : blocks * part + b + 1, :part] = marg[b : b + 1, :]


def pack(row_emb, row_marg, col_emb, col_marg):
    args = (row_emb, row_marg, col_emb, col_marg)
    return pl.pallas_call(
        pack_kernel,
        out_shape=[
            shape((e.shape[0] * e.shape[1] + MARG_ROWS, e.shape[2]), bf16) for e in args[::2]
        ],
        in_specs=[ANY] * 4,
        out_specs=[VMEM] * 2,
        scratch_shapes=[pltpu.VMEM(x.shape, x.dtype) for x in args]
        + [pltpu.SemaphoreType.DMA((4,))],
        compiler_params=pltpu.CompilerParams(vmem_limit_bytes=PACK),
        cost_estimate=cost(0, 1 << 20),
    )(*args)


def levels_kernel(used, tiles, logs, weights, token, tile_buf, sem):
    slots, size, _ = tile_buf.shape
    count = used[0]
    chunk = 64

    def load(slot):
        return pltpu.make_async_copy(tiles.at[slot], tile_buf.at[slot], sem.at[slot])

    for slot in range(slots):

        @pl.when(slot < count)
        def _():
            load(slot).start()

    token[...] = jnp.zeros_like(token)

    def one_tile(slot, carry):
        load(slot).wait()

        def one_chunk(n, carry):
            rows = pl.ds(pl.multiple_of(n * chunk, chunk), chunk)
            counts = tile_buf[slot, rows, :].astype(f32)
            level = jnp.maximum(counts, 1.0)
            logs[slot, rows, :] = jnp.log(level)
            weight = 0.1 + 0.25 * (level * lax.rsqrt(level))
            weights[slot, rows, :] = jnp.where(counts > 0.0, weight, 0.0)
            return carry

        lax.fori_loop(0, size // chunk, one_chunk, 0)
        return carry

    lax.fori_loop(0, count, one_tile, 0)


def levels(used, tiles):
    return pl.pallas_call(
        levels_kernel,
        out_shape=[shape(tiles.shape, f32)] * 2 + [shape((8, 128), f32)],
        in_specs=[SMEM, HBM],
        out_specs=[VMEM] * 3,
        scratch_shapes=[
            pltpu.VMEM(tiles.shape, jnp.int32),
            pltpu.SemaphoreType.DMA((tiles.shape[0],)),
        ],
        compiler_params=pltpu.CompilerParams(vmem_limit_bytes=LEVELS),
        cost_estimate=cost(0, 12 << 20),
    )(used, tiles)


def join_kernel(n_parts, *refs):
    out = refs[-1]
    for n in range(n_parts):
        out[n] = refs[n][...]


def join(parts, afters):
    return pl.pallas_call(
        functools.partial(join_kernel, len(parts)),
        out_shape=shape((len(parts), *parts[0].shape), parts[0].dtype),
        in_specs=[VMEM] * len(parts) + [ANY] * len(afters),
        out_specs=VMEM,
        compiler_params=pltpu.CompilerParams(vmem_limit_bytes=SMALL),
        cost_estimate=cost(0, 1 << 20),
    )(*parts, *afters)


def marg_table(pieces, owners, part, size):
    table = jnp.zeros((MARG_ROWS, size), f32)
    for piece, owner in zip(pieces, owners):
        tail = piece[piece.shape[0] - MARG_ROWS :, :MARG_LANES]
        k = lax.broadcasted_iota(jnp.int32, (MARG_LANES, size), 0)
        at = lax.broadcasted_iota(jnp.int32, (MARG_LANES, size), 1)
        place = ((at == k + owner * part) & (k < part)).astype(bf16)
        table += jnp.dot(tail, place, preferred_element_type=f32)
    return table


def work_kernel(first, n_row, n_col, row_owner, col_owner, *refs):
    refs = list(refs)

    def take(n):
        return [refs.pop(0) for _ in range(n)]

    listing, used, logs, weights, row_near, row_far = take(6)
    col_in = take(n_col)
    if not first:
        left, right = take(2)
    keep, swap = take(2)
    col_out = take(n_col)
    if first:
        left, right = take(2)
    row_panel, row_turned, col_panel, grad_row, grad_turned, grad_col, even, odd = take(8)

    row_blocks, size, width = row_panel.shape
    col_blocks = col_panel.shape[0]
    row_part, col_part = size // n_row, size // n_col
    half = n_row // 2
    me_row, me_col = lax.axis_index("row"), lax.axis_index("col")
    row_owners = [me_col ^ k for k in row_owner]
    col_owners = [me_row ^ k for k in col_owner]
    row_zero, col_zero = me_row * row_blocks, me_col * col_blocks
    count = used[0]
    row_in = [side.at[n] for side in (row_near, row_far) for n in range(half)]

    for pieces, owners, panel, part in (
        (row_in, row_owners, row_panel, row_part),
        (col_in, col_owners, col_panel, col_part),
    ):
        for piece, owner in zip(pieces, owners):
            start = pl.multiple_of(owner * part, part)
            for b in range(panel.shape[0]):
                panel[b, pl.ds(start, part), :] = piece[b * part : (b + 1) * part, :]
    for b in range(row_blocks):
        row_turned[b] = row_panel[b].T
    grad_row[...] = jnp.zeros_like(grad_row)
    grad_turned[...] = jnp.zeros_like(grad_turned)

    if first:
        row_table = marg_table(row_in, row_owners, row_part, size).astype(bf16)
        for b in range(row_blocks):
            pick = (lax.broadcasted_iota(jnp.int32, (MARG_ROWS, 128), 0) == b).astype(bf16)
            left[b] = lax.dot_general(
                row_table, pick, (((0,), (0,)), ((), ())), preferred_element_type=f32
            )
        col_table = marg_table(col_in, col_owners, col_part, size)
        for b in range(col_blocks):
            right[b] = jnp.broadcast_to(col_table[b : b + 1, :], right.shape[1:])

    chunks = [slice(at, at + 256) for at in range(0, size, 256)]

    def place(slot):
        return listing[0, slot] - row_zero, listing[1, slot] - col_zero

    def make_signal(slot, rows, signal):
        i, j = place(slot)
        scores = lax.dot_general(
            row_panel[i, rows, :], col_panel[j], (((1,), (1,)), ((), ())), preferred_element_type=f32
        )
        marg_left = jnp.concatenate([left[i, rows, :]] * (size // 128), axis=1)
        diff = scores + marg_left + right[j, 0:1, :] - logs[slot, rows, :]
        weight = weights[slot, rows, :]
        flat = 0.5 * jnp.tanh(0.5 * diff) + 0.5
        signal[rows, :] = jnp.where(weight > 0.0, weight * diff, flat).astype(bf16)

    def add_row(slot, rows, signal):
        i, j = place(slot)
        grad_row[i, rows, :] += jnp.dot(signal[rows, :], col_panel[j], preferred_element_type=f32)

    def add_col(slot, signal):
        i, j = place(slot)
        grad_turned[j] += jnp.dot(row_turned[i], signal[...], preferred_element_type=f32)

    def step(slot, before, now):
        for rows in chunks:
            make_signal(slot, rows, now)
            add_row(slot - 1, rows, before)
        add_col(slot - 1, before)

    pairs = (count - 1) // 2

    def pair(n, carry):
        step(2 * n + 1, even, odd)
        step(2 * n + 2, odd, even)
        return carry

    for rows in chunks:
        make_signal(0, rows, even)
    lax.fori_loop(0, pairs, pair, 0)

    @pl.when(2 * pairs + 1 < count)
    def _():
        step(2 * pairs + 1, even, odd)

    for parity, signal in enumerate((even, odd)):

        @pl.when(lax.rem(count - 1, 2) == parity)
        def _():
            for rows in chunks:
                add_row(count - 1, rows, signal)
            add_col(count - 1, signal)

    for n in range(n_row):
        place, sibling = row_owner[n] >> 1, row_owner[n] & 1
        start = pl.multiple_of(row_owners[n] * row_part, row_part)
        piece = grad_row[:, pl.ds(start, row_part), :]
        if sibling:
            swap[place] = piece.astype(bf16)
        else:
            keep[place] = piece
    for b in range(col_blocks):
        grad_col[b] = grad_turned[b].astype(bf16).T
    for n in range(n_col):
        start = pl.multiple_of(col_owners[n] * col_part, col_part)
        col_out[n][...] = grad_col[:, pl.ds(start, col_part), :]


def work(listing, used, tabs, row_near, row_far, col_in, tables, row_owner, col_owner, dims):
    row_blocks, col_blocks, size, width = dims
    first = tables is None
    n_row, n_col = len(row_owner), len(col_owner)
    row_part, col_part = size // n_row, size // n_col
    half = n_row // 2
    outs = [
        shape((half, row_blocks, row_part, width), f32),
        shape((half, row_blocks, row_part, width), bf16),
    ] + [shape((col_blocks, col_part, width), bf16)] * n_col
    if first:
        outs += [shape((row_blocks, size, 128), f32), shape((col_blocks, 8, size), f32)]
    args = [listing, used, *tabs, row_near, row_far, *col_in] + ([] if first else list(tables))
    res = pl.pallas_call(
        functools.partial(work_kernel, first, n_row, n_col, row_owner, col_owner),
        out_shape=outs,
        in_specs=[SMEM, SMEM] + [VMEM] * (len(args) - 2),
        out_specs=[VMEM] * len(outs),
        scratch_shapes=[
            pltpu.VMEM((row_blocks, size, width), bf16),
            pltpu.VMEM((row_blocks, width, size), bf16),
            pltpu.VMEM((col_blocks, size, width), bf16),
            pltpu.VMEM((row_blocks, size, width), f32),
            pltpu.VMEM((col_blocks, width, size), f32),
            pltpu.VMEM((col_blocks, size, width), bf16),
            pltpu.VMEM((size, size), bf16),
            pltpu.VMEM((size, size), bf16),
        ],
        compiler_params=pltpu.CompilerParams(vmem_limit_bytes=LARGE),
        cost_estimate=cost(8 * 6 * size * size * width, 16 << 20),
    )(*args)
    return res[0], res[1], res[2 : 2 + n_col], res[2 + n_col :]


def merge_kernel(kept, keep, got, *outs):
    for n, out in enumerate(outs):
        out[...] = (keep[n] + got[n].astype(f32)).astype(out.dtype)


def merge(keep, got, kept):
    n, *piece = keep.shape
    return pl.pallas_call(
        functools.partial(merge_kernel, kept),
        out_shape=[shape(tuple(piece), f32 if k in kept else bf16) for k in range(n)],
        in_specs=[VMEM] * 2,
        out_specs=[VMEM] * n,
        compiler_params=pltpu.CompilerParams(vmem_limit_bytes=SMALL),
        cost_estimate=cost(0, 2 << 20),
    )(keep, got)


def add_kernel(*refs):
    total = refs[0][...]
    for ref in refs[1:-1]:
        total += ref[...].astype(f32)
    refs[-1][...] = total.astype(bf16)


def add(own, parts):
    return pl.pallas_call(
        add_kernel,
        out_shape=shape(own.shape, bf16),
        in_specs=[VMEM] * (1 + len(parts)),
        out_specs=VMEM,
        compiler_params=pltpu.CompilerParams(vmem_limit_bytes=SMALL),
        cost_estimate=cost(0, 1 << 20),
    )(own, *parts)


def update_kernel(n_row, n_col, row_emb, col_emb, *refs):
    row_parts, col_parts, outs = refs[:n_row], refs[n_row : n_row + n_col], refs[n_row + n_col :]
    for n, (emb, parts) in enumerate(((row_emb, row_parts), (col_emb, col_parts))):
        total = parts[0][...].astype(f32)
        for part in parts[1:]:
            total += part[...].astype(f32)
        new = emb[...] - RATE * total
        outs[n][...] = new
        if len(outs) > 2:
            outs[2 + n][...] = new.astype(bf16).reshape(outs[2 + n].shape)


def update(row_emb, col_emb, row_parts, col_parts, last):
    embs = (row_emb, col_emb)
    outs = [shape(e.shape, f32) for e in embs]
    if not last:
        outs += [shape((e.shape[0] * e.shape[1], e.shape[2]), bf16) for e in embs]
    return pl.pallas_call(
        functools.partial(update_kernel, len(row_parts), len(col_parts)),
        out_shape=outs,
        in_specs=[VMEM] * (2 + len(row_parts) + len(col_parts)),
        out_specs=[VMEM] * len(outs),
        compiler_params=pltpu.CompilerParams(vmem_limit_bytes=SMALL),
        cost_estimate=cost(0, 2 << 20),
    )(row_emb, col_emb, *row_parts, *col_parts)


def send(x, axis, count, mask):
    return lax.ppermute(x, axis, [(k, k ^ mask) for k in range(count)])


def shards(n_row_dev, n_col_dev, row_emb, col_emb, row_marg, col_marg, tile_list, tile_count, tile_data):
    listing = tile_list[0, 0].T
    used = tile_count[0]
    tiles = tile_data[0, 0]
    dims = (row_emb.shape[0], col_emb.shape[0], tiles.shape[-1], row_emb.shape[-1])
    half = n_col_dev // 2
    far = half // 2
    near = range(1, far)
    row_owner = [2 * k for k in range(half)] + [2 * k + 1 for k in range(half)]
    col_owner = list(range(n_row_dev))

    def hop(x, distance):
        return send(x, "col", n_col_dev, 2 * distance)

    row_pay, col_pay = pack(row_emb, row_marg, col_emb, col_marg)
    *tabs, tabs_made = levels(used, tiles)
    tables = None
    for substep in range(2):
        crossed = hop(row_pay, far)
        if substep == 0:
            (crossed,) = join([crossed], [tabs_made])
        row_near = [row_pay] + [hop(row_pay, k) for k in near] + [crossed] + [hop(crossed, k) for k in near]
        col_in = [col_pay] + [send(col_pay, "row", n_row_dev, k) for k in col_owner[1:]]
        row_near = join(row_near, col_in[1:])
        row_far = send(row_near, "col", n_col_dev, 1)
        keep, swap, col_out, made = work(
            listing, used, tabs, row_near, row_far, col_in, tables, row_owner, col_owner, dims
        )
        tables = tables or made
        merged = merge(keep, send(swap, "col", n_col_dev, 1), (0, far))
        crossing = add(merged[far], [hop(merged[far + k], k) for k in near])
        col_parts = [col_out[0]] + [send(col_out[k], "row", n_row_dev, k) for k in col_owner[1:]]
        row_parts = [merged[0], hop(crossing, far)] + [hop(merged[k], k) for k in near]
        if substep == 0:
            row_emb, col_emb, row_pay, col_pay = update(row_emb, col_emb, row_parts, col_parts, False)
    return tuple(update(row_emb, col_emb, row_parts, col_parts, True))


def solution(mesh):
    placed = (
        P("row", "col", None),
        P("col", "row", None),
        P("row", "col"),
        P("col", "row"),
        P("row", "col", None, None),
        P("row", "col"),
        P("row", "col", None, None, None),
    )
    return jax.shard_map(
        functools.partial(shards, mesh.shape["row"], mesh.shape["col"]),
        mesh=mesh,
        in_specs=placed,
        out_specs=(P("row", "col", None), P("col", "row", None)),
        check_vma=False,
    )
```

```python
import functools

import jax
import jax.numpy as jnp
from jax import lax
from jax.experimental import pallas as pl
from jax.experimental.pallas import tpu as pltpu
from jax.sharding import PartitionSpec as P

RATE = 0.0004
MARG_ROWS = 16
MARG_LANES = 128
ANY = pl.BlockSpec(memory_space=pl.ANY)
HBM = pl.BlockSpec(memory_space=pltpu.HBM)
VMEM = pl.BlockSpec(memory_space=pltpu.VMEM)
SMEM = pl.BlockSpec(memory_space=pltpu.SMEM)
SMALL = 12 << 20
LARGE = 16 << 20
LEVELS = 31 << 20
PACK = 62 << 20
f32, bf16 = jnp.float32, jnp.bfloat16
shape = jax.ShapeDtypeStruct


def cost(flops, moved):
    return pl.CostEstimate(flops=flops, bytes_accessed=moved, transcendentals=0)


def pack_kernel(row_emb, row_marg, col_emb, col_marg, row_out, col_out, *scratch):
    bufs, sem = scratch[:4], scratch[4]
    copies = [
        pltpu.make_async_copy(src, dst, sem.at[n])
        for n, (src, dst) in enumerate(zip((row_emb, row_marg, col_emb, col_marg), bufs))
    ]
    for copy in copies:
        copy.start()
    for n, out in enumerate((row_out, col_out)):
        copies[2 * n].wait()
        copies[2 * n + 1].wait()
        emb, marg = bufs[2 * n], bufs[2 * n + 1]
        blocks, part, width = emb.shape
        out[: blocks * part, :] = emb[...].astype(bf16).reshape(blocks * part, width)
        out[blocks * part :, :] = jnp.zeros((MARG_ROWS, width), bf16)
        for b in range(blocks):
            out[blocks * part + b : blocks * part + b + 1, :part] = marg[b : b + 1, :]


def pack(row_emb, row_marg, col_emb, col_marg):
    args = (row_emb, row_marg, col_emb, col_marg)
    return pl.pallas_call(
        pack_kernel,
        out_shape=[
            shape((e.shape[0] * e.shape[1] + MARG_ROWS, e.shape[2]), bf16) for e in args[::2]
        ],
        in_specs=[ANY] * 4,
        out_specs=[VMEM] * 2,
        scratch_shapes=[pltpu.VMEM(x.shape, x.dtype) for x in args]
        + [pltpu.SemaphoreType.DMA((4,))],
        compiler_params=pltpu.CompilerParams(vmem_limit_bytes=PACK),
        cost_estimate=cost(0, 1 << 20),
    )(*args)


def levels_kernel(used, tiles, logs, weights, token, tile_buf, sem):
    slots, size, _ = tile_buf.shape
    count = used[0]
    chunk = 64

    def load(slot):
        return pltpu.make_async_copy(tiles.at[slot], tile_buf.at[slot], sem.at[slot])

    for slot in range(slots):

        @pl.when(slot < count)
        def _():
            load(slot).start()

    token[...] = jnp.zeros_like(token)

    def one_tile(slot, carry):
        load(slot).wait()

        def one_chunk(n, carry):
            rows = pl.ds(pl.multiple_of(n * chunk, chunk), chunk)
            counts = tile_buf[slot, rows, :].astype(f32)
            level = jnp.maximum(counts, 1.0)
            logs[slot, rows, :] = jnp.log(level)
            weight = 0.1 + 0.25 * (level * lax.rsqrt(level))
            weights[slot, rows, :] = jnp.where(counts > 0.0, weight, 0.0)
            return carry

        lax.fori_loop(0, size // chunk, one_chunk, 0)
        return carry

    lax.fori_loop(0, count, one_tile, 0)


def levels(used, tiles):
    return pl.pallas_call(
        levels_kernel,
        out_shape=[shape(tiles.shape, f32)] * 2 + [shape((8, 128), f32)],
        in_specs=[SMEM, HBM],
        out_specs=[VMEM] * 3,
        scratch_shapes=[
            pltpu.VMEM(tiles.shape, jnp.int32),
            pltpu.SemaphoreType.DMA((tiles.shape[0],)),
        ],
        compiler_params=pltpu.CompilerParams(vmem_limit_bytes=LEVELS),
        cost_estimate=cost(0, 12 << 20),
    )(used, tiles)


def join_kernel(n_parts, *refs):
    out = refs[-1]
    for n in range(n_parts):
        out[n] = refs[n][...]


def join(parts, afters):
    return pl.pallas_call(
        functools.partial(join_kernel, len(parts)),
        out_shape=shape((len(parts), *parts[0].shape), parts[0].dtype),
        in_specs=[VMEM] * len(parts) + [ANY] * len(afters),
        out_specs=VMEM,
        compiler_params=pltpu.CompilerParams(vmem_limit_bytes=SMALL),
        cost_estimate=cost(0, 1 << 20),
    )(*parts, *afters)


def marg_table(pieces, owners, part, size):
    table = jnp.zeros((MARG_ROWS, size), f32)
    for piece, owner in zip(pieces, owners):
        tail = piece[piece.shape[0] - MARG_ROWS :, :MARG_LANES]
        k = lax.broadcasted_iota(jnp.int32, (MARG_LANES, size), 0)
        at = lax.broadcasted_iota(jnp.int32, (MARG_LANES, size), 1)
        place = ((at == k + owner * part) & (k < part)).astype(bf16)
        table += jnp.dot(tail, place, preferred_element_type=f32)
    return table


def work_kernel(first, n_sides, n_row, n_col, row_owner, col_owner, *refs):
    refs = list(refs)

    def take(n):
        return [refs.pop(0) for _ in range(n)]

    listing, used, logs, weights = take(4)
    sides = take(n_sides)
    col_in = take(n_col)
    if not first:
        left, right = take(2)
    keep, swap = take(2)
    col_out = take(n_col)
    if first:
        left, right = take(2)
    row_panel, col_panel, grad_row, grad_col, even, odd = take(6)

    row_blocks, size, width = row_panel.shape
    col_blocks = col_panel.shape[0]
    row_part, col_part = size // n_row, size // n_col
    half = n_row // 2
    me_row, me_col = lax.axis_index("row"), lax.axis_index("col")
    row_owners = [me_col ^ k for k in row_owner]
    col_owners = [me_row ^ k for k in col_owner]
    row_zero, col_zero = me_row * row_blocks, me_col * col_blocks
    count = used[0]
    row_in = [side.at[n] for side in sides for n in range(side.shape[0])]

    for pieces, owners, panel, part in (
        (row_in, row_owners, row_panel, row_part),
        (col_in, col_owners, col_panel, col_part),
    ):
        for piece, owner in zip(pieces, owners):
            start = pl.multiple_of(owner * part, part)
            for b in range(panel.shape[0]):
                panel[b, pl.ds(start, part), :] = piece[b * part : (b + 1) * part, :]
    grad_row[...] = jnp.zeros_like(grad_row)
    grad_col[...] = jnp.zeros_like(grad_col)

    if first:
        row_table = marg_table(row_in, row_owners, row_part, size).astype(bf16)
        for b in range(row_blocks):
            pick = (lax.broadcasted_iota(jnp.int32, (MARG_ROWS, 128), 0) == b).astype(bf16)
            left[b] = lax.dot_general(
                row_table, pick, (((0,), (0,)), ((), ())), preferred_element_type=f32
            )
        col_table = marg_table(col_in, col_owners, col_part, size)
        for b in range(col_blocks):
            right[b] = jnp.broadcast_to(col_table[b : b + 1, :], right.shape[1:])

    chunks = [slice(at, at + 256) for at in range(0, size, 256)]

    def place(slot):
        return listing[0, slot] - row_zero, listing[1, slot] - col_zero

    def make_signal(slot, rows, signal):
        i, j = place(slot)
        scores = lax.dot_general(
            row_panel[i, rows, :], col_panel[j], (((1,), (1,)), ((), ())), preferred_element_type=f32
        )
        marg_left = jnp.concatenate([left[i, rows, :]] * (size // 128), axis=1)
        diff = scores + marg_left + right[j, 0:1, :] - logs[slot, rows, :]
        weight = weights[slot, rows, :]
        flat = 0.5 * jnp.tanh(0.5 * diff) + 0.5
        signal[rows, :] = jnp.where(weight > 0.0, weight * diff, flat).astype(bf16)

    def add_row(slot, rows, signal):
        i, j = place(slot)
        grad_row[i, rows, :] += jnp.dot(signal[rows, :], col_panel[j], preferred_element_type=f32)

    def add_col(slot, signal):
        i, j = place(slot)
        grad_col[j] += lax.dot_general(
            signal[...], row_panel[i], (((0,), (0,)), ((), ())), preferred_element_type=f32
        )

    def step(slot, before, now):
        for rows in chunks:
            make_signal(slot, rows, now)
            add_row(slot - 1, rows, before)
        add_col(slot - 1, before)

    pairs = (count - 1) // 2

    def pair(n, carry):
        step(2 * n + 1, even, odd)
        step(2 * n + 2, odd, even)
        return carry

    for rows in chunks:
        make_signal(0, rows, even)
    lax.fori_loop(0, pairs, pair, 0)

    @pl.when(2 * pairs + 1 < count)
    def _():
        step(2 * pairs + 1, even, odd)

    for parity, signal in enumerate((even, odd)):

        @pl.when(lax.rem(count - 1, 2) == parity)
        def _():
            for rows in chunks:
                add_row(count - 1, rows, signal)
            add_col(count - 1, signal)

    for n in range(n_row):
        place, sibling = row_owner[n] >> 1, row_owner[n] & 1
        start = pl.multiple_of(row_owners[n] * row_part, row_part)
        piece = grad_row[:, pl.ds(start, row_part), :]
        if sibling:
            swap[place] = piece.astype(bf16)
        else:
            keep[place] = piece
    for n in range(n_col):
        start = pl.multiple_of(col_owners[n] * col_part, col_part)
        col_out[n][...] = grad_col[:, pl.ds(start, col_part), :].astype(bf16)


def work(listing, used, tabs, row_in, col_in, tables, row_owner, col_owner, dims):
    row_blocks, col_blocks, size, width = dims
    first = tables is None
    n_row, n_col = len(row_owner), len(col_owner)
    row_part, col_part = size // n_row, size // n_col
    half = n_row // 2
    outs = [
        shape((half, row_blocks, row_part, width), f32),
        shape((half, row_blocks, row_part, width), bf16),
    ] + [shape((col_blocks, col_part, width), bf16)] * n_col
    if first:
        outs += [shape((row_blocks, size, 128), f32), shape((col_blocks, 8, size), f32)]
    args = [listing, used, *tabs, *row_in, *col_in] + ([] if first else list(tables))
    res = pl.pallas_call(
        functools.partial(work_kernel, first, len(row_in), n_row, n_col, row_owner, col_owner),
        out_shape=outs,
        in_specs=[SMEM, SMEM] + [VMEM] * (len(args) - 2),
        out_specs=[VMEM] * len(outs),
        scratch_shapes=[
            pltpu.VMEM((row_blocks, size, width), bf16),
            pltpu.VMEM((col_blocks, size, width), bf16),
            pltpu.VMEM((row_blocks, size, width), f32),
            pltpu.VMEM((col_blocks, size, width), f32),
            pltpu.VMEM((size, size), bf16),
            pltpu.VMEM((size, size), bf16),
        ],
        compiler_params=pltpu.CompilerParams(vmem_limit_bytes=LARGE),
        cost_estimate=cost(8 * 6 * size * size * width, 16 << 20),
    )(*args)
    return res[0], res[1], res[2 : 2 + n_col], res[2 + n_col :]


def merge_kernel(kept, keep, got, *outs):
    for n, out in enumerate(outs):
        out[...] = (keep[n] + got[n].astype(f32)).astype(out.dtype)


def merge(keep, got, kept):
    n, *piece = keep.shape
    return pl.pallas_call(
        functools.partial(merge_kernel, kept),
        out_shape=[shape(tuple(piece), f32 if k in kept else bf16) for k in range(n)],
        in_specs=[VMEM] * 2,
        out_specs=[VMEM] * n,
        compiler_params=pltpu.CompilerParams(vmem_limit_bytes=SMALL),
        cost_estimate=cost(0, 2 << 20),
    )(keep, got)


def add_kernel(*refs):
    total = refs[0][...]
    for ref in refs[1:-1]:
        total += ref[...].astype(f32)
    refs[-1][...] = total.astype(bf16)


def add(own, parts):
    return pl.pallas_call(
        add_kernel,
        out_shape=shape(own.shape, bf16),
        in_specs=[VMEM] * (1 + len(parts)),
        out_specs=VMEM,
        compiler_params=pltpu.CompilerParams(vmem_limit_bytes=SMALL),
        cost_estimate=cost(0, 1 << 20),
    )(own, *parts)


def update_kernel(n_row, n_col, row_emb, col_emb, *refs):
    row_parts, col_parts, outs = refs[:n_row], refs[n_row : n_row + n_col], refs[n_row + n_col :]
    for n, (emb, parts) in enumerate(((row_emb, row_parts), (col_emb, col_parts))):
        total = parts[0][...].astype(f32)
        for part in parts[1:]:
            total += part[...].astype(f32)
        new = emb[...] - RATE * total
        outs[n][...] = new
        if len(outs) > 2:
            outs[2 + n][...] = new.astype(bf16).reshape(outs[2 + n].shape)


def update(row_emb, col_emb, row_parts, col_parts, last):
    embs = (row_emb, col_emb)
    outs = [shape(e.shape, f32) for e in embs]
    if not last:
        outs += [shape((e.shape[0] * e.shape[1], e.shape[2]), bf16) for e in embs]
    return pl.pallas_call(
        functools.partial(update_kernel, len(row_parts), len(col_parts)),
        out_shape=outs,
        in_specs=[VMEM] * (2 + len(row_parts) + len(col_parts)),
        out_specs=[VMEM] * len(outs),
        compiler_params=pltpu.CompilerParams(vmem_limit_bytes=SMALL),
        cost_estimate=cost(0, 2 << 20),
    )(row_emb, col_emb, *row_parts, *col_parts)


def send(x, axis, count, mask):
    return lax.ppermute(x, axis, [(k, k ^ mask) for k in range(count)])


def shards(n_row_dev, n_col_dev, row_emb, col_emb, row_marg, col_marg, tile_list, tile_count, tile_data):
    listing = tile_list[0, 0].T
    used = tile_count[0]
    tiles = tile_data[0, 0]
    dims = (row_emb.shape[0], col_emb.shape[0], tiles.shape[-1], row_emb.shape[-1])
    half = n_col_dev // 2
    far = half // 2
    near = range(1, far)
    row_owner = [2 * k for k in range(half)] + [2 * k + 1 for k in range(half)]
    col_owner = list(range(n_row_dev))

    def hop(x, distance):
        return send(x, "col", n_col_dev, 2 * distance)

    row_pay, col_pay = pack(row_emb, row_marg, col_emb, col_marg)
    *tabs, tabs_made = levels(used, tiles)
    tables = None
    for substep in range(2):
        crossed = hop(row_pay, far)
        col_in = [col_pay] + [send(col_pay, "row", n_row_dev, k) for k in col_owner[1:]]
        if substep == 0:
            (crossed,) = join([crossed], [tabs_made])
        straight = [row_pay] + [hop(row_pay, k) for k in near] + [crossed]
        relayed = [hop(crossed, k) for k in near]
        if substep == 0:
            row_in = [join(straight + relayed, col_in[1:])]
        else:
            row_in = [join(straight, []), join(relayed, col_in[1:])]
        row_in += [send(pieces, "col", n_col_dev, 1) for pieces in row_in]
        keep, swap, col_out, made = work(
            listing, used, tabs, row_in, col_in, tables, row_owner, col_owner, dims
        )
        tables = tables or made
        merged = merge(keep, send(swap, "col", n_col_dev, 1), (0, far))
        crossing = add(merged[far], [hop(merged[far + k], k) for k in near])
        col_parts = [col_out[0]] + [send(col_out[k], "row", n_row_dev, k) for k in col_owner[1:]]
        row_parts = [merged[0], hop(crossing, far)] + [hop(merged[k], k) for k in near]
        if substep == 0:
            row_emb, col_emb, row_pay, col_pay = update(row_emb, col_emb, row_parts, col_parts, False)
    return tuple(update(row_emb, col_emb, row_parts, col_parts, True))


def solution(mesh):
    placed = (
        P("row", "col", None),
        P("col", "row", None),
        P("row", "col"),
        P("col", "row"),
        P("row", "col", None, None),
        P("row", "col"),
        P("row", "col", None, None, None),
    )
    return jax.shard_map(
        functools.partial(shards, mesh.shape["row"], mesh.shape["col"]),
        mesh=mesh,
        in_specs=placed,
        out_specs=(P("row", "col", None), P("col", "row", None)),
        check_vma=False,
    )
```

```python
import functools

import jax
import jax.numpy as jnp
from jax import lax
from jax.experimental import pallas as pl
from jax.experimental.pallas import tpu as pltpu
from jax.sharding import PartitionSpec as P

RATE = 0.0004
MARG_ROWS = 16
MARG_LANES = 128
ANY = pl.BlockSpec(memory_space=pl.ANY)
HBM = pl.BlockSpec(memory_space=pltpu.HBM)
VMEM = pl.BlockSpec(memory_space=pltpu.VMEM)
SMEM = pl.BlockSpec(memory_space=pltpu.SMEM)
SMALL = 12 << 20
LARGE = 16 << 20
LEVELS = 35 << 20
PACK = 62 << 20
f32, bf16 = jnp.float32, jnp.bfloat16
shape = jax.ShapeDtypeStruct


def cost(flops, moved):
    return pl.CostEstimate(flops=flops, bytes_accessed=moved, transcendentals=0)


def pack_kernel(row_emb, row_marg, col_emb, col_marg, row_out, col_out, *scratch):
    bufs, sem = scratch[:4], scratch[4]
    copies = [
        pltpu.make_async_copy(src, dst, sem.at[n])
        for n, (src, dst) in enumerate(zip((row_emb, row_marg, col_emb, col_marg), bufs))
    ]
    for copy in copies:
        copy.start()
    for n, out in enumerate((row_out, col_out)):
        copies[2 * n].wait()
        copies[2 * n + 1].wait()
        emb, marg = bufs[2 * n], bufs[2 * n + 1]
        blocks, part, width = emb.shape
        out[: blocks * part, :] = emb[...].astype(bf16).reshape(blocks * part, width)
        out[blocks * part :, :] = jnp.zeros((MARG_ROWS, width), bf16)
        for b in range(blocks):
            out[blocks * part + b : blocks * part + b + 1, :part] = marg[b : b + 1, :]


def pack(row_emb, row_marg, col_emb, col_marg):
    args = (row_emb, row_marg, col_emb, col_marg)
    return pl.pallas_call(
        pack_kernel,
        out_shape=[
            shape((e.shape[0] * e.shape[1] + MARG_ROWS, e.shape[2]), bf16) for e in args[::2]
        ],
        in_specs=[ANY] * 4,
        out_specs=[VMEM] * 2,
        scratch_shapes=[pltpu.VMEM(x.shape, x.dtype) for x in args]
        + [pltpu.SemaphoreType.DMA((4,))],
        compiler_params=pltpu.CompilerParams(vmem_limit_bytes=PACK),
        cost_estimate=cost(0, 1 << 20),
    )(*args)


def levels_kernel(used, tiles, logs, weights, token, tile_buf, sem):
    slots, size, _ = tile_buf.shape
    count = used[0]
    chunk = 64

    def load(slot):
        return pltpu.make_async_copy(tiles.at[slot], tile_buf.at[slot], sem.at[slot])

    for slot in range(slots):

        @pl.when(slot < count)
        def _():
            load(slot).start()

    token[...] = jnp.zeros_like(token)

    def one_tile(slot, carry):
        load(slot).wait()

        def one_chunk(n, carry):
            rows = pl.ds(pl.multiple_of(n * chunk, chunk), chunk)
            counts = tile_buf[slot, rows, :].astype(f32)
            level = jnp.maximum(counts, 1.0)
            logs[slot, rows, :] = jnp.log(level)
            weight = 0.1 + 0.25 * (level * lax.rsqrt(level))
            weights[slot, rows, :] = jnp.where(counts > 0.0, weight, 0.0).astype(bf16)
            return carry

        lax.fori_loop(0, size // chunk, one_chunk, 0)
        return carry

    lax.fori_loop(0, count, one_tile, 0)


def levels(used, tiles):
    return pl.pallas_call(
        levels_kernel,
        out_shape=[shape(tiles.shape, f32), shape(tiles.shape, bf16), shape((8, 128), f32)],
        in_specs=[SMEM, HBM],
        out_specs=[VMEM] * 3,
        scratch_shapes=[
            pltpu.VMEM(tiles.shape, jnp.int32),
            pltpu.SemaphoreType.DMA((tiles.shape[0],)),
        ],
        compiler_params=pltpu.CompilerParams(vmem_limit_bytes=LEVELS),
        cost_estimate=cost(0, 12 << 20),
    )(used, tiles)


def join_kernel(n_parts, *refs):
    out = refs[-1]
    for n in range(n_parts):
        out[n] = refs[n][...]


def join(parts, afters):
    return pl.pallas_call(
        functools.partial(join_kernel, len(parts)),
        out_shape=shape((len(parts), *parts[0].shape), parts[0].dtype),
        in_specs=[VMEM] * len(parts) + [ANY] * len(afters),
        out_specs=VMEM,
        compiler_params=pltpu.CompilerParams(vmem_limit_bytes=SMALL),
        cost_estimate=cost(0, 1 << 20),
    )(*parts, *afters)


def marg_table(pieces, owners, part, size):
    table = jnp.zeros((MARG_ROWS, size), f32)
    for piece, owner in zip(pieces, owners):
        tail = piece[piece.shape[0] - MARG_ROWS :, :MARG_LANES]
        k = lax.broadcasted_iota(jnp.int32, (MARG_LANES, size), 0)
        at = lax.broadcasted_iota(jnp.int32, (MARG_LANES, size), 1)
        place = ((at == k + owner * part) & (k < part)).astype(bf16)
        table += jnp.dot(tail, place, preferred_element_type=f32)
    return table


def work_kernel(first, n_sides, n_row, n_col, row_owner, col_owner, *refs):
    refs = list(refs)

    def take(n):
        return [refs.pop(0) for _ in range(n)]

    listing, used, logs, weights = take(4)
    sides = take(n_sides)
    col_in = take(n_col)
    if not first:
        left, right = take(2)
    keep, swap = take(2)
    col_out = take(n_col)
    if first:
        left, right = take(2)
    row_panel, row_turned, col_panel, grad_row, grad_turned, grad_col, even, odd = take(8)

    row_blocks, size, width = row_panel.shape
    col_blocks = col_panel.shape[0]
    row_part, col_part = size // n_row, size // n_col
    half = n_row // 2
    me_row, me_col = lax.axis_index("row"), lax.axis_index("col")
    row_owners = [me_col ^ k for k in row_owner]
    col_owners = [me_row ^ k for k in col_owner]
    row_zero, col_zero = me_row * row_blocks, me_col * col_blocks
    count = used[0]
    row_in = [side.at[n] for side in sides for n in range(side.shape[0])]

    for pieces, owners, panel, part in (
        (row_in, row_owners, row_panel, row_part),
        (col_in, col_owners, col_panel, col_part),
    ):
        for piece, owner in zip(pieces, owners):
            start = pl.multiple_of(owner * part, part)
            for b in range(panel.shape[0]):
                panel[b, pl.ds(start, part), :] = piece[b * part : (b + 1) * part, :]
    for b in range(row_blocks):
        row_turned[b] = row_panel[b].T
    grad_row[...] = jnp.zeros_like(grad_row)
    grad_turned[...] = jnp.zeros_like(grad_turned)

    if first:
        row_table = marg_table(row_in, row_owners, row_part, size).astype(bf16)
        for b in range(row_blocks):
            pick = (lax.broadcasted_iota(jnp.int32, (MARG_ROWS, 128), 0) == b).astype(bf16)
            left[b] = lax.dot_general(
                row_table, pick, (((0,), (0,)), ((), ())), preferred_element_type=f32
            )
        col_table = marg_table(col_in, col_owners, col_part, size)
        for b in range(col_blocks):
            right[b] = jnp.broadcast_to(col_table[b : b + 1, :], right.shape[1:])

    chunks = [slice(at, at + 256) for at in range(0, size, 256)]

    def place(slot):
        return listing[0, slot] - row_zero, listing[1, slot] - col_zero

    def make_signal(slot, rows, signal):
        i, j = place(slot)
        scores = lax.dot_general(
            row_panel[i, rows, :], col_panel[j], (((1,), (1,)), ((), ())), preferred_element_type=f32
        )
        marg_left = jnp.concatenate([left[i, rows, :]] * (size // 128), axis=1)
        diff = (scores + marg_left + right[j, 0:1, :] - logs[slot, rows, :]).astype(bf16)
        weight = weights[slot, rows, :]
        half_one = jnp.asarray(0.5, bf16)
        flat = half_one * jnp.tanh(half_one * diff) + half_one
        signal[rows, :] = jnp.where(weight > 0, weight * diff, flat)

    def add_row(slot, rows, signal):
        i, j = place(slot)
        grad_row[i, rows, :] += jnp.dot(signal[rows, :], col_panel[j], preferred_element_type=f32)

    def add_col(slot, signal):
        i, j = place(slot)
        grad_turned[j] += jnp.dot(row_turned[i], signal[...], preferred_element_type=f32)

    def step(slot, before, now):
        for rows in chunks:
            make_signal(slot, rows, now)
            add_row(slot - 1, rows, before)
        add_col(slot - 1, before)

    pairs = (count - 1) // 2

    def pair(n, carry):
        step(2 * n + 1, even, odd)
        step(2 * n + 2, odd, even)
        return carry

    for rows in chunks:
        make_signal(0, rows, even)
    lax.fori_loop(0, pairs, pair, 0)

    @pl.when(2 * pairs + 1 < count)
    def _():
        step(2 * pairs + 1, even, odd)

    for parity, signal in enumerate((even, odd)):

        @pl.when(lax.rem(count - 1, 2) == parity)
        def _():
            for rows in chunks:
                add_row(count - 1, rows, signal)
            add_col(count - 1, signal)

    for n in range(n_row):
        place, sibling = row_owner[n] >> 1, row_owner[n] & 1
        start = pl.multiple_of(row_owners[n] * row_part, row_part)
        piece = grad_row[:, pl.ds(start, row_part), :]
        if sibling:
            swap[place] = piece.astype(bf16)
        else:
            keep[place] = piece
    for b in range(col_blocks):
        grad_col[b] = grad_turned[b].astype(bf16).T
    for n in range(n_col):
        start = pl.multiple_of(col_owners[n] * col_part, col_part)
        col_out[n][...] = grad_col[:, pl.ds(start, col_part), :]


def work(listing, used, tabs, row_in, col_in, tables, row_owner, col_owner, dims):
    row_blocks, col_blocks, size, width = dims
    first = tables is None
    n_row, n_col = len(row_owner), len(col_owner)
    row_part, col_part = size // n_row, size // n_col
    half = n_row // 2
    outs = [
        shape((half, row_blocks, row_part, width), f32),
        shape((half, row_blocks, row_part, width), bf16),
    ] + [shape((col_blocks, col_part, width), bf16)] * n_col
    if first:
        outs += [shape((row_blocks, size, 128), f32), shape((col_blocks, 8, size), f32)]
    args = [listing, used, *tabs, *row_in, *col_in] + ([] if first else list(tables))
    res = pl.pallas_call(
        functools.partial(work_kernel, first, len(row_in), n_row, n_col, row_owner, col_owner),
        out_shape=outs,
        in_specs=[SMEM, SMEM] + [VMEM] * (len(args) - 2),
        out_specs=[VMEM] * len(outs),
        scratch_shapes=[
            pltpu.VMEM((row_blocks, size, width), bf16),
            pltpu.VMEM((row_blocks, width, size), bf16),
            pltpu.VMEM((col_blocks, size, width), bf16),
            pltpu.VMEM((row_blocks, size, width), f32),
            pltpu.VMEM((col_blocks, width, size), f32),
            pltpu.VMEM((col_blocks, size, width), bf16),
            pltpu.VMEM((size, size), bf16),
            pltpu.VMEM((size, size), bf16),
        ],
        compiler_params=pltpu.CompilerParams(vmem_limit_bytes=LARGE),
        cost_estimate=cost(8 * 6 * size * size * width, 16 << 20),
    )(*args)
    return res[0], res[1], res[2 : 2 + n_col], res[2 + n_col :]


def merge_kernel(kept, keep, got, *outs):
    for n, out in enumerate(outs):
        out[...] = (keep[n] + got[n].astype(f32)).astype(out.dtype)


def merge(keep, got, kept):
    n, *piece = keep.shape
    return pl.pallas_call(
        functools.partial(merge_kernel, kept),
        out_shape=[shape(tuple(piece), f32 if k in kept else bf16) for k in range(n)],
        in_specs=[VMEM] * 2,
        out_specs=[VMEM] * n,
        compiler_params=pltpu.CompilerParams(vmem_limit_bytes=SMALL),
        cost_estimate=cost(0, 2 << 20),
    )(keep, got)


def add_kernel(*refs):
    total = refs[0][...]
    for ref in refs[1:-1]:
        total += ref[...].astype(f32)
    refs[-1][...] = total.astype(bf16)


def add(own, parts):
    return pl.pallas_call(
        add_kernel,
        out_shape=shape(own.shape, bf16),
        in_specs=[VMEM] * (1 + len(parts)),
        out_specs=VMEM,
        compiler_params=pltpu.CompilerParams(vmem_limit_bytes=SMALL),
        cost_estimate=cost(0, 1 << 20),
    )(own, *parts)


def update_kernel(n_parts, emb, *refs):
    parts, outs = refs[:n_parts], refs[n_parts + 1 :]
    total = parts[0][...].astype(f32)
    for part in parts[1:]:
        total += part[...].astype(f32)
    new = emb[...] - RATE * total
    outs[0][...] = new
    if len(outs) > 1:
        outs[1][...] = new.astype(bf16).reshape(outs[1].shape)


def update(emb, parts, after, last):
    blocks, part, width = emb.shape
    outs = [shape(emb.shape, f32)]
    if not last:
        outs.append(shape((blocks * part, width), bf16))
    res = pl.pallas_call(
        functools.partial(update_kernel, len(parts)),
        out_shape=outs,
        in_specs=[VMEM] * (1 + len(parts)) + [ANY],
        out_specs=[VMEM] * len(outs),
        compiler_params=pltpu.CompilerParams(vmem_limit_bytes=SMALL),
        cost_estimate=cost(0, 1 << 20),
    )(emb, *parts, after)
    return res if not last else (res[0], None)


def send(x, axis, count, mask):
    return lax.ppermute(x, axis, [(k, k ^ mask) for k in range(count)])


def shards(n_row_dev, n_col_dev, row_emb, col_emb, row_marg, col_marg, tile_list, tile_count, tile_data):
    listing = tile_list[0, 0].T
    used = tile_count[0]
    tiles = tile_data[0, 0]
    dims = (row_emb.shape[0], col_emb.shape[0], tiles.shape[-1], row_emb.shape[-1])
    half = n_col_dev // 2
    far = half // 2
    near = range(1, far)
    row_owner = [2 * k for k in range(half)] + [2 * k + 1 for k in range(half)]
    col_owner = list(range(n_row_dev))

    def hop(x, distance):
        return send(x, "col", n_col_dev, 2 * distance)

    row_pay, col_pay = pack(row_emb, row_marg, col_emb, col_marg)
    *tabs, tabs_made = levels(used, tiles)
    tables = None
    for substep in range(2):
        crossed = hop(row_pay, far)
        col_in = [col_pay] + [send(col_pay, "row", n_row_dev, k) for k in col_owner[1:]]
        (crossed,) = join([crossed], [tabs_made if substep == 0 else col_in[-1]])
        row_in = [row_pay] + [hop(row_pay, k) for k in near] + [crossed] + [hop(crossed, k) for k in near]
        row_in = [join(row_in, col_in[1:])]
        row_in += [send(pieces, "col", n_col_dev, 1) for pieces in row_in]
        keep, swap, col_out, made = work(
            listing, used, tabs, row_in, col_in, tables, row_owner, col_owner, dims
        )
        tables = tables or made
        merged = merge(keep, send(swap, "col", n_col_dev, 1), (0, far))
        crossing = add(merged[far], [hop(merged[far + k], k) for k in near])
        col_parts = [col_out[0]] + [send(col_out[k], "row", n_row_dev, k) for k in col_owner[1:]]
        row_parts = [merged[0], hop(crossing, far)] + [hop(merged[k], k) for k in near]
        col_emb, col_pay = update(col_emb, col_parts, crossing, substep == 1)
        row_emb, row_pay = update(row_emb, row_parts, col_pay if substep == 0 else crossing, substep == 1)
    return (row_emb, col_emb)


def solution(mesh):
    placed = (
        P("row", "col", None),
        P("col", "row", None),
        P("row", "col"),
        P("col", "row"),
        P("row", "col", None, None),
        P("row", "col"),
        P("row", "col", None, None, None),
    )
    return jax.shard_map(
        functools.partial(shards, mesh.shape["row"], mesh.shape["col"]),
        mesh=mesh,
        in_specs=placed,
        out_specs=(P("row", "col", None), P("col", "row", None)),
        check_vma=False,
    )
```

```python
import functools

import jax
import jax.numpy as jnp
from jax import lax
from jax.experimental import pallas as pl
from jax.experimental.pallas import tpu as pltpu
from jax.sharding import PartitionSpec as P

RATE = 0.0004
MARG_ROWS = 16
MARG_LANES = 128
ANY = pl.BlockSpec(memory_space=pl.ANY)
HBM = pl.BlockSpec(memory_space=pltpu.HBM)
VMEM = pl.BlockSpec(memory_space=pltpu.VMEM)
SMEM = pl.BlockSpec(memory_space=pltpu.SMEM)
SMALL = 12 << 20
LARGE = 16 << 20
LEVELS = 35 << 20
PACK = 62 << 20
f32, bf16 = jnp.float32, jnp.bfloat16
shape = jax.ShapeDtypeStruct


def cost(flops, moved):
    return pl.CostEstimate(flops=flops, bytes_accessed=moved, transcendentals=0)


def pack_kernel(row_emb, row_marg, col_emb, col_marg, row_out, col_out, *scratch):
    bufs, sem = scratch[:4], scratch[4]
    copies = [
        pltpu.make_async_copy(src, dst, sem.at[n])
        for n, (src, dst) in enumerate(zip((row_emb, row_marg, col_emb, col_marg), bufs))
    ]
    for copy in copies:
        copy.start()
    for n, out in enumerate((row_out, col_out)):
        copies[2 * n].wait()
        copies[2 * n + 1].wait()
        emb, marg = bufs[2 * n], bufs[2 * n + 1]
        blocks, part, width = emb.shape
        out[: blocks * part, :] = emb[...].astype(bf16).reshape(blocks * part, width)
        out[blocks * part :, :] = jnp.zeros((MARG_ROWS, width), bf16)
        for b in range(blocks):
            out[blocks * part + b : blocks * part + b + 1, :part] = marg[b : b + 1, :]


def pack(row_emb, row_marg, col_emb, col_marg):
    args = (row_emb, row_marg, col_emb, col_marg)
    return pl.pallas_call(
        pack_kernel,
        out_shape=[
            shape((e.shape[0] * e.shape[1] + MARG_ROWS, e.shape[2]), bf16) for e in args[::2]
        ],
        in_specs=[ANY] * 4,
        out_specs=[VMEM] * 2,
        scratch_shapes=[pltpu.VMEM(x.shape, x.dtype) for x in args]
        + [pltpu.SemaphoreType.DMA((4,))],
        compiler_params=pltpu.CompilerParams(vmem_limit_bytes=PACK),
        cost_estimate=cost(0, 1 << 20),
    )(*args)


def levels_kernel(used, tiles, logs, weights, token, tile_buf, sem):
    slots, size, _ = tile_buf.shape
    count = used[0]
    chunk = 64

    def load(slot):
        return pltpu.make_async_copy(tiles.at[slot], tile_buf.at[slot], sem.at[slot])

    for slot in range(slots):

        @pl.when(slot < count)
        def _():
            load(slot).start()

    token[...] = jnp.zeros_like(token)

    def one_tile(slot, carry):
        load(slot).wait()

        def one_chunk(n, carry):
            rows = pl.ds(pl.multiple_of(n * chunk, chunk), chunk)
            counts = tile_buf[slot, rows, :].astype(f32)
            level = jnp.maximum(counts, 1.0)
            logs[slot, rows, :] = jnp.log(level)
            weight = 0.1 + 0.25 * (level * lax.rsqrt(level))
            weights[slot, rows, :] = jnp.where(counts > 0.0, weight, 0.0).astype(bf16)
            return carry

        lax.fori_loop(0, size // chunk, one_chunk, 0)
        return carry

    lax.fori_loop(0, count, one_tile, 0)


def levels(used, tiles):
    return pl.pallas_call(
        levels_kernel,
        out_shape=[shape(tiles.shape, f32), shape(tiles.shape, bf16), shape((8, 128), f32)],
        in_specs=[SMEM, HBM],
        out_specs=[VMEM] * 3,
        scratch_shapes=[
            pltpu.VMEM(tiles.shape, jnp.int32),
            pltpu.SemaphoreType.DMA((tiles.shape[0],)),
        ],
        compiler_params=pltpu.CompilerParams(vmem_limit_bytes=LEVELS),
        cost_estimate=cost(0, 12 << 20),
    )(used, tiles)


def join_kernel(sizes, *refs):
    parts, outs = list(refs[: sum(sizes)]), refs[-len(sizes) :]
    for out in outs:
        for n in range(out.shape[0]):
            part = parts.pop(0)
            out[n] = part[0] if len(part.shape) == 3 else part[...]


def join(parts, sizes, afters):
    piece = parts[0].shape[-2:]
    return list(
        pl.pallas_call(
            functools.partial(join_kernel, sizes),
            out_shape=[shape((size, *piece), bf16) for size in sizes],
            in_specs=[VMEM] * len(parts) + [ANY] * len(afters),
            out_specs=[VMEM] * len(sizes),
            compiler_params=pltpu.CompilerParams(vmem_limit_bytes=SMALL),
            cost_estimate=cost(0, 1 << 20),
        )(*parts, *afters)
    )


def marg_table(pieces, owners, part, size):
    table = jnp.zeros((MARG_ROWS, size), f32)
    for piece, owner in zip(pieces, owners):
        tail = piece[piece.shape[0] - MARG_ROWS :, :MARG_LANES]
        k = lax.broadcasted_iota(jnp.int32, (MARG_LANES, size), 0)
        at = lax.broadcasted_iota(jnp.int32, (MARG_LANES, size), 1)
        place = ((at == k + owner * part) & (k < part)).astype(bf16)
        table += jnp.dot(tail, place, preferred_element_type=f32)
    return table


def work_kernel(first, n_sides, n_row, n_col, row_owner, col_owner, *refs):
    refs = list(refs)

    def take(n):
        return [refs.pop(0) for _ in range(n)]

    listing, used, logs, weights = take(4)
    sides, col_in = take(n_sides), take(n_col)
    row_in = [side.at[n] for side in sides for n in range(side.shape[0])]
    if not first:
        left, right = take(2)
    keep, swap = take(2)
    col_out = take(n_col)
    if first:
        left, right = take(2)
    row_panel, row_turned, col_panel, grad_row, grad_turned, grad_col, even, odd = take(8)

    row_blocks, size, width = row_panel.shape
    col_blocks = col_panel.shape[0]
    row_part, col_part = size // n_row, size // n_col
    half = n_row // 2
    me_row, me_col = lax.axis_index("row"), lax.axis_index("col")
    row_owners = [me_col ^ k for k in row_owner]
    col_owners = [me_row ^ k for k in col_owner]
    row_zero, col_zero = me_row * row_blocks, me_col * col_blocks
    count = used[0]

    for pieces, owners, panel, part in (
        (row_in, row_owners, row_panel, row_part),
        (col_in, col_owners, col_panel, col_part),
    ):
        for piece, owner in zip(pieces, owners):
            start = pl.multiple_of(owner * part, part)
            for b in range(panel.shape[0]):
                panel[b, pl.ds(start, part), :] = piece[b * part : (b + 1) * part, :]
    for b in range(row_blocks):
        row_turned[b] = row_panel[b].T
    grad_row[...] = jnp.zeros_like(grad_row)
    grad_turned[...] = jnp.zeros_like(grad_turned)

    if first:
        row_table = marg_table(row_in, row_owners, row_part, size).astype(bf16)
        for b in range(row_blocks):
            pick = (lax.broadcasted_iota(jnp.int32, (MARG_ROWS, 128), 0) == b).astype(bf16)
            left[b] = lax.dot_general(
                row_table, pick, (((0,), (0,)), ((), ())), preferred_element_type=f32
            )
        col_table = marg_table(col_in, col_owners, col_part, size)
        for b in range(col_blocks):
            right[b] = jnp.broadcast_to(col_table[b : b + 1, :], right.shape[1:])

    chunks = [slice(at, at + 256) for at in range(0, size, 256)]

    def place(slot):
        return listing[0, slot] - row_zero, listing[1, slot] - col_zero

    def make_signal(slot, rows, signal):
        i, j = place(slot)
        scores = lax.dot_general(
            row_panel[i, rows, :], col_panel[j], (((1,), (1,)), ((), ())), preferred_element_type=f32
        )
        marg_left = jnp.concatenate([left[i, rows, :]] * (size // 128), axis=1)
        diff = (scores + marg_left + right[j, 0:1, :] - logs[slot, rows, :]).astype(bf16)
        weight = weights[slot, rows, :]
        half_one = jnp.asarray(0.5, bf16)
        flat = half_one * jnp.tanh(half_one * diff) + half_one
        signal[rows, :] = jnp.where(weight > 0, weight * diff, flat)

    def add_row(slot, rows, signal):
        i, j = place(slot)
        grad_row[i, rows, :] += jnp.dot(signal[rows, :], col_panel[j], preferred_element_type=f32)

    def add_col(slot, signal):
        i, j = place(slot)
        grad_turned[j] += jnp.dot(row_turned[i], signal[...], preferred_element_type=f32)

    def step(slot, before, now):
        for rows in chunks:
            make_signal(slot, rows, now)
            add_row(slot - 1, rows, before)
        add_col(slot - 1, before)

    pairs = (count - 1) // 2

    def pair(n, carry):
        step(2 * n + 1, even, odd)
        step(2 * n + 2, odd, even)
        return carry

    for rows in chunks:
        make_signal(0, rows, even)
    lax.fori_loop(0, pairs, pair, 0)

    @pl.when(2 * pairs + 1 < count)
    def _():
        step(2 * pairs + 1, even, odd)

    for parity, signal in enumerate((even, odd)):

        @pl.when(lax.rem(count - 1, 2) == parity)
        def _():
            for rows in chunks:
                add_row(count - 1, rows, signal)
            add_col(count - 1, signal)

    for n in range(n_row):
        place, sibling = row_owner[n] >> 1, row_owner[n] & 1
        start = pl.multiple_of(row_owners[n] * row_part, row_part)
        piece = grad_row[:, pl.ds(start, row_part), :]
        if sibling:
            swap[place] = piece.astype(bf16)
        else:
            keep[place] = piece
    for b in range(col_blocks):
        grad_col[b] = grad_turned[b].astype(bf16).T
    for n in range(n_col):
        start = pl.multiple_of(col_owners[n] * col_part, col_part)
        col_out[n][...] = grad_col[:, pl.ds(start, col_part), :]


def work(listing, used, tabs, row_in, col_in, tables, row_owner, col_owner, dims):
    row_blocks, col_blocks, size, width = dims
    first = tables is None
    n_row, n_col = len(row_owner), len(col_owner)
    row_part, col_part = size // n_row, size // n_col
    half = n_row // 2
    outs = [
        shape((half, row_blocks, row_part, width), f32),
        shape((half, row_blocks, row_part, width), bf16),
    ] + [shape((col_blocks, col_part, width), bf16)] * n_col
    if first:
        outs += [shape((row_blocks, size, 128), f32), shape((col_blocks, 8, size), f32)]
    args = [listing, used, *tabs, *row_in, *col_in] + ([] if first else list(tables))
    res = pl.pallas_call(
        functools.partial(work_kernel, first, len(row_in), n_row, n_col, row_owner, col_owner),
        out_shape=outs,
        in_specs=[SMEM, SMEM] + [VMEM] * (len(args) - 2),
        out_specs=[VMEM] * len(outs),
        scratch_shapes=[
            pltpu.VMEM((row_blocks, size, width), bf16),
            pltpu.VMEM((row_blocks, width, size), bf16),
            pltpu.VMEM((col_blocks, size, width), bf16),
            pltpu.VMEM((row_blocks, size, width), f32),
            pltpu.VMEM((col_blocks, width, size), f32),
            pltpu.VMEM((col_blocks, size, width), bf16),
            pltpu.VMEM((size, size), bf16),
            pltpu.VMEM((size, size), bf16),
        ],
        compiler_params=pltpu.CompilerParams(vmem_limit_bytes=LARGE),
        cost_estimate=cost(8 * 6 * size * size * width, 16 << 20),
    )(*args)
    return res[0], res[1], res[2 : 2 + n_col], res[2 + n_col :]


def merge_kernel(kept, keep, got, *outs):
    for n, out in enumerate(outs):
        out[...] = (keep[n] + got[n].astype(f32)).astype(out.dtype)


def merge(keep, got, kept):
    n, *piece = keep.shape
    return pl.pallas_call(
        functools.partial(merge_kernel, kept),
        out_shape=[shape(tuple(piece), f32 if k in kept else bf16) for k in range(n)],
        in_specs=[VMEM] * 2,
        out_specs=[VMEM] * n,
        compiler_params=pltpu.CompilerParams(vmem_limit_bytes=SMALL),
        cost_estimate=cost(0, 2 << 20),
    )(keep, got)


def add_kernel(*refs):
    total = refs[0][...]
    for ref in refs[1:-1]:
        total += ref[...].astype(f32)
    refs[-1][...] = total.astype(bf16)


def add(own, parts):
    return pl.pallas_call(
        add_kernel,
        out_shape=shape(own.shape, bf16),
        in_specs=[VMEM] * (1 + len(parts)),
        out_specs=VMEM,
        compiler_params=pltpu.CompilerParams(vmem_limit_bytes=SMALL),
        cost_estimate=cost(0, 1 << 20),
    )(own, *parts)


def update_kernel(n_parts, emb, *refs):
    parts, outs = refs[:n_parts], refs[n_parts + 1 :]
    total = parts[0][...].astype(f32)
    for part in parts[1:]:
        total += part[...].astype(f32)
    new = emb[...] - RATE * total
    outs[0][...] = new
    if len(outs) > 1:
        outs[1][...] = new.astype(bf16).reshape(outs[1].shape)


def update(emb, parts, after, last):
    blocks, part, width = emb.shape
    outs = [shape(emb.shape, f32)]
    if not last:
        outs.append(shape((blocks * part, width), bf16))
    res = pl.pallas_call(
        functools.partial(update_kernel, len(parts)),
        out_shape=outs,
        in_specs=[VMEM] * (1 + len(parts)) + [ANY],
        out_specs=[VMEM] * len(outs),
        compiler_params=pltpu.CompilerParams(vmem_limit_bytes=SMALL),
        cost_estimate=cost(0, 1 << 20),
    )(emb, *parts, after)
    return res if not last else (res[0], None)


def send(x, axis, count, mask):
    return lax.ppermute(x, axis, [(k, k ^ mask) for k in range(count)])


def shards(n_row_dev, n_col_dev, row_emb, col_emb, row_marg, col_marg, tile_list, tile_count, tile_data):
    listing = tile_list[0, 0].T
    used = tile_count[0]
    tiles = tile_data[0, 0]
    dims = (row_emb.shape[0], col_emb.shape[0], tiles.shape[-1], row_emb.shape[-1])
    half = n_col_dev // 2
    far = half // 2
    near = range(1, far)
    row_owner = [2 * k for k in range(half)] + [2 * k + 1 for k in range(half)]
    col_owner = list(range(n_row_dev))

    def hop(x, distance):
        return send(x, "col", n_col_dev, 2 * distance)

    row_pay, col_pay = pack(row_emb, row_marg, col_emb, col_marg)
    *tabs, tabs_made = levels(used, tiles)
    tables = None
    for substep in range(2):
        crossed = hop(row_pay, far)
        col_in = [col_pay] + [send(col_pay, "row", n_row_dev, k) for k in col_owner[1:]]
        if substep == 0:
            before_leg, before_swap, sizes = [tabs_made], col_in[1:-1], [1, far - 1, 1, far - 1]
        else:
            before_leg, before_swap, sizes = col_in[-1:], [], [far, 1, far - 1]
        (crossed,) = join([crossed], [1], before_leg)
        row_in = [row_pay] + [hop(row_pay, k) for k in near] + [crossed] + [hop(crossed, k) for k in near]
        row_in = join(row_in, sizes, before_swap)
        row_in += [send(piece, "col", n_col_dev, 1) for piece in row_in]
        keep, swap, col_out, made = work(
            listing, used, tabs, row_in, col_in, tables, row_owner, col_owner, dims
        )
        tables = tables or made
        merged = merge(keep, send(swap, "col", n_col_dev, 1), (0, far))
        crossing = add(merged[far], [hop(merged[far + k], k) for k in near])
        col_parts = [col_out[0]] + [send(col_out[k], "row", n_row_dev, k) for k in col_owner[1:]]
        row_parts = [merged[0], hop(crossing, far)] + [hop(merged[k], k) for k in near]
        col_emb, col_pay = update(col_emb, col_parts, crossing, substep == 1)
        row_emb, row_pay = update(row_emb, row_parts, col_pay if substep == 0 else crossing, substep == 1)
    return (row_emb, col_emb)


def solution(mesh):
    placed = (
        P("row", "col", None),
        P("col", "row", None),
        P("row", "col"),
        P("col", "row"),
        P("row", "col", None, None),
        P("row", "col"),
        P("row", "col", None, None, None),
    )
    return jax.shard_map(
        functools.partial(shards, mesh.shape["row"], mesh.shape["col"]),
        mesh=mesh,
        in_specs=placed,
        out_specs=(P("row", "col", None), P("col", "row", None)),
        check_vma=False,
    )
```

```python
import functools

import jax
import jax.numpy as jnp
from jax import lax
from jax.experimental import pallas as pl
from jax.experimental.pallas import tpu as pltpu
from jax.sharding import PartitionSpec as P

RATE = 0.0004
MARG_ROWS = 16
MARG_LANES = 128
ANY = pl.BlockSpec(memory_space=pl.ANY)
HBM = pl.BlockSpec(memory_space=pltpu.HBM)
VMEM = pl.BlockSpec(memory_space=pltpu.VMEM)
SMEM = pl.BlockSpec(memory_space=pltpu.SMEM)
SMALL = 12 << 20
LARGE = 16 << 20
LEVELS = 35 << 20
PACK = 62 << 20
f32, bf16 = jnp.float32, jnp.bfloat16
shape = jax.ShapeDtypeStruct


def cost(flops, moved):
    return pl.CostEstimate(flops=flops, bytes_accessed=moved, transcendentals=0)


def pack_kernel(row_emb, row_marg, col_emb, col_marg, row_out, col_out, *scratch):
    bufs, sem = scratch[:4], scratch[4]
    copies = [
        pltpu.make_async_copy(src, dst, sem.at[n])
        for n, (src, dst) in enumerate(zip((row_emb, row_marg, col_emb, col_marg), bufs))
    ]
    for copy in copies:
        copy.start()
    for n, out in enumerate((row_out, col_out)):
        copies[2 * n].wait()
        copies[2 * n + 1].wait()
        emb, marg = bufs[2 * n], bufs[2 * n + 1]
        blocks, part, width = emb.shape
        out[: blocks * part, :] = emb[...].astype(bf16).reshape(blocks * part, width)
        out[blocks * part :, :] = jnp.zeros((MARG_ROWS, width), bf16)
        for b in range(blocks):
            out[blocks * part + b : blocks * part + b + 1, :part] = marg[b : b + 1, :]


def pack(row_emb, row_marg, col_emb, col_marg):
    args = (row_emb, row_marg, col_emb, col_marg)
    return pl.pallas_call(
        pack_kernel,
        out_shape=[
            shape((e.shape[0] * e.shape[1] + MARG_ROWS, e.shape[2]), bf16) for e in args[::2]
        ],
        in_specs=[ANY] * 4,
        out_specs=[VMEM] * 2,
        scratch_shapes=[pltpu.VMEM(x.shape, x.dtype) for x in args]
        + [pltpu.SemaphoreType.DMA((4,))],
        compiler_params=pltpu.CompilerParams(vmem_limit_bytes=PACK),
        cost_estimate=cost(0, 1 << 20),
    )(*args)


def levels_kernel(used, tiles, logs, weights, token, tile_buf, sem):
    slots, size, _ = tile_buf.shape
    count = used[0]
    chunk = 64

    def load(slot):
        return pltpu.make_async_copy(tiles.at[slot], tile_buf.at[slot], sem.at[slot])

    for slot in range(slots):

        @pl.when(slot < count)
        def _():
            load(slot).start()

    token[...] = jnp.zeros_like(token)

    def one_tile(slot, carry):
        load(slot).wait()

        def one_chunk(n, carry):
            rows = pl.ds(pl.multiple_of(n * chunk, chunk), chunk)
            counts = tile_buf[slot, rows, :].astype(f32)
            level = jnp.maximum(counts, 1.0)
            logs[slot, rows, :] = jnp.log(level)
            weight = 0.1 + 0.25 * (level * lax.rsqrt(level))
            weights[slot, rows, :] = jnp.where(counts > 0.0, weight, 0.0).astype(bf16)
            return carry

        lax.fori_loop(0, size // chunk, one_chunk, 0)
        return carry

    lax.fori_loop(0, count, one_tile, 0)


def levels(used, tiles):
    return pl.pallas_call(
        levels_kernel,
        out_shape=[shape(tiles.shape, f32), shape(tiles.shape, bf16), shape((8, 128), f32)],
        in_specs=[SMEM, HBM],
        out_specs=[VMEM] * 3,
        scratch_shapes=[
            pltpu.VMEM(tiles.shape, jnp.int32),
            pltpu.SemaphoreType.DMA((tiles.shape[0],)),
        ],
        compiler_params=pltpu.CompilerParams(vmem_limit_bytes=LEVELS),
        cost_estimate=cost(0, 12 << 20),
    )(used, tiles)


def join_kernel(sizes, *refs):
    parts, outs = list(refs[: sum(sizes)]), refs[-len(sizes) :]
    for out in outs:
        for n in range(out.shape[0]):
            part = parts.pop(0)
            out[n] = part[0] if len(part.shape) == 3 else part[...]


def join(parts, sizes, afters):
    piece = parts[0].shape[-2:]
    return list(
        pl.pallas_call(
            functools.partial(join_kernel, sizes),
            out_shape=[shape((size, *piece), bf16) for size in sizes],
            in_specs=[VMEM] * len(parts) + [ANY] * len(afters),
            out_specs=[VMEM] * len(sizes),
            compiler_params=pltpu.CompilerParams(vmem_limit_bytes=SMALL),
            cost_estimate=cost(0, 1 << 20),
        )(*parts, *afters)
    )


def marg_table(pieces, owners, part, size):
    table = jnp.zeros((MARG_ROWS, size), f32)
    for piece, owner in zip(pieces, owners):
        tail = piece[piece.shape[0] - MARG_ROWS :, :MARG_LANES]
        k = lax.broadcasted_iota(jnp.int32, (MARG_LANES, size), 0)
        at = lax.broadcasted_iota(jnp.int32, (MARG_LANES, size), 1)
        place = ((at == k + owner * part) & (k < part)).astype(bf16)
        table += jnp.dot(tail, place, preferred_element_type=f32)
    return table


def work_kernel(first, n_sides, n_row, n_col, row_owner, col_owner, *refs):
    refs = list(refs)

    def take(n):
        return [refs.pop(0) for _ in range(n)]

    listing, used, logs, weights = take(4)
    sides, col_in = take(n_sides), take(n_col)
    row_in = [side.at[n] for side in sides for n in range(side.shape[0])]
    if not first:
        left, right = take(2)
    keep, swap = take(2)
    col_out = take(n_col)
    if first:
        left, right = take(2)
    row_panel, row_turned, col_panel, grad_row, grad_turned, grad_col, even, odd = take(8)

    row_blocks, size, width = row_panel.shape
    col_blocks = col_panel.shape[0]
    row_part, col_part = size // n_row, size // n_col
    half = n_row // 2
    me_row, me_col = lax.axis_index("row"), lax.axis_index("col")
    row_owners = [me_col ^ k for k in row_owner]
    col_owners = [me_row ^ k for k in col_owner]
    row_zero, col_zero = me_row * row_blocks, me_col * col_blocks
    count = used[0]

    for pieces, owners, panel, part in (
        (row_in, row_owners, row_panel, row_part),
        (col_in, col_owners, col_panel, col_part),
    ):
        for piece, owner in zip(pieces, owners):
            start = pl.multiple_of(owner * part, part)
            for b in range(panel.shape[0]):
                panel[b, pl.ds(start, part), :] = piece[b * part : (b + 1) * part, :]
    for b in range(row_blocks):
        row_turned[b] = row_panel[b].T
    grad_row[...] = jnp.zeros_like(grad_row)
    grad_turned[...] = jnp.zeros_like(grad_turned)

    if first:
        row_table = marg_table(row_in, row_owners, row_part, size).astype(bf16)
        for b in range(row_blocks):
            pick = (lax.broadcasted_iota(jnp.int32, (MARG_ROWS, 128), 0) == b).astype(bf16)
            left[b] = lax.dot_general(
                row_table, pick, (((0,), (0,)), ((), ())), preferred_element_type=f32
            )
        col_table = marg_table(col_in, col_owners, col_part, size)
        for b in range(col_blocks):
            right[b] = jnp.broadcast_to(col_table[b : b + 1, :], right.shape[1:])

    chunks = [slice(at, at + 256) for at in range(0, size, 256)]

    def place(slot):
        return listing[0, slot] - row_zero, listing[1, slot] - col_zero

    def make_signal(slot, rows, signal):
        i, j = place(slot)
        scores = lax.dot_general(
            row_panel[i, rows, :], col_panel[j], (((1,), (1,)), ((), ())), preferred_element_type=f32
        )
        marg_left = jnp.concatenate([left[i, rows, :]] * (size // 128), axis=1)
        diff = (scores + marg_left + right[j, 0:1, :] - logs[slot, rows, :]).astype(bf16)
        weight = weights[slot, rows, :]
        half_one = jnp.asarray(0.5, bf16)
        flat = half_one * jnp.tanh(half_one * diff) + half_one
        signal[rows, :] = jnp.where(weight > 0, weight * diff, flat)

    def add_row(slot, rows, signal):
        i, j = place(slot)
        grad_row[i, rows, :] += jnp.dot(signal[rows, :], col_panel[j], preferred_element_type=f32)

    def add_col(slot, signal):
        i, j = place(slot)
        grad_turned[j] += jnp.dot(row_turned[i], signal[...], preferred_element_type=f32)

    def step(slot, before, now):
        for rows in chunks:
            make_signal(slot, rows, now)
            add_row(slot - 1, rows, before)
        add_col(slot - 1, before)

    pairs = (count - 1) // 2

    def pair(n, carry):
        step(2 * n + 1, even, odd)
        step(2 * n + 2, odd, even)
        return carry

    for rows in chunks:
        make_signal(0, rows, even)
    lax.fori_loop(0, pairs, pair, 0)

    @pl.when(2 * pairs + 1 < count)
    def _():
        step(2 * pairs + 1, even, odd)

    for parity, signal in enumerate((even, odd)):

        @pl.when(lax.rem(count - 1, 2) == parity)
        def _():
            for rows in chunks:
                add_row(count - 1, rows, signal)
            add_col(count - 1, signal)

    for n in range(n_row):
        place, sibling = row_owner[n] >> 1, row_owner[n] & 1
        start = pl.multiple_of(row_owners[n] * row_part, row_part)
        piece = grad_row[:, pl.ds(start, row_part), :]
        if sibling:
            swap[place] = piece.astype(bf16)
        else:
            keep[place] = piece
    for b in range(col_blocks):
        grad_col[b] = grad_turned[b].astype(bf16).T
    for n in range(n_col):
        start = pl.multiple_of(col_owners[n] * col_part, col_part)
        col_out[n][...] = grad_col[:, pl.ds(start, col_part), :]


def work(listing, used, tabs, row_in, col_in, tables, row_owner, col_owner, dims):
    row_blocks, col_blocks, size, width = dims
    first = tables is None
    n_row, n_col = len(row_owner), len(col_owner)
    row_part, col_part = size // n_row, size // n_col
    half = n_row // 2
    outs = [
        shape((half, row_blocks, row_part, width), f32),
        shape((half, row_blocks, row_part, width), bf16),
    ] + [shape((col_blocks, col_part, width), bf16)] * n_col
    if first:
        outs += [shape((row_blocks, size, 128), f32), shape((col_blocks, 8, size), f32)]
    args = [listing, used, *tabs, *row_in, *col_in] + ([] if first else list(tables))
    res = pl.pallas_call(
        functools.partial(work_kernel, first, len(row_in), n_row, n_col, row_owner, col_owner),
        out_shape=outs,
        in_specs=[SMEM, SMEM] + [VMEM] * (len(args) - 2),
        out_specs=[VMEM] * len(outs),
        scratch_shapes=[
            pltpu.VMEM((row_blocks, size, width), bf16),
            pltpu.VMEM((row_blocks, width, size), bf16),
            pltpu.VMEM((col_blocks, size, width), bf16),
            pltpu.VMEM((row_blocks, size, width), f32),
            pltpu.VMEM((col_blocks, width, size), f32),
            pltpu.VMEM((col_blocks, size, width), bf16),
            pltpu.VMEM((size, size), bf16),
            pltpu.VMEM((size, size), bf16),
        ],
        compiler_params=pltpu.CompilerParams(vmem_limit_bytes=LARGE),
        cost_estimate=cost(8 * 6 * size * size * width, 16 << 20),
    )(*args)
    return res[0], res[1], res[2 : 2 + n_col], res[2 + n_col :]


def merge_kernel(n_held, keep, got, *refs):
    held, outs = refs[:n_held], refs[n_held:]
    for n in range(keep.shape[0]):
        outs[n][...] = (keep[n] + got[n].astype(f32)).astype(outs[n].dtype)
    for src, out in zip(held, outs[keep.shape[0] :]):
        out[...] = src[...]


def merge(keep, got, kept, held):
    n, *piece = keep.shape
    outs = [shape(tuple(piece), f32 if k in kept else bf16) for k in range(n)]
    outs += [shape(x.shape, x.dtype) for x in held]
    return pl.pallas_call(
        functools.partial(merge_kernel, len(held)),
        out_shape=outs,
        in_specs=[VMEM] * (2 + len(held)),
        out_specs=[VMEM] * len(outs),
        compiler_params=pltpu.CompilerParams(vmem_limit_bytes=SMALL),
        cost_estimate=cost(0, 2 << 20),
    )(keep, got, *held)


def add_kernel(n_parts, n_held, own, *refs):
    parts, held, outs = refs[:n_parts], refs[n_parts : n_parts + n_held], refs[n_parts + n_held :]
    total = own[...]
    for part in parts:
        total += part[...].astype(f32)
    outs[0][...] = total.astype(bf16)
    for src, out in zip(held, outs[1:]):
        out[...] = src[...]


def add(own, parts, held):
    return pl.pallas_call(
        functools.partial(add_kernel, len(parts), len(held)),
        out_shape=[shape(own.shape, bf16)] + [shape(x.shape, x.dtype) for x in held],
        in_specs=[VMEM] * (1 + len(parts) + len(held)),
        out_specs=[VMEM] * (1 + len(held)),
        compiler_params=pltpu.CompilerParams(vmem_limit_bytes=SMALL),
        cost_estimate=cost(0, 1 << 20),
    )(own, *parts, *held)


def update_kernel(n_parts, n_outs, emb, *refs):
    parts, outs = refs[:n_parts], refs[-n_outs:]
    total = parts[0][...].astype(f32)
    for part in parts[1:]:
        total += part[...].astype(f32)
    new = emb[...] - RATE * total
    outs[0][...] = new
    if len(outs) > 1:
        outs[1][...] = new.astype(bf16).reshape(outs[1].shape)


def update(emb, parts, afters, last):
    blocks, part, width = emb.shape
    outs = [shape(emb.shape, f32)]
    if not last:
        outs.append(shape((blocks * part, width), bf16))
    res = pl.pallas_call(
        functools.partial(update_kernel, len(parts), len(outs)),
        out_shape=outs,
        in_specs=[VMEM] * (1 + len(parts)) + [ANY] * len(afters),
        out_specs=[VMEM] * len(outs),
        compiler_params=pltpu.CompilerParams(vmem_limit_bytes=SMALL),
        cost_estimate=cost(0, 1 << 20),
    )(emb, *parts, *afters)
    return res if not last else (res[0], None)


def send(x, axis, count, mask):
    return lax.ppermute(x, axis, [(k, k ^ mask) for k in range(count)])


def shards(n_row_dev, n_col_dev, row_emb, col_emb, row_marg, col_marg, tile_list, tile_count, tile_data):
    listing = tile_list[0, 0].T
    used = tile_count[0]
    tiles = tile_data[0, 0]
    dims = (row_emb.shape[0], col_emb.shape[0], tiles.shape[-1], row_emb.shape[-1])
    half = n_col_dev // 2
    far = half // 2
    near = range(1, far)
    row_owner = [2 * k for k in range(half)] + [2 * k + 1 for k in range(half)]
    col_owner = list(range(n_row_dev))

    def hop(x, distance):
        return send(x, "col", n_col_dev, 2 * distance)

    row_pay, col_pay = pack(row_emb, row_marg, col_emb, col_marg)
    *tabs, tabs_made = levels(used, tiles)
    tables = None
    for substep in range(2):
        crossed = hop(row_pay, far)
        col_in = [col_pay] + [send(col_pay, "row", n_row_dev, k) for k in col_owner[1:]]
        if substep == 0:
            before_leg, before_swap, sizes = [tabs_made], col_in[1:-1], [1, far - 1, 1, far - 1]
        else:
            before_leg, before_swap, sizes = col_in[-1:], [], [far, 1, far - 1]
        (crossed,) = join([crossed], [1], before_leg)
        row_in = [row_pay] + [hop(row_pay, k) for k in near] + [crossed] + [hop(crossed, k) for k in near]
        row_in = join(row_in, sizes, before_swap)
        row_in += [send(piece, "col", n_col_dev, 1) for piece in row_in]
        keep, swap, col_out, made = work(
            listing, used, tabs, row_in, col_in, tables, row_owner, col_owner, dims
        )
        tables = tables or made
        held = col_out[-1:] if substep == 1 else []
        merged = merge(keep, send(swap, "col", n_col_dev, 1), (0, far), held)
        col_out = [*col_out[: len(col_out) - len(held)], *merged[half:]]
        relays = [hop(merged[far + k], k) for k in near]
        crossing, *straight = add(merged[far], relays, [merged[k] for k in near])
        col_parts = [col_out[0]] + [send(col_out[k], "row", n_row_dev, k) for k in col_owner[1:]]
        row_parts = [merged[0]] + [hop(x, k) for x, k in zip(straight, near)] + [hop(crossing, far)]
        col_emb, col_pay = update(col_emb, col_parts, [straight[0]], substep == 1)
        row_emb, row_pay = update(row_emb, row_parts, [col_pay if substep == 0 else straight[0]], substep == 1)
    return (row_emb, col_emb)


def solution(mesh):
    placed = (
        P("row", "col", None),
        P("col", "row", None),
        P("row", "col"),
        P("col", "row"),
        P("row", "col", None, None),
        P("row", "col"),
        P("row", "col", None, None, None),
    )
    return jax.shard_map(
        functools.partial(shards, mesh.shape["row"], mesh.shape["col"]),
        mesh=mesh,
        in_specs=placed,
        out_specs=(P("row", "col", None), P("col", "row", None)),
        check_vma=False,
    )
```

```python
import functools

import jax
import jax.numpy as jnp
from jax import lax
from jax.experimental import pallas as pl
from jax.experimental.pallas import tpu as pltpu
from jax.sharding import PartitionSpec as P

RATE = 0.0004
MARG_ROWS = 16
MARG_LANES = 128
ANY = pl.BlockSpec(memory_space=pl.ANY)
HBM = pl.BlockSpec(memory_space=pltpu.HBM)
VMEM = pl.BlockSpec(memory_space=pltpu.VMEM)
SMEM = pl.BlockSpec(memory_space=pltpu.SMEM)
SMALL = 12 << 20
LARGE = 16 << 20
LEVELS = 35 << 20
PACK = 62 << 20
f32, bf16 = jnp.float32, jnp.bfloat16
shape = jax.ShapeDtypeStruct


def cost(flops, moved):
    return pl.CostEstimate(flops=flops, bytes_accessed=moved, transcendentals=0)


def pack_kernel(row_emb, row_marg, col_emb, col_marg, row_out, col_out, *scratch):
    bufs, sem = scratch[:4], scratch[4]
    copies = [
        pltpu.make_async_copy(src, dst, sem.at[n])
        for n, (src, dst) in enumerate(zip((row_emb, row_marg, col_emb, col_marg), bufs))
    ]
    for copy in copies:
        copy.start()
    for n, out in enumerate((row_out, col_out)):
        copies[2 * n].wait()
        copies[2 * n + 1].wait()
        emb, marg = bufs[2 * n], bufs[2 * n + 1]
        blocks, part, width = emb.shape
        out[: blocks * part, :] = emb[...].astype(bf16).reshape(blocks * part, width)
        out[blocks * part :, :] = jnp.zeros((MARG_ROWS, width), bf16)
        for b in range(blocks):
            out[blocks * part + b : blocks * part + b + 1, :part] = marg[b : b + 1, :]


def pack(row_emb, row_marg, col_emb, col_marg):
    args = (row_emb, row_marg, col_emb, col_marg)
    return pl.pallas_call(
        pack_kernel,
        out_shape=[
            shape((e.shape[0] * e.shape[1] + MARG_ROWS, e.shape[2]), bf16) for e in args[::2]
        ],
        in_specs=[ANY] * 4,
        out_specs=[VMEM] * 2,
        scratch_shapes=[pltpu.VMEM(x.shape, x.dtype) for x in args]
        + [pltpu.SemaphoreType.DMA((4,))],
        compiler_params=pltpu.CompilerParams(vmem_limit_bytes=PACK),
        cost_estimate=cost(0, 1 << 20),
    )(*args)


def levels_kernel(used, tiles, logs, weights, token, tile_buf, sem):
    slots, size, _ = tile_buf.shape
    count = used[0]
    chunk = 64

    def load(slot):
        return pltpu.make_async_copy(tiles.at[slot], tile_buf.at[slot], sem.at[slot])

    for slot in range(slots):

        @pl.when(slot < count)
        def _():
            load(slot).start()

    token[...] = jnp.zeros_like(token)

    def one_tile(slot, carry):
        load(slot).wait()

        def one_chunk(n, carry):
            rows = pl.ds(pl.multiple_of(n * chunk, chunk), chunk)
            counts = tile_buf[slot, rows, :].astype(f32)
            level = jnp.maximum(counts, 1.0)
            logs[slot, rows, :] = jnp.log(level)
            weight = 0.1 + 0.25 * (level * lax.rsqrt(level))
            weights[slot, rows, :] = jnp.where(counts > 0.0, weight, 0.0).astype(bf16)
            return carry

        lax.fori_loop(0, size // chunk, one_chunk, 0)
        return carry

    lax.fori_loop(0, count, one_tile, 0)


def levels(used, tiles):
    return pl.pallas_call(
        levels_kernel,
        out_shape=[shape(tiles.shape, f32), shape(tiles.shape, bf16), shape((8, 128), f32)],
        in_specs=[SMEM, HBM],
        out_specs=[VMEM] * 3,
        scratch_shapes=[
            pltpu.VMEM(tiles.shape, jnp.int32),
            pltpu.SemaphoreType.DMA((tiles.shape[0],)),
        ],
        compiler_params=pltpu.CompilerParams(vmem_limit_bytes=LEVELS),
        cost_estimate=cost(0, 12 << 20),
    )(used, tiles)


def join_kernel(sizes, *refs):
    parts, outs = list(refs[: sum(sizes)]), refs[-len(sizes) :]
    for out in outs:
        for n in range(out.shape[0]):
            part = parts.pop(0)
            out[n] = part[0] if len(part.shape) == 3 else part[...]


def join(parts, sizes, afters):
    piece = parts[0].shape[-2:]
    return list(
        pl.pallas_call(
            functools.partial(join_kernel, sizes),
            out_shape=[shape((size, *piece), bf16) for size in sizes],
            in_specs=[VMEM] * len(parts) + [ANY] * len(afters),
            out_specs=[VMEM] * len(sizes),
            compiler_params=pltpu.CompilerParams(vmem_limit_bytes=SMALL),
            cost_estimate=cost(0, 1 << 20),
        )(*parts, *afters)
    )


def marg_table(pieces, owners, part, size):
    table = jnp.zeros((MARG_ROWS, size), f32)
    for piece, owner in zip(pieces, owners):
        tail = piece[piece.shape[0] - MARG_ROWS :, :MARG_LANES]
        k = lax.broadcasted_iota(jnp.int32, (MARG_LANES, size), 0)
        at = lax.broadcasted_iota(jnp.int32, (MARG_LANES, size), 1)
        place = ((at == k + owner * part) & (k < part)).astype(bf16)
        table += jnp.dot(tail, place, preferred_element_type=f32)
    return table


def work_kernel(first, n_sides, n_row, n_col, row_owner, col_owner, *refs):
    refs = list(refs)

    def take(n):
        return [refs.pop(0) for _ in range(n)]

    listing, used, logs, weights = take(4)
    sides, col_in = take(n_sides), take(n_col)
    row_in = [side.at[n] for side in sides for n in range(side.shape[0])]
    if not first:
        left, right = take(2)
    keep, swap = take(2)
    col_out = take(n_col)
    if first:
        left, right = take(2)
    row_panel, row_turned, col_panel, grad_row, grad_turned, grad_col, even, odd = take(8)

    row_blocks, size, width = row_panel.shape
    col_blocks = col_panel.shape[0]
    row_part, col_part = size // n_row, size // n_col
    half = n_row // 2
    me_row, me_col = lax.axis_index("row"), lax.axis_index("col")
    row_owners = [me_col ^ k for k in row_owner]
    col_owners = [me_row ^ k for k in col_owner]
    row_zero, col_zero = me_row * row_blocks, me_col * col_blocks
    count = used[0]

    for pieces, owners, panel, part in (
        (row_in, row_owners, row_panel, row_part),
        (col_in, col_owners, col_panel, col_part),
    ):
        for piece, owner in zip(pieces, owners):
            start = pl.multiple_of(owner * part, part)
            for b in range(panel.shape[0]):
                panel[b, pl.ds(start, part), :] = piece[b * part : (b + 1) * part, :]

    if first:
        row_table = marg_table(row_in, row_owners, row_part, size).astype(bf16)
        for b in range(row_blocks):
            pick = (lax.broadcasted_iota(jnp.int32, (MARG_ROWS, 128), 0) == b).astype(bf16)
            left[b] = lax.dot_general(
                row_table, pick, (((0,), (0,)), ((), ())), preferred_element_type=f32
            )
        col_table = marg_table(col_in, col_owners, col_part, size)
        for b in range(col_blocks):
            right[b] = jnp.broadcast_to(col_table[b : b + 1, :], right.shape[1:])

    chunks = [slice(at, at + 256) for at in range(0, size, 256)]

    def place(slot):
        return listing[0, slot] - row_zero, listing[1, slot] - col_zero

    def make_signal(slot, rows, signal):
        i, j = place(slot)
        scores = lax.dot_general(
            row_panel[i, rows, :], col_panel[j], (((1,), (1,)), ((), ())), preferred_element_type=f32
        )
        marg_left = jnp.concatenate([left[i, rows, :]] * (size // 128), axis=1)
        diff = (scores + marg_left + right[j, 0:1, :] - logs[slot, rows, :]).astype(bf16)
        weight = weights[slot, rows, :]
        half_one = jnp.asarray(0.5, bf16)
        flat = half_one * jnp.tanh(half_one * diff) + half_one
        signal[rows, :] = jnp.where(weight > 0, weight * diff, flat)

    def add_row(slot, rows, signal):
        i, j = place(slot)
        grad_row[i, rows, :] += jnp.dot(signal[rows, :], col_panel[j], preferred_element_type=f32)

    def add_col(slot, signal):
        i, j = place(slot)
        grad_turned[j] += jnp.dot(row_turned[i], signal[...], preferred_element_type=f32)

    def step(slot, before, now):
        for rows in chunks:
            make_signal(slot, rows, now)
            add_row(slot - 1, rows, before)
        add_col(slot - 1, before)

    pairs = (count - 1) // 2

    def pair(n, carry):
        step(2 * n + 1, even, odd)
        step(2 * n + 2, odd, even)
        return carry

    for rows in chunks:
        make_signal(0, rows, even)
    for b in range(row_blocks):
        row_turned[b] = row_panel[b].T
    grad_row[...] = jnp.zeros_like(grad_row)
    grad_turned[...] = jnp.zeros_like(grad_turned)
    lax.fori_loop(0, pairs, pair, 0)

    @pl.when(2 * pairs + 1 < count)
    def _():
        step(2 * pairs + 1, even, odd)

    for parity, signal in enumerate((even, odd)):

        @pl.when(lax.rem(count - 1, 2) == parity)
        def _():
            for rows in chunks:
                add_row(count - 1, rows, signal)
            add_col(count - 1, signal)

    for n in range(n_row):
        place, sibling = row_owner[n] >> 1, row_owner[n] & 1
        start = pl.multiple_of(row_owners[n] * row_part, row_part)
        piece = grad_row[:, pl.ds(start, row_part), :]
        if sibling:
            swap[place] = piece.astype(bf16)
        else:
            keep[place] = piece
    for b in range(col_blocks):
        grad_col[b] = grad_turned[b].astype(bf16).T
    for n in range(n_col):
        start = pl.multiple_of(col_owners[n] * col_part, col_part)
        col_out[n][...] = grad_col[:, pl.ds(start, col_part), :]


def work(listing, used, tabs, row_in, col_in, tables, row_owner, col_owner, dims):
    row_blocks, col_blocks, size, width = dims
    first = tables is None
    n_row, n_col = len(row_owner), len(col_owner)
    row_part, col_part = size // n_row, size // n_col
    half = n_row // 2
    outs = [
        shape((half, row_blocks, row_part, width), f32),
        shape((half, row_blocks, row_part, width), bf16),
    ] + [shape((col_blocks, col_part, width), bf16)] * n_col
    if first:
        outs += [shape((row_blocks, size, 128), f32), shape((col_blocks, 8, size), f32)]
    args = [listing, used, *tabs, *row_in, *col_in] + ([] if first else list(tables))
    res = pl.pallas_call(
        functools.partial(work_kernel, first, len(row_in), n_row, n_col, row_owner, col_owner),
        out_shape=outs,
        in_specs=[SMEM, SMEM] + [VMEM] * (len(args) - 2),
        out_specs=[VMEM] * len(outs),
        scratch_shapes=[
            pltpu.VMEM((row_blocks, size, width), bf16),
            pltpu.VMEM((row_blocks, width, size), bf16),
            pltpu.VMEM((col_blocks, size, width), bf16),
            pltpu.VMEM((row_blocks, size, width), f32),
            pltpu.VMEM((col_blocks, width, size), f32),
            pltpu.VMEM((col_blocks, size, width), bf16),
            pltpu.VMEM((size, size), bf16),
            pltpu.VMEM((size, size), bf16),
        ],
        compiler_params=pltpu.CompilerParams(vmem_limit_bytes=LARGE),
        cost_estimate=cost(8 * 6 * size * size * width, 16 << 20),
    )(*args)
    return res[0], res[1], res[2 : 2 + n_col], res[2 + n_col :]


def merge_kernel(n_held, keep, got, *refs):
    held, outs = refs[:n_held], refs[n_held:]
    for n in range(keep.shape[0]):
        outs[n][...] = (keep[n] + got[n].astype(f32)).astype(outs[n].dtype)
    for src, out in zip(held, outs[keep.shape[0] :]):
        out[...] = src[...]


def merge(keep, got, kept, held):
    n, *piece = keep.shape
    outs = [shape(tuple(piece), f32 if k in kept else bf16) for k in range(n)]
    outs += [shape(x.shape, x.dtype) for x in held]
    return pl.pallas_call(
        functools.partial(merge_kernel, len(held)),
        out_shape=outs,
        in_specs=[VMEM] * (2 + len(held)),
        out_specs=[VMEM] * len(outs),
        compiler_params=pltpu.CompilerParams(vmem_limit_bytes=SMALL),
        cost_estimate=cost(0, 2 << 20),
    )(keep, got, *held)


def add_kernel(n_parts, n_held, own, *refs):
    parts, held, outs = refs[:n_parts], refs[n_parts : n_parts + n_held], refs[n_parts + n_held :]
    total = own[...]
    for part in parts:
        total += part[...].astype(f32)
    outs[0][...] = total.astype(bf16)
    for src, out in zip(held, outs[1:]):
        out[...] = src[...]


def add(own, parts, held):
    return pl.pallas_call(
        functools.partial(add_kernel, len(parts), len(held)),
        out_shape=[shape(own.shape, bf16)] + [shape(x.shape, x.dtype) for x in held],
        in_specs=[VMEM] * (1 + len(parts) + len(held)),
        out_specs=[VMEM] * (1 + len(held)),
        compiler_params=pltpu.CompilerParams(vmem_limit_bytes=SMALL),
        cost_estimate=cost(0, 1 << 20),
    )(own, *parts, *held)


def update_kernel(n_parts, n_outs, emb, *refs):
    parts, outs = refs[:n_parts], refs[-n_outs:]
    total = parts[0][...].astype(f32)
    for part in parts[1:]:
        total += part[...].astype(f32)
    new = emb[...] - RATE * total
    outs[0][...] = new
    if len(outs) > 1:
        outs[1][...] = new.astype(bf16).reshape(outs[1].shape)


def update(emb, parts, afters, last):
    blocks, part, width = emb.shape
    outs = [shape(emb.shape, f32)]
    if not last:
        outs.append(shape((blocks * part, width), bf16))
    res = pl.pallas_call(
        functools.partial(update_kernel, len(parts), len(outs)),
        out_shape=outs,
        in_specs=[VMEM] * (1 + len(parts)) + [ANY] * len(afters),
        out_specs=[VMEM] * len(outs),
        compiler_params=pltpu.CompilerParams(vmem_limit_bytes=SMALL),
        cost_estimate=cost(0, 1 << 20),
    )(emb, *parts, *afters)
    return res if not last else (res[0], None)


def send(x, axis, count, mask):
    return lax.ppermute(x, axis, [(k, k ^ mask) for k in range(count)])


def shards(n_row_dev, n_col_dev, row_emb, col_emb, row_marg, col_marg, tile_list, tile_count, tile_data):
    listing = tile_list[0, 0].T
    used = tile_count[0]
    tiles = tile_data[0, 0]
    dims = (row_emb.shape[0], col_emb.shape[0], tiles.shape[-1], row_emb.shape[-1])
    half = n_col_dev // 2
    far = half // 2
    near = range(1, far)
    row_owner = [2 * k for k in range(half)] + [2 * k + 1 for k in range(half)]
    col_owner = list(range(n_row_dev))

    def hop(x, distance):
        return send(x, "col", n_col_dev, 2 * distance)

    row_pay, col_pay = pack(row_emb, row_marg, col_emb, col_marg)
    *tabs, tabs_made = levels(used, tiles)
    tables = None
    for substep in range(2):
        crossed = hop(row_pay, far)
        col_in = [col_pay] + [send(col_pay, "row", n_row_dev, k) for k in col_owner[1:]]
        if substep == 0:
            before_leg, before_swap, sizes = [tabs_made], col_in[1:-1], [1, far - 1, 1, far - 1]
        else:
            before_leg, before_swap, sizes = col_in[-1:], [], [far, 1, far - 1]
        (crossed,) = join([crossed], [1], before_leg)
        row_in = [row_pay] + [hop(row_pay, k) for k in near] + [crossed] + [hop(crossed, k) for k in near]
        row_in = join(row_in, sizes, before_swap)
        row_in += [send(piece, "col", n_col_dev, 1) for piece in row_in]
        keep, swap, col_out, made = work(
            listing, used, tabs, row_in, col_in, tables, row_owner, col_owner, dims
        )
        tables = tables or made
        held = col_out[-1:] if substep == 1 else []
        merged = merge(keep, send(swap, "col", n_col_dev, 1), (0, far), held)
        col_out = [*col_out[: len(col_out) - len(held)], *merged[half:]]
        relays = [hop(merged[far + k], k) for k in near]
        crossing, *straight = add(merged[far], relays, [merged[k] for k in near])
        col_parts = [col_out[0]] + [send(col_out[k], "row", n_row_dev, k) for k in col_owner[1:]]
        row_parts = [merged[0]] + [hop(x, k) for x, k in zip(straight, near)] + [hop(crossing, far)]
        col_emb, col_pay = update(col_emb, col_parts, [straight[0]], substep == 1)
        row_emb, row_pay = update(row_emb, row_parts, [col_pay if substep == 0 else straight[0]], substep == 1)
    return (row_emb, col_emb)


def solution(mesh):
    placed = (
        P("row", "col", None),
        P("col", "row", None),
        P("row", "col"),
        P("col", "row"),
        P("row", "col", None, None),
        P("row", "col"),
        P("row", "col", None, None, None),
    )
    return jax.shard_map(
        functools.partial(shards, mesh.shape["row"], mesh.shape["col"]),
        mesh=mesh,
        in_specs=placed,
        out_specs=(P("row", "col", None), P("col", "row", None)),
        check_vma=False,
    )
```

```python
import functools

import jax
import jax.numpy as jnp
from jax import lax
from jax.experimental import pallas as pl
from jax.experimental.pallas import tpu as pltpu
from jax.sharding import PartitionSpec as P

RATE = 0.0004
MARG_ROWS = 16
MARG_LANES = 128
ANY = pl.BlockSpec(memory_space=pl.ANY)
HBM = pl.BlockSpec(memory_space=pltpu.HBM)
VMEM = pl.BlockSpec(memory_space=pltpu.VMEM)
SMEM = pl.BlockSpec(memory_space=pltpu.SMEM)
SMALL = 12 << 20
LARGE = 16 << 20
LEVELS = 35 << 20
PACK = 62 << 20
f32, bf16 = jnp.float32, jnp.bfloat16
shape = jax.ShapeDtypeStruct


def cost(flops, moved):
    return pl.CostEstimate(flops=flops, bytes_accessed=moved, transcendentals=0)


def pack_kernel(row_emb, row_marg, col_emb, col_marg, row_out, col_out, *scratch):
    bufs, sem = scratch[:4], scratch[4]
    copies = [
        pltpu.make_async_copy(src, dst, sem.at[n])
        for n, (src, dst) in enumerate(zip((row_emb, row_marg, col_emb, col_marg), bufs))
    ]
    for copy in copies:
        copy.start()
    for n, out in enumerate((row_out, col_out)):
        copies[2 * n].wait()
        copies[2 * n + 1].wait()
        emb, marg = bufs[2 * n], bufs[2 * n + 1]
        blocks, part, width = emb.shape
        out[: blocks * part, :] = emb[...].astype(bf16).reshape(blocks * part, width)
        out[blocks * part :, :] = jnp.zeros((MARG_ROWS, width), bf16)
        for b in range(blocks):
            out[blocks * part + b : blocks * part + b + 1, :part] = marg[b : b + 1, :]


def pack(row_emb, row_marg, col_emb, col_marg):
    args = (row_emb, row_marg, col_emb, col_marg)
    return pl.pallas_call(
        pack_kernel,
        out_shape=[
            shape((e.shape[0] * e.shape[1] + MARG_ROWS, e.shape[2]), bf16) for e in args[::2]
        ],
        in_specs=[ANY] * 4,
        out_specs=[VMEM] * 2,
        scratch_shapes=[pltpu.VMEM(x.shape, x.dtype) for x in args]
        + [pltpu.SemaphoreType.DMA((4,))],
        compiler_params=pltpu.CompilerParams(vmem_limit_bytes=PACK),
        cost_estimate=cost(0, 1 << 20),
    )(*args)


def levels_kernel(used, tiles, logs, weights, token, tile_buf, sem):
    slots, size, _ = tile_buf.shape
    count = used[0]
    chunk = 64

    def load(slot):
        return pltpu.make_async_copy(tiles.at[slot], tile_buf.at[slot], sem.at[slot])

    for slot in range(slots):

        @pl.when(slot < count)
        def _():
            load(slot).start()

    token[...] = jnp.zeros_like(token)

    def one_tile(slot, carry):
        load(slot).wait()

        def one_chunk(n, carry):
            rows = pl.ds(pl.multiple_of(n * chunk, chunk), chunk)
            counts = tile_buf[slot, rows, :].astype(f32)
            level = jnp.maximum(counts, 1.0)
            logs[slot, rows, :] = jnp.log(level)
            weight = 0.1 + 0.25 * (level * lax.rsqrt(level))
            weights[slot, rows, :] = jnp.where(counts > 0.0, weight, 0.0).astype(bf16)
            return carry

        lax.fori_loop(0, size // chunk, one_chunk, 0)
        return carry

    lax.fori_loop(0, count, one_tile, 0)


def levels(used, tiles):
    return pl.pallas_call(
        levels_kernel,
        out_shape=[shape(tiles.shape, f32), shape(tiles.shape, bf16), shape((8, 128), f32)],
        in_specs=[SMEM, HBM],
        out_specs=[VMEM] * 3,
        scratch_shapes=[
            pltpu.VMEM(tiles.shape, jnp.int32),
            pltpu.SemaphoreType.DMA((tiles.shape[0],)),
        ],
        compiler_params=pltpu.CompilerParams(vmem_limit_bytes=LEVELS),
        cost_estimate=cost(0, 12 << 20),
    )(used, tiles)


def join_kernel(sizes, *refs):
    parts, outs = list(refs[: sum(sizes)]), refs[-len(sizes) :]
    for out in outs:
        for n in range(out.shape[0]):
            part = parts.pop(0)
            out[n] = part[0] if len(part.shape) == 3 else part[...]


def join(parts, sizes, afters):
    piece = parts[0].shape[-2:]
    return list(
        pl.pallas_call(
            functools.partial(join_kernel, sizes),
            out_shape=[shape((size, *piece), bf16) for size in sizes],
            in_specs=[VMEM] * len(parts) + [ANY] * len(afters),
            out_specs=[VMEM] * len(sizes),
            compiler_params=pltpu.CompilerParams(vmem_limit_bytes=SMALL),
            cost_estimate=cost(0, 1 << 20),
        )(*parts, *afters)
    )


def halves_kernel(upper, lower, first, second):
    first[...] = upper[: first.shape[0], :]
    second[...] = lower[lower.shape[0] - second.shape[0] :, :]


def halves(upper, lower, rows):
    return pl.pallas_call(
        halves_kernel,
        out_shape=[
            shape((rows, upper.shape[1]), bf16),
            shape((lower.shape[0] - rows, lower.shape[1]), bf16),
        ],
        in_specs=[VMEM] * 2,
        out_specs=[VMEM] * 2,
        compiler_params=pltpu.CompilerParams(vmem_limit_bytes=SMALL),
        cost_estimate=cost(0, 1 << 20),
    )(upper, lower)


def marg_table(pieces, owners, part, size):
    table = jnp.zeros((MARG_ROWS, size), f32)
    for piece, owner in zip(pieces, owners):
        last = piece[-1]
        tail = last[last.shape[0] - MARG_ROWS :, :MARG_LANES]
        k = lax.broadcasted_iota(jnp.int32, (MARG_LANES, size), 0)
        at = lax.broadcasted_iota(jnp.int32, (MARG_LANES, size), 1)
        place = ((at == k + owner * part) & (k < part)).astype(bf16)
        table += jnp.dot(tail, place, preferred_element_type=f32)
    return table


def fill(panel, pieces, owners, part):
    blocks = panel.shape[0]
    for piece, owner in zip(pieces, owners):
        start = pl.multiple_of(owner * part, part)
        each = blocks // len(piece)
        for b in range(blocks):
            at = b % each * part
            panel[b, pl.ds(start, part), :] = piece[b // each][at : at + part, :]


def work_kernel(first, n_sides, n_cut, n_row, n_col, row_owner, col_owner, *refs):
    refs = list(refs)

    def take(n):
        return [refs.pop(0) for _ in range(n)]

    listing, used, logs, weights = take(4)
    sides = take(n_sides)
    row_in = [[side.at[n]] for side in sides for n in range(side.shape[0])]
    col_in = [take(2 if n >= n_col - n_cut else 1) for n in range(n_col)]
    if not first:
        left, right = take(2)
    keep, swap = take(2)
    col_out = take(n_col)
    if first:
        left, right = take(2)
    row_panel, row_turned, col_panel, grad_row, grad_turned, grad_col, even, odd = take(8)

    row_blocks, size, width = row_panel.shape
    col_blocks = col_panel.shape[0]
    row_part, col_part = size // n_row, size // n_col
    half = n_row // 2
    me_row, me_col = lax.axis_index("row"), lax.axis_index("col")
    row_owners = [me_col ^ k for k in row_owner]
    col_owners = [me_row ^ k for k in col_owner]
    row_zero, col_zero = me_row * row_blocks, me_col * col_blocks
    count = used[0]

    fill(row_panel, row_in, row_owners, row_part)
    fill(col_panel, col_in, col_owners, col_part)

    if first:
        row_table = marg_table(row_in, row_owners, row_part, size).astype(bf16)
        for b in range(row_blocks):
            pick = (lax.broadcasted_iota(jnp.int32, (MARG_ROWS, 128), 0) == b).astype(bf16)
            left[b] = lax.dot_general(
                row_table, pick, (((0,), (0,)), ((), ())), preferred_element_type=f32
            )
        col_table = marg_table(col_in, col_owners, col_part, size)
        for b in range(col_blocks):
            right[b] = jnp.broadcast_to(col_table[b : b + 1, :], right.shape[1:])

    chunks = [slice(at, at + 256) for at in range(0, size, 256)]

    def place(slot):
        return listing[0, slot] - row_zero, listing[1, slot] - col_zero

    def make_signal(slot, rows, signal):
        i, j = place(slot)
        scores = lax.dot_general(
            row_panel[i, rows, :], col_panel[j], (((1,), (1,)), ((), ())), preferred_element_type=f32
        )
        marg_left = jnp.concatenate([left[i, rows, :]] * (size // 128), axis=1)
        diff = (scores + marg_left + right[j, 0:1, :] - logs[slot, rows, :]).astype(bf16)
        weight = weights[slot, rows, :]
        half_one = jnp.asarray(0.5, bf16)
        flat = half_one * jnp.tanh(half_one * diff) + half_one
        signal[rows, :] = jnp.where(weight > 0, weight * diff, flat)

    def add_row(slot, rows, signal):
        i, j = place(slot)
        grad_row[i, rows, :] += jnp.dot(signal[rows, :], col_panel[j], preferred_element_type=f32)

    def add_col(slot, signal):
        i, j = place(slot)
        grad_turned[j] += jnp.dot(row_turned[i], signal[...], preferred_element_type=f32)

    def step(slot, before, now):
        for rows in chunks:
            make_signal(slot, rows, now)
            add_row(slot - 1, rows, before)
        add_col(slot - 1, before)

    pairs = (count - 1) // 2

    def pair(n, carry):
        step(2 * n + 1, even, odd)
        step(2 * n + 2, odd, even)
        return carry

    for rows in chunks:
        make_signal(0, rows, even)
    for b in range(row_blocks):
        row_turned[b] = row_panel[b].T
    grad_row[...] = jnp.zeros_like(grad_row)
    grad_turned[...] = jnp.zeros_like(grad_turned)
    lax.fori_loop(0, pairs, pair, 0)

    @pl.when(2 * pairs + 1 < count)
    def _():
        step(2 * pairs + 1, even, odd)

    for parity, signal in enumerate((even, odd)):

        @pl.when(lax.rem(count - 1, 2) == parity)
        def _():
            for rows in chunks:
                add_row(count - 1, rows, signal)
            add_col(count - 1, signal)

    for n in range(n_row):
        place, sibling = row_owner[n] >> 1, row_owner[n] & 1
        start = pl.multiple_of(row_owners[n] * row_part, row_part)
        piece = grad_row[:, pl.ds(start, row_part), :]
        if sibling:
            swap[place] = piece.astype(bf16)
        else:
            keep[place] = piece
    for b in range(col_blocks):
        grad_col[b] = grad_turned[b].astype(bf16).T
    for n in range(n_col):
        start = pl.multiple_of(col_owners[n] * col_part, col_part)
        col_out[n][...] = grad_col[:, pl.ds(start, col_part), :]


def work(listing, used, tabs, row_in, col_in, n_cut, tables, row_owner, col_owner, dims):
    row_blocks, col_blocks, size, width = dims
    first = tables is None
    n_row, n_col = len(row_owner), len(col_owner)
    row_part, col_part = size // n_row, size // n_col
    half = n_row // 2
    outs = [
        shape((half, row_blocks, row_part, width), f32),
        shape((half, row_blocks, row_part, width), bf16),
    ] + [shape((col_blocks, col_part, width), bf16)] * n_col
    if first:
        outs += [shape((row_blocks, size, 128), f32), shape((col_blocks, 8, size), f32)]
    args = [listing, used, *tabs, *row_in, *col_in] + ([] if first else list(tables))
    res = pl.pallas_call(
        functools.partial(work_kernel, first, len(row_in), n_cut, n_row, n_col, row_owner, col_owner),
        out_shape=outs,
        in_specs=[SMEM, SMEM] + [VMEM] * (len(args) - 2),
        out_specs=[VMEM] * len(outs),
        scratch_shapes=[
            pltpu.VMEM((row_blocks, size, width), bf16),
            pltpu.VMEM((row_blocks, width, size), bf16),
            pltpu.VMEM((col_blocks, size, width), bf16),
            pltpu.VMEM((row_blocks, size, width), f32),
            pltpu.VMEM((col_blocks, width, size), f32),
            pltpu.VMEM((col_blocks, size, width), bf16),
            pltpu.VMEM((size, size), bf16),
            pltpu.VMEM((size, size), bf16),
        ],
        compiler_params=pltpu.CompilerParams(vmem_limit_bytes=LARGE),
        cost_estimate=cost(8 * 6 * size * size * width, 16 << 20),
    )(*args)
    return res[0], res[1], res[2 : 2 + n_col], res[2 + n_col :]


def merge_kernel(n_held, keep, got, *refs):
    held, outs = refs[:n_held], refs[n_held:]
    for n in range(keep.shape[0]):
        outs[n][...] = (keep[n] + got[n].astype(f32)).astype(outs[n].dtype)
    for src, out in zip(held, outs[keep.shape[0] :]):
        out[...] = src[...]


def merge(keep, got, kept, held):
    n, *piece = keep.shape
    outs = [shape(tuple(piece), f32 if k in kept else bf16) for k in range(n)]
    outs += [shape(x.shape, x.dtype) for x in held]
    return pl.pallas_call(
        functools.partial(merge_kernel, len(held)),
        out_shape=outs,
        in_specs=[VMEM] * (2 + len(held)),
        out_specs=[VMEM] * len(outs),
        compiler_params=pltpu.CompilerParams(vmem_limit_bytes=SMALL),
        cost_estimate=cost(0, 2 << 20),
    )(keep, got, *held)


def add_kernel(n_parts, n_held, own, *refs):
    parts, held, outs = refs[:n_parts], refs[n_parts : n_parts + n_held], refs[n_parts + n_held :]
    total = own[...]
    for part in parts:
        total += part[...].astype(f32)
    outs[0][...] = total.astype(bf16)
    for src, out in zip(held, outs[1:]):
        out[...] = src[...]


def add(own, parts, held):
    return pl.pallas_call(
        functools.partial(add_kernel, len(parts), len(held)),
        out_shape=[shape(own.shape, bf16)] + [shape(x.shape, x.dtype) for x in held],
        in_specs=[VMEM] * (1 + len(parts) + len(held)),
        out_specs=[VMEM] * (1 + len(held)),
        compiler_params=pltpu.CompilerParams(vmem_limit_bytes=SMALL),
        cost_estimate=cost(0, 1 << 20),
    )(own, *parts, *held)


def update_kernel(n_parts, n_outs, emb, *refs):
    parts, outs = refs[:n_parts], refs[-n_outs:]
    total = parts[0][...].astype(f32)
    for part in parts[1:]:
        total += part[...].astype(f32)
    new = emb[...] - RATE * total
    outs[0][...] = new
    if len(outs) > 1:
        outs[1][...] = new.astype(bf16).reshape(outs[1].shape)


def update(emb, parts, afters, last):
    blocks, part, width = emb.shape
    outs = [shape(emb.shape, f32)]
    if not last:
        outs.append(shape((blocks * part, width), bf16))
    res = pl.pallas_call(
        functools.partial(update_kernel, len(parts), len(outs)),
        out_shape=outs,
        in_specs=[VMEM] * (1 + len(parts)) + [ANY] * len(afters),
        out_specs=[VMEM] * len(outs),
        compiler_params=pltpu.CompilerParams(vmem_limit_bytes=SMALL),
        cost_estimate=cost(0, 1 << 20),
    )(emb, *parts, *afters)
    return res if not last else (res[0], None)


def send(x, axis, count, mask):
    return lax.ppermute(x, axis, [(k, k ^ mask) for k in range(count)])


def shards(n_row_dev, n_col_dev, row_emb, col_emb, row_marg, col_marg, tile_list, tile_count, tile_data):
    listing = tile_list[0, 0].T
    used = tile_count[0]
    tiles = tile_data[0, 0]
    dims = (row_emb.shape[0], col_emb.shape[0], tiles.shape[-1], row_emb.shape[-1])
    half = n_col_dev // 2
    far = half // 2
    near = range(1, far)
    row_owner = [2 * k for k in range(half)] + [2 * k + 1 for k in range(half)]
    col_owner = list(range(n_row_dev))

    def hop(x, distance):
        return send(x, "col", n_col_dev, 2 * distance)

    n_cut = 1 if n_row_dev == 4 and dims[1] % 2 == 0 else 0
    row_pay, col_pay = pack(row_emb, row_marg, col_emb, col_marg)
    *tabs, tabs_made = levels(used, tiles)
    tables = None
    for substep in range(2):
        crossed = hop(row_pay, far)
        if substep == 0:
            (crossed,) = join([crossed], [1], [tabs_made])
        straight = [row_pay] + [hop(row_pay, k) for k in near] + [crossed]
        relayed = [hop(crossed, k) for k in near]
        if n_cut:
            x_piece, y_piece = (send(col_pay, "row", n_row_dev, k) for k in (1, 2))
            first, second = halves(x_piece, y_piece, dims[1] // 2 * col_emb.shape[1])
            legs = [send(first, "row", n_row_dev, 2), send(second, "row", n_row_dev, 1)]
            col_in = [col_pay, x_piece, y_piece, *legs]
        else:
            legs = [send(col_pay, "row", n_row_dev, k) for k in col_owner[1:]]
            col_in = [col_pay, *legs]
        row_in = join(straight, [far + 1], []) + join(relayed, [far - 1], legs)
        row_in += [send(piece, "col", n_col_dev, 1) for piece in row_in]
        keep, swap, col_out, made = work(
            listing, used, tabs, row_in, col_in, n_cut, tables, row_owner, col_owner, dims
        )
        tables = tables or made
        held = col_out[-1:] if substep == 1 else []
        merged = merge(keep, send(swap, "col", n_col_dev, 1), (0, far), held)
        col_out = [*col_out[: len(col_out) - len(held)], *merged[half:]]
        relays = [hop(merged[far + k], k) for k in near]
        crossing, *straight = add(merged[far], relays, [merged[k] for k in near])
        col_parts = [col_out[0]] + [send(col_out[k], "row", n_row_dev, k) for k in col_owner[1:]]
        row_parts = [merged[0]] + [hop(x, k) for x, k in zip(straight, near)] + [hop(crossing, far)]
        col_emb, col_pay = update(col_emb, col_parts, [straight[0]], substep == 1)
        row_emb, row_pay = update(row_emb, row_parts, [col_pay if substep == 0 else straight[0]], substep == 1)
    return (row_emb, col_emb)


def solution(mesh):
    placed = (
        P("row", "col", None),
        P("col", "row", None),
        P("row", "col"),
        P("col", "row"),
        P("row", "col", None, None),
        P("row", "col"),
        P("row", "col", None, None, None),
    )
    return jax.shard_map(
        functools.partial(shards, mesh.shape["row"], mesh.shape["col"]),
        mesh=mesh,
        in_specs=placed,
        out_specs=(P("row", "col", None), P("col", "row", None)),
        check_vma=False,
    )
```

```python
import functools

import jax
import jax.numpy as jnp
from jax import lax
from jax.experimental import pallas as pl
from jax.experimental.pallas import tpu as pltpu
from jax.sharding import PartitionSpec as P

RATE = 0.0004
MARG_ROWS = 16
MARG_LANES = 128
ANY = pl.BlockSpec(memory_space=pl.ANY)
HBM = pl.BlockSpec(memory_space=pltpu.HBM)
VMEM = pl.BlockSpec(memory_space=pltpu.VMEM)
SMEM = pl.BlockSpec(memory_space=pltpu.SMEM)
SMALL = 12 << 20
LARGE = 16 << 20
LEVELS = 35 << 20
PACK = 62 << 20
f32, bf16 = jnp.float32, jnp.bfloat16
shape = jax.ShapeDtypeStruct


def cost(flops, moved):
    return pl.CostEstimate(flops=flops, bytes_accessed=moved, transcendentals=0)


def pack_kernel(row_emb, row_marg, col_emb, col_marg, row_out, col_out, *scratch):
    bufs, sem = scratch[:4], scratch[4]
    copies = [
        pltpu.make_async_copy(src, dst, sem.at[n])
        for n, (src, dst) in enumerate(zip((row_emb, row_marg, col_emb, col_marg), bufs))
    ]
    for copy in copies:
        copy.start()
    for n, out in enumerate((row_out, col_out)):
        copies[2 * n].wait()
        copies[2 * n + 1].wait()
        emb, marg = bufs[2 * n], bufs[2 * n + 1]
        blocks, part, width = emb.shape
        out[: blocks * part, :] = emb[...].astype(bf16).reshape(blocks * part, width)
        out[blocks * part :, :] = jnp.zeros((MARG_ROWS, width), bf16)
        for b in range(blocks):
            out[blocks * part + b : blocks * part + b + 1, :part] = marg[b : b + 1, :]


def pack(row_emb, row_marg, col_emb, col_marg):
    args = (row_emb, row_marg, col_emb, col_marg)
    return pl.pallas_call(
        pack_kernel,
        out_shape=[
            shape((e.shape[0] * e.shape[1] + MARG_ROWS, e.shape[2]), bf16) for e in args[::2]
        ],
        in_specs=[ANY] * 4,
        out_specs=[VMEM] * 2,
        scratch_shapes=[pltpu.VMEM(x.shape, x.dtype) for x in args]
        + [pltpu.SemaphoreType.DMA((4,))],
        compiler_params=pltpu.CompilerParams(vmem_limit_bytes=PACK),
        cost_estimate=cost(0, 1 << 20),
    )(*args)


def levels_kernel(used, tiles, logs, weights, token, tile_buf, sem):
    slots, size, _ = tile_buf.shape
    count = used[0]
    chunk = 64

    def load(slot):
        return pltpu.make_async_copy(tiles.at[slot], tile_buf.at[slot], sem.at[slot])

    for slot in range(slots):

        @pl.when(slot < count)
        def _():
            load(slot).start()

    token[...] = jnp.zeros_like(token)

    def one_tile(slot, carry):
        load(slot).wait()

        def one_chunk(n, carry):
            rows = pl.ds(pl.multiple_of(n * chunk, chunk), chunk)
            counts = tile_buf[slot, rows, :].astype(f32)
            level = jnp.maximum(counts, 1.0)
            logs[slot, rows, :] = jnp.log(level)
            weight = 0.1 + 0.25 * (level * lax.rsqrt(level))
            weights[slot, rows, :] = jnp.where(counts > 0.0, weight, 0.0).astype(bf16)
            return carry

        lax.fori_loop(0, size // chunk, one_chunk, 0)
        return carry

    lax.fori_loop(0, count, one_tile, 0)


def levels(used, tiles):
    return pl.pallas_call(
        levels_kernel,
        out_shape=[shape(tiles.shape, f32), shape(tiles.shape, bf16), shape((8, 128), f32)],
        in_specs=[SMEM, HBM],
        out_specs=[VMEM] * 3,
        scratch_shapes=[
            pltpu.VMEM(tiles.shape, jnp.int32),
            pltpu.SemaphoreType.DMA((tiles.shape[0],)),
        ],
        compiler_params=pltpu.CompilerParams(vmem_limit_bytes=LEVELS),
        cost_estimate=cost(0, 12 << 20),
    )(used, tiles)


def join_kernel(sizes, *refs):
    parts, outs = list(refs[: sum(sizes)]), refs[-len(sizes) :]
    for out in outs:
        for n in range(out.shape[0]):
            part = parts.pop(0)
            out[n] = part[0] if len(part.shape) == 3 else part[...]


def join(parts, sizes, afters):
    piece = parts[0].shape[-2:]
    return list(
        pl.pallas_call(
            functools.partial(join_kernel, sizes),
            out_shape=[shape((size, *piece), bf16) for size in sizes],
            in_specs=[VMEM] * len(parts) + [ANY] * len(afters),
            out_specs=[VMEM] * len(sizes),
            compiler_params=pltpu.CompilerParams(vmem_limit_bytes=SMALL),
            cost_estimate=cost(0, 1 << 20),
        )(*parts, *afters)
    )


def marg_table(pieces, owners, part, size):
    table = jnp.zeros((MARG_ROWS, size), f32)
    for piece, owner in zip(pieces, owners):
        tail = piece[piece.shape[0] - MARG_ROWS :, :MARG_LANES]
        k = lax.broadcasted_iota(jnp.int32, (MARG_LANES, size), 0)
        at = lax.broadcasted_iota(jnp.int32, (MARG_LANES, size), 1)
        place = ((at == k + owner * part) & (k < part)).astype(bf16)
        table += jnp.dot(tail, place, preferred_element_type=f32)
    return table


def work_kernel(first, n_sides, n_row, n_col, row_owner, col_owner, *refs):
    refs = list(refs)

    def take(n):
        return [refs.pop(0) for _ in range(n)]

    listing, used, logs, weights = take(4)
    sides, col_in = take(n_sides), take(n_col)
    row_in = [side.at[n] for side in sides for n in range(side.shape[0])]
    if not first:
        left, right = take(2)
    keep, swap = take(2)
    col_out = take(n_col)
    if first:
        left, right = take(2)
    row_panel, row_turned, col_panel, grad_row, grad_turned, grad_col, even, odd = take(8)

    row_blocks, size, width = row_panel.shape
    col_blocks = col_panel.shape[0]
    row_part, col_part = size // n_row, size // n_col
    half = n_row // 2
    me_row, me_col = lax.axis_index("row"), lax.axis_index("col")
    row_owners = [me_col ^ k for k in row_owner]
    col_owners = [me_row ^ k for k in col_owner]
    row_zero, col_zero = me_row * row_blocks, me_col * col_blocks
    count = used[0]

    for pieces, owners, panel, part in (
        (row_in, row_owners, row_panel, row_part),
        (col_in, col_owners, col_panel, col_part),
    ):
        for piece, owner in zip(pieces, owners):
            start = pl.multiple_of(owner * part, part)
            for b in range(panel.shape[0]):
                panel[b, pl.ds(start, part), :] = piece[b * part : (b + 1) * part, :]

    if first:
        row_table = marg_table(row_in, row_owners, row_part, size).astype(bf16)
        for b in range(row_blocks):
            pick = (lax.broadcasted_iota(jnp.int32, (MARG_ROWS, 128), 0) == b).astype(bf16)
            left[b] = lax.dot_general(
                row_table, pick, (((0,), (0,)), ((), ())), preferred_element_type=f32
            )
        col_table = marg_table(col_in, col_owners, col_part, size)
        for b in range(col_blocks):
            right[b] = jnp.broadcast_to(col_table[b : b + 1, :], right.shape[1:])

    chunks = [slice(at, at + 256) for at in range(0, size, 256)]

    def place(slot):
        return listing[0, slot] - row_zero, listing[1, slot] - col_zero

    def make_signal(slot, rows, signal):
        i, j = place(slot)
        scores = lax.dot_general(
            row_panel[i, rows, :], col_panel[j], (((1,), (1,)), ((), ())), preferred_element_type=f32
        )
        marg_left = jnp.concatenate([left[i, rows, :]] * (size // 128), axis=1)
        diff = (scores + marg_left + right[j, 0:1, :] - logs[slot, rows, :]).astype(bf16)
        weight = weights[slot, rows, :]
        half_one = jnp.asarray(0.5, bf16)
        flat = half_one * jnp.tanh(half_one * diff) + half_one
        signal[rows, :] = jnp.where(weight > 0, weight * diff, flat)

    def add_row(slot, rows, signal):
        i, j = place(slot)
        grad_row[i, rows, :] += jnp.dot(signal[rows, :], col_panel[j], preferred_element_type=f32)

    def add_col(slot, signal):
        i, j = place(slot)
        grad_turned[j] += jnp.dot(row_turned[i], signal[...], preferred_element_type=f32)

    def step(slot, before, now):
        for rows in chunks:
            make_signal(slot, rows, now)
            add_row(slot - 1, rows, before)
        add_col(slot - 1, before)

    pairs = (count - 1) // 2

    def pair(n, carry):
        step(2 * n + 1, even, odd)
        step(2 * n + 2, odd, even)
        return carry

    for rows in chunks:
        make_signal(0, rows, even)
    for b in range(row_blocks):
        row_turned[b] = row_panel[b].T
    grad_row[...] = jnp.zeros_like(grad_row)
    grad_turned[...] = jnp.zeros_like(grad_turned)
    lax.fori_loop(0, pairs, pair, 0)

    @pl.when(2 * pairs + 1 < count)
    def _():
        step(2 * pairs + 1, even, odd)

    for parity, signal in enumerate((even, odd)):

        @pl.when(lax.rem(count - 1, 2) == parity)
        def _():
            for rows in chunks:
                add_row(count - 1, rows, signal)
            add_col(count - 1, signal)

    for n in range(n_row):
        place, sibling = row_owner[n] >> 1, row_owner[n] & 1
        start = pl.multiple_of(row_owners[n] * row_part, row_part)
        piece = grad_row[:, pl.ds(start, row_part), :]
        if sibling:
            swap[place] = piece.astype(bf16)
        else:
            keep[place] = piece
    for b in range(col_blocks):
        grad_col[b] = grad_turned[b].astype(bf16).T
    for n in range(n_col):
        start = pl.multiple_of(col_owners[n] * col_part, col_part)
        col_out[n][...] = grad_col[:, pl.ds(start, col_part), :]


def work(listing, used, tabs, row_in, col_in, tables, row_owner, col_owner, dims):
    row_blocks, col_blocks, size, width = dims
    first = tables is None
    n_row, n_col = len(row_owner), len(col_owner)
    row_part, col_part = size // n_row, size // n_col
    half = n_row // 2
    outs = [
        shape((half, row_blocks, row_part, width), f32),
        shape((half, row_blocks, row_part, width), bf16),
    ] + [shape((col_blocks, col_part, width), bf16)] * n_col
    if first:
        outs += [shape((row_blocks, size, 128), f32), shape((col_blocks, 8, size), f32)]
    args = [listing, used, *tabs, *row_in, *col_in] + ([] if first else list(tables))
    res = pl.pallas_call(
        functools.partial(work_kernel, first, len(row_in), n_row, n_col, row_owner, col_owner),
        out_shape=outs,
        in_specs=[SMEM, SMEM] + [VMEM] * (len(args) - 2),
        out_specs=[VMEM] * len(outs),
        scratch_shapes=[
            pltpu.VMEM((row_blocks, size, width), bf16),
            pltpu.VMEM((row_blocks, width, size), bf16),
            pltpu.VMEM((col_blocks, size, width), bf16),
            pltpu.VMEM((row_blocks, size, width), f32),
            pltpu.VMEM((col_blocks, width, size), f32),
            pltpu.VMEM((col_blocks, size, width), bf16),
            pltpu.VMEM((size, size), bf16),
            pltpu.VMEM((size, size), bf16),
        ],
        compiler_params=pltpu.CompilerParams(vmem_limit_bytes=LARGE),
        cost_estimate=cost(8 * 6 * size * size * width, 16 << 20),
    )(*args)
    return res[0], res[1], res[2 : 2 + n_col], res[2 + n_col :]


def merge_kernel(n_held, keep, got, *refs):
    held, outs = refs[:n_held], refs[n_held:]
    for n in range(keep.shape[0]):
        outs[n][...] = (keep[n] + got[n].astype(f32)).astype(outs[n].dtype)
    for src, out in zip(held, outs[keep.shape[0] :]):
        out[...] = src[...]


def merge(keep, got, kept, held):
    n, *piece = keep.shape
    outs = [shape(tuple(piece), f32 if k in kept else bf16) for k in range(n)]
    outs += [shape(x.shape, x.dtype) for x in held]
    return pl.pallas_call(
        functools.partial(merge_kernel, len(held)),
        out_shape=outs,
        in_specs=[VMEM] * (2 + len(held)),
        out_specs=[VMEM] * len(outs),
        compiler_params=pltpu.CompilerParams(vmem_limit_bytes=SMALL),
        cost_estimate=cost(0, 2 << 20),
    )(keep, got, *held)


def add_kernel(n_parts, n_held, own, *refs):
    parts, held, outs = refs[:n_parts], refs[n_parts : n_parts + n_held], refs[n_parts + n_held :]
    total = own[...]
    for part in parts:
        total += part[...].astype(f32)
    outs[0][...] = total.astype(bf16)
    for src, out in zip(held, outs[1:]):
        out[...] = src[...]


def add(own, parts, held):
    return pl.pallas_call(
        functools.partial(add_kernel, len(parts), len(held)),
        out_shape=[shape(own.shape, bf16)] + [shape(x.shape, x.dtype) for x in held],
        in_specs=[VMEM] * (1 + len(parts) + len(held)),
        out_specs=[VMEM] * (1 + len(held)),
        compiler_params=pltpu.CompilerParams(vmem_limit_bytes=SMALL),
        cost_estimate=cost(0, 1 << 20),
    )(own, *parts, *held)


def update_kernel(n_parts, n_outs, emb, *refs):
    parts, outs = refs[:n_parts], refs[-n_outs:]
    total = parts[0][...].astype(f32)
    for part in parts[1:]:
        total += part[...].astype(f32)
    new = emb[...] - RATE * total
    outs[0][...] = new
    if len(outs) > 1:
        outs[1][...] = new.astype(bf16).reshape(outs[1].shape)


def update(emb, parts, afters, last):
    blocks, part, width = emb.shape
    outs = [shape(emb.shape, f32)]
    if not last:
        outs.append(shape((blocks * part, width), bf16))
    res = pl.pallas_call(
        functools.partial(update_kernel, len(parts), len(outs)),
        out_shape=outs,
        in_specs=[VMEM] * (1 + len(parts)) + [ANY] * len(afters),
        out_specs=[VMEM] * len(outs),
        compiler_params=pltpu.CompilerParams(vmem_limit_bytes=SMALL),
        cost_estimate=cost(0, 1 << 20),
    )(emb, *parts, *afters)
    return res if not last else (res[0], None)


def send(x, axis, count, mask):
    return lax.ppermute(x, axis, [(k, k ^ mask) for k in range(count)])


def shards(n_row_dev, n_col_dev, row_emb, col_emb, row_marg, col_marg, tile_list, tile_count, tile_data):
    listing = tile_list[0, 0].T
    used = tile_count[0]
    tiles = tile_data[0, 0]
    dims = (row_emb.shape[0], col_emb.shape[0], tiles.shape[-1], row_emb.shape[-1])
    half = n_col_dev // 2
    far = half // 2
    near = range(1, far)
    distances = [0, *reversed(range(1, half))]
    row_owner = [2 * k for k in distances] + [2 * k + 1 for k in distances]
    col_owner = list(range(n_row_dev))

    def hop(x, distance):
        return send(x, "col", n_col_dev, 2 * distance)

    row_pay, col_pay = pack(row_emb, row_marg, col_emb, col_marg)
    *tabs, tabs_made = levels(used, tiles)
    tables = None
    for substep in range(2):
        row_in = [row_pay] + [hop(row_pay, k) for k in distances[1:]]
        col_in = [col_pay] + [send(col_pay, "row", n_row_dev, k) for k in col_owner[1:]]
        row_in = join(row_in, [1] * half, col_in[1:-1] + ([tabs_made] if substep == 0 else []))
        row_in += [send(piece, "col", n_col_dev, 1) for piece in row_in]
        keep, swap, col_out, made = work(
            listing, used, tabs, row_in, col_in, tables, row_owner, col_owner, dims
        )
        tables = tables or made
        held = col_out[-1:] if substep == 1 else []
        merged = merge(keep, send(swap, "col", n_col_dev, 1), (0, far), held)
        col_out = [*col_out[: len(col_out) - len(held)], *merged[half:]]
        relays = [hop(merged[far + k], k) for k in near]
        crossing, *straight = add(merged[far], relays, [merged[k] for k in near])
        col_parts = [col_out[0]] + [send(col_out[k], "row", n_row_dev, k) for k in col_owner[1:]]
        row_parts = [merged[0]] + [hop(x, k) for x, k in zip(straight, near)] + [hop(crossing, far)]
        col_emb, col_pay = update(col_emb, col_parts, [straight[0]], substep == 1)
        row_emb, row_pay = update(row_emb, row_parts, [col_pay if substep == 0 else straight[0]], substep == 1)
    return (row_emb, col_emb)


def solution(mesh):
    placed = (
        P("row", "col", None),
        P("col", "row", None),
        P("row", "col"),
        P("col", "row"),
        P("row", "col", None, None),
        P("row", "col"),
        P("row", "col", None, None, None),
    )
    return jax.shard_map(
        functools.partial(shards, mesh.shape["row"], mesh.shape["col"]),
        mesh=mesh,
        in_specs=placed,
        out_specs=(P("row", "col", None), P("col", "row", None)),
        check_vma=False,
    )
```

```python
import functools

import jax
import jax.numpy as jnp
from jax import lax
from jax.experimental import pallas as pl
from jax.experimental.pallas import tpu as pltpu
from jax.sharding import PartitionSpec as P

RATE = 0.0004
MARG_ROWS = 16
MARG_LANES = 128
ANY = pl.BlockSpec(memory_space=pl.ANY)
HBM = pl.BlockSpec(memory_space=pltpu.HBM)
VMEM = pl.BlockSpec(memory_space=pltpu.VMEM)
SMEM = pl.BlockSpec(memory_space=pltpu.SMEM)
SMALL = 12 << 20
LARGE = 16 << 20
LEVELS = 35 << 20
PACK = 62 << 20
f32, bf16 = jnp.float32, jnp.bfloat16
shape = jax.ShapeDtypeStruct


def cost(flops, moved):
    return pl.CostEstimate(flops=flops, bytes_accessed=moved, transcendentals=0)


def pack_kernel(row_emb, row_marg, col_emb, col_marg, row_out, col_out, *scratch):
    bufs, sem = scratch[:4], scratch[4]
    copies = [
        pltpu.make_async_copy(src, dst, sem.at[n])
        for n, (src, dst) in enumerate(zip((row_emb, row_marg, col_emb, col_marg), bufs))
    ]
    for copy in copies:
        copy.start()
    for n, out in enumerate((row_out, col_out)):
        copies[2 * n].wait()
        copies[2 * n + 1].wait()
        emb, marg = bufs[2 * n], bufs[2 * n + 1]
        blocks, part, width = emb.shape
        out[: blocks * part, :] = emb[...].astype(bf16).reshape(blocks * part, width)
        out[blocks * part :, :] = jnp.zeros((MARG_ROWS, width), bf16)
        for b in range(blocks):
            out[blocks * part + b : blocks * part + b + 1, :part] = marg[b : b + 1, :]


def pack(row_emb, row_marg, col_emb, col_marg):
    args = (row_emb, row_marg, col_emb, col_marg)
    return pl.pallas_call(
        pack_kernel,
        out_shape=[
            shape((e.shape[0] * e.shape[1] + MARG_ROWS, e.shape[2]), bf16) for e in args[::2]
        ],
        in_specs=[ANY] * 4,
        out_specs=[VMEM] * 2,
        scratch_shapes=[pltpu.VMEM(x.shape, x.dtype) for x in args]
        + [pltpu.SemaphoreType.DMA((4,))],
        compiler_params=pltpu.CompilerParams(vmem_limit_bytes=PACK),
        cost_estimate=cost(0, 1 << 20),
    )(*args)


def levels_kernel(used, tiles, logs, weights, token, tile_buf, sem):
    slots, size, _ = tile_buf.shape
    count = used[0]
    chunk = 64

    def load(slot):
        return pltpu.make_async_copy(tiles.at[slot], tile_buf.at[slot], sem.at[slot])

    for slot in range(slots):

        @pl.when(slot < count)
        def _():
            load(slot).start()

    token[...] = jnp.zeros_like(token)

    def one_tile(slot, carry):
        load(slot).wait()

        def one_chunk(n, carry):
            rows = pl.ds(pl.multiple_of(n * chunk, chunk), chunk)
            counts = tile_buf[slot, rows, :].astype(f32)
            level = jnp.maximum(counts, 1.0)
            logs[slot, rows, :] = jnp.log(level)
            weight = 0.1 + 0.25 * (level * lax.rsqrt(level))
            weights[slot, rows, :] = jnp.where(counts > 0.0, weight, 0.0).astype(bf16)
            return carry

        lax.fori_loop(0, size // chunk, one_chunk, 0)
        return carry

    lax.fori_loop(0, count, one_tile, 0)


def levels(used, tiles):
    return pl.pallas_call(
        levels_kernel,
        out_shape=[shape(tiles.shape, f32), shape(tiles.shape, bf16), shape((8, 128), f32)],
        in_specs=[SMEM, HBM],
        out_specs=[VMEM] * 3,
        scratch_shapes=[
            pltpu.VMEM(tiles.shape, jnp.int32),
            pltpu.SemaphoreType.DMA((tiles.shape[0],)),
        ],
        compiler_params=pltpu.CompilerParams(vmem_limit_bytes=LEVELS),
        cost_estimate=cost(0, 12 << 20),
    )(used, tiles)


def join_kernel(sizes, *refs):
    parts, outs = list(refs[: sum(sizes)]), refs[-len(sizes) :]
    for out in outs:
        for n in range(out.shape[0]):
            part = parts.pop(0)
            out[n] = part[0] if len(part.shape) == 3 else part[...]


def join(parts, sizes, afters):
    piece = parts[0].shape[-2:]
    return list(
        pl.pallas_call(
            functools.partial(join_kernel, sizes),
            out_shape=[shape((size, *piece), bf16) for size in sizes],
            in_specs=[VMEM] * len(parts) + [ANY] * len(afters),
            out_specs=[VMEM] * len(sizes),
            compiler_params=pltpu.CompilerParams(vmem_limit_bytes=SMALL),
            cost_estimate=cost(0, 1 << 20),
        )(*parts, *afters)
    )


def marg_table(pieces, owners, part, size):
    table = jnp.zeros((MARG_ROWS, size), f32)
    for piece, owner in zip(pieces, owners):
        tail = piece[piece.shape[0] - MARG_ROWS :, :MARG_LANES]
        k = lax.broadcasted_iota(jnp.int32, (MARG_LANES, size), 0)
        at = lax.broadcasted_iota(jnp.int32, (MARG_LANES, size), 1)
        place = ((at == k + owner * part) & (k < part)).astype(bf16)
        table += jnp.dot(tail, place, preferred_element_type=f32)
    return table


def work_kernel(first, n_sides, n_row, n_col, row_owner, col_owner, *refs):
    refs = list(refs)

    def take(n):
        return [refs.pop(0) for _ in range(n)]

    listing, used, logs, weights = take(4)
    sides, col_in = take(n_sides), take(n_col)
    row_in = [side.at[n] for side in sides for n in range(side.shape[0])]
    if not first:
        left, right = take(2)
    keep, swap = take(2)
    col_out = take(n_col)
    if first:
        left, right = take(2)
    row_panel, row_turned, col_panel, grad_row, grad_turned, grad_col, even, odd = take(8)

    row_blocks, size, width = row_panel.shape
    col_blocks = col_panel.shape[0]
    row_part, col_part = size // n_row, size // n_col
    half = n_row // 2
    me_row, me_col = lax.axis_index("row"), lax.axis_index("col")
    row_owners = [me_col ^ k for k in row_owner]
    col_owners = [me_row ^ k for k in col_owner]
    row_zero, col_zero = me_row * row_blocks, me_col * col_blocks
    count = used[0]

    for pieces, owners, panel, part in (
        (row_in, row_owners, row_panel, row_part),
        (col_in, col_owners, col_panel, col_part),
    ):
        for piece, owner in zip(pieces, owners):
            start = pl.multiple_of(owner * part, part)
            for b in range(panel.shape[0]):
                panel[b, pl.ds(start, part), :] = piece[b * part : (b + 1) * part, :]

    if first:
        row_table = marg_table(row_in, row_owners, row_part, size).astype(bf16)
        for b in range(row_blocks):
            pick = (lax.broadcasted_iota(jnp.int32, (MARG_ROWS, 128), 0) == b).astype(bf16)
            left[b] = lax.dot_general(
                row_table, pick, (((0,), (0,)), ((), ())), preferred_element_type=f32
            )
        col_table = marg_table(col_in, col_owners, col_part, size)
        for b in range(col_blocks):
            right[b] = jnp.broadcast_to(col_table[b : b + 1, :], right.shape[1:])

    chunks = [slice(0, size)]

    def place(slot):
        return listing[0, slot] - row_zero, listing[1, slot] - col_zero

    def make_signal(slot, rows, signal):
        i, j = place(slot)
        scores = lax.dot_general(
            row_panel[i, rows, :], col_panel[j], (((1,), (1,)), ((), ())), preferred_element_type=f32
        )
        marg_left = jnp.concatenate([left[i, rows, :]] * (size // 128), axis=1)
        diff = (scores + marg_left + right[j, 0:1, :] - logs[slot, rows, :]).astype(bf16)
        weight = weights[slot, rows, :]
        half_one = jnp.asarray(0.5, bf16)
        flat = half_one * jnp.tanh(half_one * diff) + half_one
        signal[rows, :] = jnp.where(weight > 0, weight * diff, flat)

    def add_row(slot, rows, signal):
        i, j = place(slot)
        grad_row[i, rows, :] += jnp.dot(signal[rows, :], col_panel[j], preferred_element_type=f32)

    def add_col(slot, signal):
        i, j = place(slot)
        grad_turned[j] += jnp.dot(row_turned[i], signal[...], preferred_element_type=f32)

    def step(slot, before, now):
        for rows in chunks:
            make_signal(slot, rows, now)
            add_row(slot - 1, rows, before)
        add_col(slot - 1, before)

    pairs = (count - 1) // 2

    def pair(n, carry):
        step(2 * n + 1, even, odd)
        step(2 * n + 2, odd, even)
        return carry

    for rows in chunks:
        make_signal(0, rows, even)
    for b in range(row_blocks):
        row_turned[b] = row_panel[b].T
    grad_row[...] = jnp.zeros_like(grad_row)
    grad_turned[...] = jnp.zeros_like(grad_turned)
    lax.fori_loop(0, pairs, pair, 0)

    @pl.when(2 * pairs + 1 < count)
    def _():
        step(2 * pairs + 1, even, odd)

    for parity, signal in enumerate((even, odd)):

        @pl.when(lax.rem(count - 1, 2) == parity)
        def _():
            for rows in chunks:
                add_row(count - 1, rows, signal)
            add_col(count - 1, signal)

    for n in range(n_row):
        place, sibling = row_owner[n] >> 1, row_owner[n] & 1
        start = pl.multiple_of(row_owners[n] * row_part, row_part)
        piece = grad_row[:, pl.ds(start, row_part), :]
        if sibling:
            swap[place] = piece.astype(bf16)
        else:
            keep[place] = piece
    for b in range(col_blocks):
        grad_col[b] = grad_turned[b].astype(bf16).T
    for n in range(n_col):
        start = pl.multiple_of(col_owners[n] * col_part, col_part)
        col_out[n][...] = grad_col[:, pl.ds(start, col_part), :]


def work(listing, used, tabs, row_in, col_in, tables, row_owner, col_owner, dims):
    row_blocks, col_blocks, size, width = dims
    first = tables is None
    n_row, n_col = len(row_owner), len(col_owner)
    row_part, col_part = size // n_row, size // n_col
    half = n_row // 2
    outs = [
        shape((half, row_blocks, row_part, width), f32),
        shape((half, row_blocks, row_part, width), bf16),
    ] + [shape((col_blocks, col_part, width), bf16)] * n_col
    if first:
        outs += [shape((row_blocks, size, 128), f32), shape((col_blocks, 8, size), f32)]
    args = [listing, used, *tabs, *row_in, *col_in] + ([] if first else list(tables))
    res = pl.pallas_call(
        functools.partial(work_kernel, first, len(row_in), n_row, n_col, row_owner, col_owner),
        out_shape=outs,
        in_specs=[SMEM, SMEM] + [VMEM] * (len(args) - 2),
        out_specs=[VMEM] * len(outs),
        scratch_shapes=[
            pltpu.VMEM((row_blocks, size, width), bf16),
            pltpu.VMEM((row_blocks, width, size), bf16),
            pltpu.VMEM((col_blocks, size, width), bf16),
            pltpu.VMEM((row_blocks, size, width), f32),
            pltpu.VMEM((col_blocks, width, size), f32),
            pltpu.VMEM((col_blocks, size, width), bf16),
            pltpu.VMEM((size, size), bf16),
            pltpu.VMEM((size, size), bf16),
        ],
        compiler_params=pltpu.CompilerParams(vmem_limit_bytes=LARGE),
        cost_estimate=cost(8 * 6 * size * size * width, 16 << 20),
    )(*args)
    return res[0], res[1], res[2 : 2 + n_col], res[2 + n_col :]


def merge_kernel(n_held, keep, got, *refs):
    held, outs = refs[:n_held], refs[n_held:]
    for n in range(keep.shape[0]):
        outs[n][...] = (keep[n] + got[n].astype(f32)).astype(outs[n].dtype)
    for src, out in zip(held, outs[keep.shape[0] :]):
        out[...] = src[...]


def merge(keep, got, kept, held):
    n, *piece = keep.shape
    outs = [shape(tuple(piece), f32 if k in kept else bf16) for k in range(n)]
    outs += [shape(x.shape, x.dtype) for x in held]
    return pl.pallas_call(
        functools.partial(merge_kernel, len(held)),
        out_shape=outs,
        in_specs=[VMEM] * (2 + len(held)),
        out_specs=[VMEM] * len(outs),
        compiler_params=pltpu.CompilerParams(vmem_limit_bytes=SMALL),
        cost_estimate=cost(0, 2 << 20),
    )(keep, got, *held)


def add_kernel(n_parts, n_held, own, *refs):
    parts, held, outs = refs[:n_parts], refs[n_parts : n_parts + n_held], refs[n_parts + n_held :]
    total = own[...]
    for part in parts:
        total += part[...].astype(f32)
    outs[0][...] = total.astype(bf16)
    for src, out in zip(held, outs[1:]):
        out[...] = src[...]


def add(own, parts, held):
    return pl.pallas_call(
        functools.partial(add_kernel, len(parts), len(held)),
        out_shape=[shape(own.shape, bf16)] + [shape(x.shape, x.dtype) for x in held],
        in_specs=[VMEM] * (1 + len(parts) + len(held)),
        out_specs=[VMEM] * (1 + len(held)),
        compiler_params=pltpu.CompilerParams(vmem_limit_bytes=SMALL),
        cost_estimate=cost(0, 1 << 20),
    )(own, *parts, *held)


def update_kernel(n_parts, n_outs, emb, *refs):
    parts, outs = refs[:n_parts], refs[-n_outs:]
    total = parts[0][...].astype(f32)
    for part in parts[1:]:
        total += part[...].astype(f32)
    new = emb[...] - RATE * total
    outs[0][...] = new
    if len(outs) > 1:
        outs[1][...] = new.astype(bf16).reshape(outs[1].shape)


def update(emb, parts, afters, last):
    blocks, part, width = emb.shape
    outs = [shape(emb.shape, f32)]
    if not last:
        outs.append(shape((blocks * part, width), bf16))
    res = pl.pallas_call(
        functools.partial(update_kernel, len(parts), len(outs)),
        out_shape=outs,
        in_specs=[VMEM] * (1 + len(parts)) + [ANY] * len(afters),
        out_specs=[VMEM] * len(outs),
        compiler_params=pltpu.CompilerParams(vmem_limit_bytes=SMALL),
        cost_estimate=cost(0, 1 << 20),
    )(emb, *parts, *afters)
    return res if not last else (res[0], None)


def send(x, axis, count, mask):
    return lax.ppermute(x, axis, [(k, k ^ mask) for k in range(count)])


def shards(n_row_dev, n_col_dev, row_emb, col_emb, row_marg, col_marg, tile_list, tile_count, tile_data):
    listing = tile_list[0, 0].T
    used = tile_count[0]
    tiles = tile_data[0, 0]
    dims = (row_emb.shape[0], col_emb.shape[0], tiles.shape[-1], row_emb.shape[-1])
    half = n_col_dev // 2
    far = half // 2
    near = range(1, far)
    distances = [0, *reversed(range(1, half))]
    row_owner = [2 * k for k in distances] + [2 * k + 1 for k in distances]
    col_owner = list(range(n_row_dev))

    def hop(x, distance):
        return send(x, "col", n_col_dev, 2 * distance)

    row_pay, col_pay = pack(row_emb, row_marg, col_emb, col_marg)
    *tabs, tabs_made = levels(used, tiles)
    tables = None
    for substep in range(2):
        col_in = [col_pay] + [send(col_pay, "row", n_row_dev, k) for k in col_owner[1:]]
        if substep == 0:
            crossed = hop(row_pay, far)
            (leg,) = join([crossed], [1], [tabs_made])
            row_in = {0: row_pay, far: leg} | {k: hop(row_pay, k) for k in near}
            row_in |= {far + k: hop(leg, k) for k in near}
        else:
            row_in = {0: row_pay} | {k: hop(row_pay, k) for k in distances[1:]}
        row_in = join([row_in[k] for k in distances], [1] * half, col_in[1:-1])
        row_in += [send(piece, "col", n_col_dev, 1) for piece in row_in]
        keep, swap, col_out, made = work(
            listing, used, tabs, row_in, col_in, tables, row_owner, col_owner, dims
        )
        tables = tables or made
        held = col_out[-1:] if substep == 1 else []
        merged = merge(keep, send(swap, "col", n_col_dev, 1), (0, far), held)
        col_out = [*col_out[: len(col_out) - len(held)], *merged[half:]]
        relays = [hop(merged[far + k], k) for k in near]
        crossing, *straight = add(merged[far], relays, [merged[k] for k in near])
        col_parts = [col_out[0]] + [send(col_out[k], "row", n_row_dev, k) for k in col_owner[1:]]
        row_parts = [merged[0]] + [hop(x, k) for x, k in zip(straight, near)] + [hop(crossing, far)]
        col_emb, col_pay = update(col_emb, col_parts, [straight[0]], substep == 1)
        row_emb, row_pay = update(row_emb, row_parts, [col_pay if substep == 0 else straight[0]], substep == 1)
    return (row_emb, col_emb)


def solution(mesh):
    placed = (
        P("row", "col", None),
        P("col", "row", None),
        P("row", "col"),
        P("col", "row"),
        P("row", "col", None, None),
        P("row", "col"),
        P("row", "col", None, None, None),
    )
    return jax.shard_map(
        functools.partial(shards, mesh.shape["row"], mesh.shape["col"]),
        mesh=mesh,
        in_specs=placed,
        out_specs=(P("row", "col", None), P("col", "row", None)),
        check_vma=False,
    )
```

```python
import functools

import jax
import jax.numpy as jnp
from jax import lax
from jax.experimental import pallas as pl
from jax.experimental.pallas import tpu as pltpu
from jax.sharding import PartitionSpec as P

RATE = 0.0004
MARG_ROWS = 16
MARG_LANES = 128
ANY = pl.BlockSpec(memory_space=pl.ANY)
HBM = pl.BlockSpec(memory_space=pltpu.HBM)
VMEM = pl.BlockSpec(memory_space=pltpu.VMEM)
SMEM = pl.BlockSpec(memory_space=pltpu.SMEM)
SMALL = 12 << 20
LARGE = 16 << 20
LEVELS = 35 << 20
PACK = 62 << 20
f32, bf16 = jnp.float32, jnp.bfloat16
shape = jax.ShapeDtypeStruct


def cost(flops, moved):
    return pl.CostEstimate(flops=flops, bytes_accessed=moved, transcendentals=0)


def pack_kernel(row_emb, row_marg, col_emb, col_marg, row_out, col_out, *scratch):
    bufs, sem = scratch[:4], scratch[4]
    copies = [
        pltpu.make_async_copy(src, dst, sem.at[n])
        for n, (src, dst) in enumerate(zip((row_emb, row_marg, col_emb, col_marg), bufs))
    ]
    for copy in copies:
        copy.start()
    for n, out in enumerate((row_out, col_out)):
        copies[2 * n].wait()
        copies[2 * n + 1].wait()
        emb, marg = bufs[2 * n], bufs[2 * n + 1]
        blocks, part, width = emb.shape
        out[: blocks * part, :] = emb[...].astype(bf16).reshape(blocks * part, width)
        out[blocks * part :, :] = jnp.zeros((MARG_ROWS, width), bf16)
        for b in range(blocks):
            out[blocks * part + b : blocks * part + b + 1, :part] = marg[b : b + 1, :]


def pack(row_emb, row_marg, col_emb, col_marg):
    args = (row_emb, row_marg, col_emb, col_marg)
    return pl.pallas_call(
        pack_kernel,
        out_shape=[
            shape((e.shape[0] * e.shape[1] + MARG_ROWS, e.shape[2]), bf16) for e in args[::2]
        ],
        in_specs=[ANY] * 4,
        out_specs=[VMEM] * 2,
        scratch_shapes=[pltpu.VMEM(x.shape, x.dtype) for x in args]
        + [pltpu.SemaphoreType.DMA((4,))],
        compiler_params=pltpu.CompilerParams(vmem_limit_bytes=PACK),
        cost_estimate=cost(0, 1 << 20),
    )(*args)


def levels_kernel(used, tiles, logs, weights, token, tile_buf, sem):
    slots, size, _ = tile_buf.shape
    count = used[0]
    chunk = 64

    def load(slot):
        return pltpu.make_async_copy(tiles.at[slot], tile_buf.at[slot], sem.at[slot])

    for slot in range(slots):

        @pl.when(slot < count)
        def _():
            load(slot).start()

    token[...] = jnp.zeros_like(token)

    def one_tile(slot, carry):
        load(slot).wait()

        def one_chunk(n, carry):
            rows = pl.ds(pl.multiple_of(n * chunk, chunk), chunk)
            counts = tile_buf[slot, rows, :].astype(f32)
            level = jnp.maximum(counts, 1.0)
            logs[slot, rows, :] = jnp.log(level)
            weight = 0.1 + 0.25 * (level * lax.rsqrt(level))
            weights[slot, rows, :] = jnp.where(counts > 0.0, weight, 0.0).astype(bf16)
            return carry

        lax.fori_loop(0, size // chunk, one_chunk, 0)
        return carry

    lax.fori_loop(0, count, one_tile, 0)


def levels(used, tiles):
    return pl.pallas_call(
        levels_kernel,
        out_shape=[shape(tiles.shape, f32), shape(tiles.shape, bf16), shape((8, 128), f32)],
        in_specs=[SMEM, HBM],
        out_specs=[VMEM] * 3,
        scratch_shapes=[
            pltpu.VMEM(tiles.shape, jnp.int32),
            pltpu.SemaphoreType.DMA((tiles.shape[0],)),
        ],
        compiler_params=pltpu.CompilerParams(vmem_limit_bytes=LEVELS),
        cost_estimate=cost(0, 12 << 20),
    )(used, tiles)


def join_kernel(sizes, *refs):
    parts, outs = list(refs[: sum(sizes)]), refs[-len(sizes) :]
    for out in outs:
        for n in range(out.shape[0]):
            part = parts.pop(0)
            out[n] = part[0] if len(part.shape) == 3 else part[...]


def join(parts, sizes, afters):
    piece = parts[0].shape[-2:]
    return list(
        pl.pallas_call(
            functools.partial(join_kernel, sizes),
            out_shape=[shape((size, *piece), bf16) for size in sizes],
            in_specs=[VMEM] * len(parts) + [ANY] * len(afters),
            out_specs=[VMEM] * len(sizes),
            compiler_params=pltpu.CompilerParams(vmem_limit_bytes=SMALL),
            cost_estimate=cost(0, 1 << 20),
        )(*parts, *afters)
    )


def marg_table(pieces, owners, part, size):
    table = jnp.zeros((MARG_ROWS, size), f32)
    for piece, owner in zip(pieces, owners):
        tail = piece[piece.shape[0] - MARG_ROWS :, :MARG_LANES]
        k = lax.broadcasted_iota(jnp.int32, (MARG_LANES, size), 0)
        at = lax.broadcasted_iota(jnp.int32, (MARG_LANES, size), 1)
        place = ((at == k + owner * part) & (k < part)).astype(bf16)
        table += jnp.dot(tail, place, preferred_element_type=f32)
    return table


def work_kernel(first, n_sides, n_row, n_col, row_owner, col_owner, *refs):
    refs = list(refs)

    def take(n):
        return [refs.pop(0) for _ in range(n)]

    listing, used, logs, weights = take(4)
    sides, col_in = take(n_sides), take(n_col)
    row_in = [side.at[n] for side in sides for n in range(side.shape[0])]
    if not first:
        left, right = take(2)
    keep, swap = take(2)
    col_out = take(n_col)
    if first:
        left, right = take(2)
    row_panel, row_turned, col_panel, grad_row, grad_turned, grad_col, even, odd = take(8)

    row_blocks, size, width = row_panel.shape
    col_blocks = col_panel.shape[0]
    row_part, col_part = size // n_row, size // n_col
    half = n_row // 2
    me_row, me_col = lax.axis_index("row"), lax.axis_index("col")
    row_owners = [me_col ^ k for k in row_owner]
    col_owners = [me_row ^ k for k in col_owner]
    row_zero, col_zero = me_row * row_blocks, me_col * col_blocks
    count = used[0]

    for pieces, owners, panel, part in (
        (row_in, row_owners, row_panel, row_part),
        (col_in, col_owners, col_panel, col_part),
    ):
        for piece, owner in zip(pieces, owners):
            start = pl.multiple_of(owner * part, part)
            for b in range(panel.shape[0]):
                panel[b, pl.ds(start, part), :] = piece[b * part : (b + 1) * part, :]

    if first:
        row_table = marg_table(row_in, row_owners, row_part, size).astype(bf16)
        for b in range(row_blocks):
            pick = (lax.broadcasted_iota(jnp.int32, (MARG_ROWS, 128), 0) == b).astype(bf16)
            left[b] = lax.dot_general(
                row_table, pick, (((0,), (0,)), ((), ())), preferred_element_type=f32
            )
        col_table = marg_table(col_in, col_owners, col_part, size)
        for b in range(col_blocks):
            right[b] = jnp.broadcast_to(col_table[b : b + 1, :], right.shape[1:])

    chunks = [slice(at, at + 128) for at in range(0, size, 128)]

    def place(slot):
        return listing[0, slot] - row_zero, listing[1, slot] - col_zero

    def make_signal(slot, rows, signal):
        i, j = place(slot)
        scores = lax.dot_general(
            row_panel[i, rows, :], col_panel[j], (((1,), (1,)), ((), ())), preferred_element_type=f32
        )
        marg_left = jnp.concatenate([left[i, rows, :]] * (size // 128), axis=1)
        diff = (scores + marg_left + right[j, 0:1, :] - logs[slot, rows, :]).astype(bf16)
        weight = weights[slot, rows, :]
        half_one = jnp.asarray(0.5, bf16)
        flat = half_one * jnp.tanh(half_one * diff) + half_one
        signal[rows, :] = jnp.where(weight > 0, weight * diff, flat)

    def add_row(slot, rows, signal):
        i, j = place(slot)
        grad_row[i, rows, :] += jnp.dot(signal[rows, :], col_panel[j], preferred_element_type=f32)

    def add_col(slot, signal):
        i, j = place(slot)
        grad_turned[j] += jnp.dot(row_turned[i], signal[...], preferred_element_type=f32)

    def step(slot, before, now):
        for rows in chunks:
            make_signal(slot, rows, now)
            add_row(slot - 1, rows, before)
        add_col(slot - 1, before)

    pairs = (count - 1) // 2

    def pair(n, carry):
        step(2 * n + 1, even, odd)
        step(2 * n + 2, odd, even)
        return carry

    for rows in chunks:
        make_signal(0, rows, even)
    for b in range(row_blocks):
        row_turned[b] = row_panel[b].T
    grad_row[...] = jnp.zeros_like(grad_row)
    grad_turned[...] = jnp.zeros_like(grad_turned)
    lax.fori_loop(0, pairs, pair, 0)

    @pl.when(2 * pairs + 1 < count)
    def _():
        step(2 * pairs + 1, even, odd)

    for parity, signal in enumerate((even, odd)):

        @pl.when(lax.rem(count - 1, 2) == parity)
        def _():
            for rows in chunks:
                add_row(count - 1, rows, signal)
            add_col(count - 1, signal)

    for n in range(n_row):
        place, sibling = row_owner[n] >> 1, row_owner[n] & 1
        start = pl.multiple_of(row_owners[n] * row_part, row_part)
        piece = grad_row[:, pl.ds(start, row_part), :]
        if sibling:
            swap[place] = piece.astype(bf16)
        else:
            keep[place] = piece
    for b in range(col_blocks):
        grad_col[b] = grad_turned[b].astype(bf16).T
    for n in range(n_col):
        start = pl.multiple_of(col_owners[n] * col_part, col_part)
        col_out[n][...] = grad_col[:, pl.ds(start, col_part), :]


def work(listing, used, tabs, row_in, col_in, tables, row_owner, col_owner, dims):
    row_blocks, col_blocks, size, width = dims
    first = tables is None
    n_row, n_col = len(row_owner), len(col_owner)
    row_part, col_part = size // n_row, size // n_col
    half = n_row // 2
    outs = [
        shape((half, row_blocks, row_part, width), f32),
        shape((half, row_blocks, row_part, width), bf16),
    ] + [shape((col_blocks, col_part, width), bf16)] * n_col
    if first:
        outs += [shape((row_blocks, size, 128), f32), shape((col_blocks, 8, size), f32)]
    args = [listing, used, *tabs, *row_in, *col_in] + ([] if first else list(tables))
    res = pl.pallas_call(
        functools.partial(work_kernel, first, len(row_in), n_row, n_col, row_owner, col_owner),
        out_shape=outs,
        in_specs=[SMEM, SMEM] + [VMEM] * (len(args) - 2),
        out_specs=[VMEM] * len(outs),
        scratch_shapes=[
            pltpu.VMEM((row_blocks, size, width), bf16),
            pltpu.VMEM((row_blocks, width, size), bf16),
            pltpu.VMEM((col_blocks, size, width), bf16),
            pltpu.VMEM((row_blocks, size, width), f32),
            pltpu.VMEM((col_blocks, width, size), f32),
            pltpu.VMEM((col_blocks, size, width), bf16),
            pltpu.VMEM((size, size), bf16),
            pltpu.VMEM((size, size), bf16),
        ],
        compiler_params=pltpu.CompilerParams(vmem_limit_bytes=LARGE),
        cost_estimate=cost(8 * 6 * size * size * width, 16 << 20),
    )(*args)
    return res[0], res[1], res[2 : 2 + n_col], res[2 + n_col :]


def merge_kernel(n_held, keep, got, *refs):
    held, outs = refs[:n_held], refs[n_held:]
    for n in range(keep.shape[0]):
        outs[n][...] = (keep[n] + got[n].astype(f32)).astype(outs[n].dtype)
    for src, out in zip(held, outs[keep.shape[0] :]):
        out[...] = src[...]


def merge(keep, got, kept, held):
    n, *piece = keep.shape
    outs = [shape(tuple(piece), f32 if k in kept else bf16) for k in range(n)]
    outs += [shape(x.shape, x.dtype) for x in held]
    return pl.pallas_call(
        functools.partial(merge_kernel, len(held)),
        out_shape=outs,
        in_specs=[VMEM] * (2 + len(held)),
        out_specs=[VMEM] * len(outs),
        compiler_params=pltpu.CompilerParams(vmem_limit_bytes=SMALL),
        cost_estimate=cost(0, 2 << 20),
    )(keep, got, *held)


def add_kernel(n_parts, n_held, own, *refs):
    parts, held, outs = refs[:n_parts], refs[n_parts : n_parts + n_held], refs[n_parts + n_held :]
    total = own[...]
    for part in parts:
        total += part[...].astype(f32)
    outs[0][...] = total.astype(bf16)
    for src, out in zip(held, outs[1:]):
        out[...] = src[...]


def add(own, parts, held):
    return pl.pallas_call(
        functools.partial(add_kernel, len(parts), len(held)),
        out_shape=[shape(own.shape, bf16)] + [shape(x.shape, x.dtype) for x in held],
        in_specs=[VMEM] * (1 + len(parts) + len(held)),
        out_specs=[VMEM] * (1 + len(held)),
        compiler_params=pltpu.CompilerParams(vmem_limit_bytes=SMALL),
        cost_estimate=cost(0, 1 << 20),
    )(own, *parts, *held)


def update_kernel(n_parts, n_outs, emb, *refs):
    parts, outs = refs[:n_parts], refs[-n_outs:]
    total = parts[0][...].astype(f32)
    for part in parts[1:]:
        total += part[...].astype(f32)
    new = emb[...] - RATE * total
    outs[0][...] = new
    if len(outs) > 1:
        outs[1][...] = new.astype(bf16).reshape(outs[1].shape)


def update(emb, parts, afters, last):
    blocks, part, width = emb.shape
    outs = [shape(emb.shape, f32)]
    if not last:
        outs.append(shape((blocks * part, width), bf16))
    res = pl.pallas_call(
        functools.partial(update_kernel, len(parts), len(outs)),
        out_shape=outs,
        in_specs=[VMEM] * (1 + len(parts)) + [ANY] * len(afters),
        out_specs=[VMEM] * len(outs),
        compiler_params=pltpu.CompilerParams(vmem_limit_bytes=SMALL),
        cost_estimate=cost(0, 1 << 20),
    )(emb, *parts, *afters)
    return res if not last else (res[0], None)


def send(x, axis, count, mask):
    return lax.ppermute(x, axis, [(k, k ^ mask) for k in range(count)])


def shards(n_row_dev, n_col_dev, row_emb, col_emb, row_marg, col_marg, tile_list, tile_count, tile_data):
    listing = tile_list[0, 0].T
    used = tile_count[0]
    tiles = tile_data[0, 0]
    dims = (row_emb.shape[0], col_emb.shape[0], tiles.shape[-1], row_emb.shape[-1])
    half = n_col_dev // 2
    far = half // 2
    near = range(1, far)
    row_owner = [2 * k for k in range(half)] + [2 * k + 1 for k in range(half)]
    col_owner = list(range(n_row_dev))

    def hop(x, distance):
        return send(x, "col", n_col_dev, 2 * distance)

    row_pay, col_pay = pack(row_emb, row_marg, col_emb, col_marg)
    *tabs, tabs_made = levels(used, tiles)
    tables = None
    for substep in range(2):
        crossed = hop(row_pay, far)
        col_in = [col_pay] + [send(col_pay, "row", n_row_dev, k) for k in col_owner[1:]]
        if substep == 0:
            before_leg, before_swap, sizes = [tabs_made], col_in[1:-1], [1, far - 1, 1, far - 1]
        else:
            before_leg, before_swap, sizes = col_in[-1:], [], [far, 1, far - 1]
        (crossed,) = join([crossed], [1], before_leg)
        row_in = [row_pay] + [hop(row_pay, k) for k in near] + [crossed] + [hop(crossed, k) for k in near]
        row_in = join(row_in, sizes, before_swap)
        row_in += [send(piece, "col", n_col_dev, 1) for piece in row_in]
        keep, swap, col_out, made = work(
            listing, used, tabs, row_in, col_in, tables, row_owner, col_owner, dims
        )
        tables = tables or made
        held = col_out[-1:] if substep == 1 else []
        merged = merge(keep, send(swap, "col", n_col_dev, 1), (0, far), held)
        col_out = [*col_out[: len(col_out) - len(held)], *merged[half:]]
        relays = [hop(merged[far + k], k) for k in near]
        crossing, *straight = add(merged[far], relays, [merged[k] for k in near])
        col_parts = [col_out[0]] + [send(col_out[k], "row", n_row_dev, k) for k in col_owner[1:]]
        row_parts = [merged[0]] + [hop(x, k) for x, k in zip(straight, near)] + [hop(crossing, far)]
        col_emb, col_pay = update(col_emb, col_parts, [straight[0]], substep == 1)
        row_emb, row_pay = update(row_emb, row_parts, [col_pay if substep == 0 else straight[0]], substep == 1)
    return (row_emb, col_emb)


def solution(mesh):
    placed = (
        P("row", "col", None),
        P("col", "row", None),
        P("row", "col"),
        P("col", "row"),
        P("row", "col", None, None),
        P("row", "col"),
        P("row", "col", None, None, None),
    )
    return jax.shard_map(
        functools.partial(shards, mesh.shape["row"], mesh.shape["col"]),
        mesh=mesh,
        in_specs=placed,
        out_specs=(P("row", "col", None), P("col", "row", None)),
        check_vma=False,
    )
```

```python
import functools

import jax
import jax.numpy as jnp
from jax import lax
from jax.experimental import pallas as pl
from jax.experimental.pallas import tpu as pltpu
from jax.sharding import PartitionSpec as P

RATE = 0.0004
MARG_ROWS = 16
MARG_LANES = 128
ANY = pl.BlockSpec(memory_space=pl.ANY)
HBM = pl.BlockSpec(memory_space=pltpu.HBM)
VMEM = pl.BlockSpec(memory_space=pltpu.VMEM)
SMEM = pl.BlockSpec(memory_space=pltpu.SMEM)
SMALL = 12 << 20
LARGE = 16 << 20
LEVELS = 35 << 20
PACK = 62 << 20
f32, bf16 = jnp.float32, jnp.bfloat16
shape = jax.ShapeDtypeStruct


def cost(flops, moved):
    return pl.CostEstimate(flops=flops, bytes_accessed=moved, transcendentals=0)


def pack_kernel(row_emb, row_marg, col_emb, col_marg, row_out, col_out, *scratch):
    bufs, sem = scratch[:4], scratch[4]
    copies = [
        pltpu.make_async_copy(src, dst, sem.at[n])
        for n, (src, dst) in enumerate(zip((row_emb, row_marg, col_emb, col_marg), bufs))
    ]
    for copy in copies:
        copy.start()
    for n, out in enumerate((row_out, col_out)):
        copies[2 * n].wait()
        copies[2 * n + 1].wait()
        emb, marg = bufs[2 * n], bufs[2 * n + 1]
        blocks, part, width = emb.shape
        out[: blocks * part, :] = emb[...].astype(bf16).reshape(blocks * part, width)
        out[blocks * part :, :] = jnp.zeros((MARG_ROWS, width), bf16)
        for b in range(blocks):
            out[blocks * part + b : blocks * part + b + 1, :part] = marg[b : b + 1, :]


def pack(row_emb, row_marg, col_emb, col_marg):
    args = (row_emb, row_marg, col_emb, col_marg)
    return pl.pallas_call(
        pack_kernel,
        out_shape=[
            shape((e.shape[0] * e.shape[1] + MARG_ROWS, e.shape[2]), bf16) for e in args[::2]
        ],
        in_specs=[ANY] * 4,
        out_specs=[VMEM] * 2,
        scratch_shapes=[pltpu.VMEM(x.shape, x.dtype) for x in args]
        + [pltpu.SemaphoreType.DMA((4,))],
        compiler_params=pltpu.CompilerParams(vmem_limit_bytes=PACK),
        cost_estimate=cost(0, 1 << 20),
    )(*args)


def levels_kernel(used, tiles, logs, weights, token, tile_buf, sem):
    slots, size, _ = tile_buf.shape
    count = used[0]
    chunk = 64

    def load(slot):
        return pltpu.make_async_copy(tiles.at[slot], tile_buf.at[slot], sem.at[slot])

    for slot in range(slots):

        @pl.when(slot < count)
        def _():
            load(slot).start()

    token[...] = jnp.zeros_like(token)

    def one_tile(slot, carry):
        load(slot).wait()

        def one_chunk(n, carry):
            rows = pl.ds(pl.multiple_of(n * chunk, chunk), chunk)
            counts = tile_buf[slot, rows, :].astype(f32)
            level = jnp.maximum(counts, 1.0)
            logs[slot, rows, :] = jnp.log(level)
            weight = 0.1 + 0.25 * (level * lax.rsqrt(level))
            weights[slot, rows, :] = jnp.where(counts > 0.0, weight, 0.0).astype(bf16)
            return carry

        lax.fori_loop(0, size // chunk, one_chunk, 0)
        return carry

    lax.fori_loop(0, count, one_tile, 0)


def levels(used, tiles):
    return pl.pallas_call(
        levels_kernel,
        out_shape=[shape(tiles.shape, f32), shape(tiles.shape, bf16), shape((8, 128), f32)],
        in_specs=[SMEM, HBM],
        out_specs=[VMEM] * 3,
        scratch_shapes=[
            pltpu.VMEM(tiles.shape, jnp.int32),
            pltpu.SemaphoreType.DMA((tiles.shape[0],)),
        ],
        compiler_params=pltpu.CompilerParams(vmem_limit_bytes=LEVELS),
        cost_estimate=cost(0, 12 << 20),
    )(used, tiles)


def join_kernel(sizes, *refs):
    parts, outs = list(refs[: sum(sizes)]), refs[-len(sizes) :]
    for out in outs:
        for n in range(out.shape[0]):
            part = parts.pop(0)
            out[n] = part[0] if len(part.shape) == 3 else part[...]


def join(parts, sizes, afters):
    piece = parts[0].shape[-2:]
    return list(
        pl.pallas_call(
            functools.partial(join_kernel, sizes),
            out_shape=[shape((size, *piece), bf16) for size in sizes],
            in_specs=[VMEM] * len(parts) + [ANY] * len(afters),
            out_specs=[VMEM] * len(sizes),
            compiler_params=pltpu.CompilerParams(vmem_limit_bytes=SMALL),
            cost_estimate=cost(0, 1 << 20),
        )(*parts, *afters)
    )


def marg_table(pieces, owners, part, size):
    table = jnp.zeros((MARG_ROWS, size), f32)
    for piece, owner in zip(pieces, owners):
        tail = piece[piece.shape[0] - MARG_ROWS :, :MARG_LANES]
        k = lax.broadcasted_iota(jnp.int32, (MARG_LANES, size), 0)
        at = lax.broadcasted_iota(jnp.int32, (MARG_LANES, size), 1)
        place = ((at == k + owner * part) & (k < part)).astype(bf16)
        table += jnp.dot(tail, place, preferred_element_type=f32)
    return table


def work_kernel(first, n_sides, n_row, n_col, row_owner, col_owner, *refs):
    refs = list(refs)

    def take(n):
        return [refs.pop(0) for _ in range(n)]

    listing, used, logs, weights = take(4)
    sides, col_in = take(n_sides), take(n_col)
    row_in = [side.at[n] for side in sides for n in range(side.shape[0])]
    if not first:
        left, right = take(2)
    keep, swap = take(2)
    col_out = take(n_col)
    if first:
        left, right = take(2)
    row_panel, row_turned, col_panel, grad_row, grad_turned, grad_col, even, odd = take(8)

    row_blocks, size, width = row_panel.shape
    col_blocks = col_panel.shape[0]
    row_part, col_part = size // n_row, size // n_col
    half = n_row // 2
    me_row, me_col = lax.axis_index("row"), lax.axis_index("col")
    row_owners = [me_col ^ k for k in row_owner]
    col_owners = [me_row ^ k for k in col_owner]
    row_zero, col_zero = me_row * row_blocks, me_col * col_blocks
    count = used[0]

    for pieces, owners, panel, part in (
        (row_in, row_owners, row_panel, row_part),
        (col_in, col_owners, col_panel, col_part),
    ):
        for piece, owner in zip(pieces, owners):
            start = pl.multiple_of(owner * part, part)
            for b in range(panel.shape[0]):
                panel[b, pl.ds(start, part), :] = piece[b * part : (b + 1) * part, :]

    if first:
        row_table = marg_table(row_in, row_owners, row_part, size).astype(bf16)
        for b in range(row_blocks):
            pick = (lax.broadcasted_iota(jnp.int32, (MARG_ROWS, 128), 0) == b).astype(bf16)
            left[b] = lax.dot_general(
                row_table, pick, (((0,), (0,)), ((), ())), preferred_element_type=f32
            )
        col_table = marg_table(col_in, col_owners, col_part, size)
        for b in range(col_blocks):
            right[b] = jnp.broadcast_to(col_table[b : b + 1, :], right.shape[1:])

    chunks = [slice(at, at + 256) for at in range(0, size, 256)]

    def place(slot):
        return listing[0, slot] - row_zero, listing[1, slot] - col_zero

    def make_signal(slot, rows, signal):
        i, j = place(slot)
        scores = lax.dot_general(
            row_panel[i, rows, :], col_panel[j], (((1,), (1,)), ((), ())), preferred_element_type=f32
        )
        marg_left = jnp.concatenate([left[i, rows, :]] * (size // 128), axis=1)
        diff = (scores + marg_left + right[j, 0:1, :] - logs[slot, rows, :]).astype(bf16)
        weight = weights[slot, rows, :]
        half_one = jnp.asarray(0.5, bf16)
        flat = half_one * jnp.tanh(half_one * diff) + half_one
        signal[rows, :] = jnp.where(weight > 0, weight * diff, flat)

    def add_row(slot, rows, signal):
        i, j = place(slot)
        grad_row[i, rows, :] += jnp.dot(signal[rows, :], col_panel[j], preferred_element_type=f32)

    def add_col(slot, signal):
        i, j = place(slot)
        grad_turned[j] += jnp.dot(row_turned[i], signal[...], preferred_element_type=f32)

    def step(slot, before, now):
        for n, rows in enumerate(chunks):
            make_signal(slot, rows, now)
            if n == 0:
                add_row(slot - 1, slice(0, size), before)
        add_col(slot - 1, before)

    pairs = (count - 1) // 2

    def pair(n, carry):
        step(2 * n + 1, even, odd)
        step(2 * n + 2, odd, even)
        return carry

    for rows in chunks:
        make_signal(0, rows, even)
    for b in range(row_blocks):
        row_turned[b] = row_panel[b].T
    grad_row[...] = jnp.zeros_like(grad_row)
    grad_turned[...] = jnp.zeros_like(grad_turned)
    lax.fori_loop(0, pairs, pair, 0)

    @pl.when(2 * pairs + 1 < count)
    def _():
        step(2 * pairs + 1, even, odd)

    for parity, signal in enumerate((even, odd)):

        @pl.when(lax.rem(count - 1, 2) == parity)
        def _():
            for rows in chunks:
                add_row(count - 1, rows, signal)
            add_col(count - 1, signal)

    for n in range(n_row):
        place, sibling = row_owner[n] >> 1, row_owner[n] & 1
        start = pl.multiple_of(row_owners[n] * row_part, row_part)
        piece = grad_row[:, pl.ds(start, row_part), :]
        if sibling:
            swap[place] = piece.astype(bf16)
        else:
            keep[place] = piece
    for b in range(col_blocks):
        grad_col[b] = grad_turned[b].astype(bf16).T
    for n in range(n_col):
        start = pl.multiple_of(col_owners[n] * col_part, col_part)
        col_out[n][...] = grad_col[:, pl.ds(start, col_part), :]


def work(listing, used, tabs, row_in, col_in, tables, row_owner, col_owner, dims):
    row_blocks, col_blocks, size, width = dims
    first = tables is None
    n_row, n_col = len(row_owner), len(col_owner)
    row_part, col_part = size // n_row, size // n_col
    half = n_row // 2
    outs = [
        shape((half, row_blocks, row_part, width), f32),
        shape((half, row_blocks, row_part, width), bf16),
    ] + [shape((col_blocks, col_part, width), bf16)] * n_col
    if first:
        outs += [shape((row_blocks, size, 128), f32), shape((col_blocks, 8, size), f32)]
    args = [listing, used, *tabs, *row_in, *col_in] + ([] if first else list(tables))
    res = pl.pallas_call(
        functools.partial(work_kernel, first, len(row_in), n_row, n_col, row_owner, col_owner),
        out_shape=outs,
        in_specs=[SMEM, SMEM] + [VMEM] * (len(args) - 2),
        out_specs=[VMEM] * len(outs),
        scratch_shapes=[
            pltpu.VMEM((row_blocks, size, width), bf16),
            pltpu.VMEM((row_blocks, width, size), bf16),
            pltpu.VMEM((col_blocks, size, width), bf16),
            pltpu.VMEM((row_blocks, size, width), f32),
            pltpu.VMEM((col_blocks, width, size), f32),
            pltpu.VMEM((col_blocks, size, width), bf16),
            pltpu.VMEM((size, size), bf16),
            pltpu.VMEM((size, size), bf16),
        ],
        compiler_params=pltpu.CompilerParams(vmem_limit_bytes=LARGE),
        cost_estimate=cost(8 * 6 * size * size * width, 16 << 20),
    )(*args)
    return res[0], res[1], res[2 : 2 + n_col], res[2 + n_col :]


def merge_kernel(n_held, keep, got, *refs):
    held, outs = refs[:n_held], refs[n_held:]
    for n in range(keep.shape[0]):
        outs[n][...] = (keep[n] + got[n].astype(f32)).astype(outs[n].dtype)
    for src, out in zip(held, outs[keep.shape[0] :]):
        out[...] = src[...]


def merge(keep, got, kept, held):
    n, *piece = keep.shape
    outs = [shape(tuple(piece), f32 if k in kept else bf16) for k in range(n)]
    outs += [shape(x.shape, x.dtype) for x in held]
    return pl.pallas_call(
        functools.partial(merge_kernel, len(held)),
        out_shape=outs,
        in_specs=[VMEM] * (2 + len(held)),
        out_specs=[VMEM] * len(outs),
        compiler_params=pltpu.CompilerParams(vmem_limit_bytes=SMALL),
        cost_estimate=cost(0, 2 << 20),
    )(keep, got, *held)


def add_kernel(n_parts, n_held, own, *refs):
    parts, held, outs = refs[:n_parts], refs[n_parts : n_parts + n_held], refs[n_parts + n_held :]
    total = own[...]
    for part in parts:
        total += part[...].astype(f32)
    outs[0][...] = total.astype(bf16)
    for src, out in zip(held, outs[1:]):
        out[...] = src[...]


def add(own, parts, held):
    return pl.pallas_call(
        functools.partial(add_kernel, len(parts), len(held)),
        out_shape=[shape(own.shape, bf16)] + [shape(x.shape, x.dtype) for x in held],
        in_specs=[VMEM] * (1 + len(parts) + len(held)),
        out_specs=[VMEM] * (1 + len(held)),
        compiler_params=pltpu.CompilerParams(vmem_limit_bytes=SMALL),
        cost_estimate=cost(0, 1 << 20),
    )(own, *parts, *held)


def update_kernel(n_parts, n_outs, emb, *refs):
    parts, outs = refs[:n_parts], refs[-n_outs:]
    total = parts[0][...].astype(f32)
    for part in parts[1:]:
        total += part[...].astype(f32)
    new = emb[...] - RATE * total
    outs[0][...] = new
    if len(outs) > 1:
        outs[1][...] = new.astype(bf16).reshape(outs[1].shape)


def update(emb, parts, afters, last):
    blocks, part, width = emb.shape
    outs = [shape(emb.shape, f32)]
    if not last:
        outs.append(shape((blocks * part, width), bf16))
    res = pl.pallas_call(
        functools.partial(update_kernel, len(parts), len(outs)),
        out_shape=outs,
        in_specs=[VMEM] * (1 + len(parts)) + [ANY] * len(afters),
        out_specs=[VMEM] * len(outs),
        compiler_params=pltpu.CompilerParams(vmem_limit_bytes=SMALL),
        cost_estimate=cost(0, 1 << 20),
    )(emb, *parts, *afters)
    return res if not last else (res[0], None)


def send(x, axis, count, mask):
    return lax.ppermute(x, axis, [(k, k ^ mask) for k in range(count)])


def shards(n_row_dev, n_col_dev, row_emb, col_emb, row_marg, col_marg, tile_list, tile_count, tile_data):
    listing = tile_list[0, 0].T
    used = tile_count[0]
    tiles = tile_data[0, 0]
    dims = (row_emb.shape[0], col_emb.shape[0], tiles.shape[-1], row_emb.shape[-1])
    half = n_col_dev // 2
    far = half // 2
    near = range(1, far)
    row_owner = [2 * k for k in range(half)] + [2 * k + 1 for k in range(half)]
    col_owner = list(range(n_row_dev))

    def hop(x, distance):
        return send(x, "col", n_col_dev, 2 * distance)

    row_pay, col_pay = pack(row_emb, row_marg, col_emb, col_marg)
    *tabs, tabs_made = levels(used, tiles)
    tables = None
    for substep in range(2):
        crossed = hop(row_pay, far)
        col_in = [col_pay] + [send(col_pay, "row", n_row_dev, k) for k in col_owner[1:]]
        if substep == 0:
            before_leg, before_swap, sizes = [tabs_made], col_in[1:-1], [1, far - 1, 1, far - 1]
        else:
            before_leg, before_swap, sizes = col_in[-1:], [], [far, 1, far - 1]
        (crossed,) = join([crossed], [1], before_leg)
        row_in = [row_pay] + [hop(row_pay, k) for k in near] + [crossed] + [hop(crossed, k) for k in near]
        row_in = join(row_in, sizes, before_swap)
        row_in += [send(piece, "col", n_col_dev, 1) for piece in row_in]
        keep, swap, col_out, made = work(
            listing, used, tabs, row_in, col_in, tables, row_owner, col_owner, dims
        )
        tables = tables or made
        held = col_out[-1:] if substep == 1 else []
        merged = merge(keep, send(swap, "col", n_col_dev, 1), (0, far), held)
        col_out = [*col_out[: len(col_out) - len(held)], *merged[half:]]
        relays = [hop(merged[far + k], k) for k in near]
        crossing, *straight = add(merged[far], relays, [merged[k] for k in near])
        col_parts = [col_out[0]] + [send(col_out[k], "row", n_row_dev, k) for k in col_owner[1:]]
        row_parts = [merged[0]] + [hop(x, k) for x, k in zip(straight, near)] + [hop(crossing, far)]
        col_emb, col_pay = update(col_emb, col_parts, [straight[0]], substep == 1)
        row_emb, row_pay = update(row_emb, row_parts, [col_pay if substep == 0 else straight[0]], substep == 1)
    return (row_emb, col_emb)


def solution(mesh):
    placed = (
        P("row", "col", None),
        P("col", "row", None),
        P("row", "col"),
        P("col", "row"),
        P("row", "col", None, None),
        P("row", "col"),
        P("row", "col", None, None, None),
    )
    return jax.shard_map(
        functools.partial(shards, mesh.shape["row"], mesh.shape["col"]),
        mesh=mesh,
        in_specs=placed,
        out_specs=(P("row", "col", None), P("col", "row", None)),
        check_vma=False,
    )
```

```python
import functools

import jax
import jax.numpy as jnp
from jax import lax
from jax.experimental import pallas as pl
from jax.experimental.pallas import tpu as pltpu
from jax.sharding import PartitionSpec as P

RATE = 0.0004
MARG_ROWS = 16
MARG_LANES = 128
ANY = pl.BlockSpec(memory_space=pl.ANY)
HBM = pl.BlockSpec(memory_space=pltpu.HBM)
VMEM = pl.BlockSpec(memory_space=pltpu.VMEM)
SMEM = pl.BlockSpec(memory_space=pltpu.SMEM)
SMALL = 12 << 20
LARGE = 16 << 20
LEVELS = 35 << 20
PACK = 62 << 20
f32, bf16 = jnp.float32, jnp.bfloat16
shape = jax.ShapeDtypeStruct


def cost(flops, moved):
    return pl.CostEstimate(flops=flops, bytes_accessed=moved, transcendentals=0)


def pack_kernel(row_emb, row_marg, col_emb, col_marg, row_out, col_out, *scratch):
    bufs, sem = scratch[:4], scratch[4]
    copies = [
        pltpu.make_async_copy(src, dst, sem.at[n])
        for n, (src, dst) in enumerate(zip((row_emb, row_marg, col_emb, col_marg), bufs))
    ]
    for copy in copies:
        copy.start()
    for n, out in enumerate((row_out, col_out)):
        copies[2 * n].wait()
        copies[2 * n + 1].wait()
        emb, marg = bufs[2 * n], bufs[2 * n + 1]
        blocks, part, width = emb.shape
        out[: blocks * part, :] = emb[...].astype(bf16).reshape(blocks * part, width)
        out[blocks * part :, :] = jnp.zeros((MARG_ROWS, width), bf16)
        for b in range(blocks):
            out[blocks * part + b : blocks * part + b + 1, :part] = marg[b : b + 1, :]


def pack(row_emb, row_marg, col_emb, col_marg):
    args = (row_emb, row_marg, col_emb, col_marg)
    return pl.pallas_call(
        pack_kernel,
        out_shape=[
            shape((e.shape[0] * e.shape[1] + MARG_ROWS, e.shape[2]), bf16) for e in args[::2]
        ],
        in_specs=[ANY] * 4,
        out_specs=[VMEM] * 2,
        scratch_shapes=[pltpu.VMEM(x.shape, x.dtype) for x in args]
        + [pltpu.SemaphoreType.DMA((4,))],
        compiler_params=pltpu.CompilerParams(vmem_limit_bytes=PACK),
        cost_estimate=cost(0, 1 << 20),
    )(*args)


def levels_kernel(used, tiles, logs, weights, token, tile_buf, sem):
    slots, size, _ = tile_buf.shape
    count = used[0]
    chunk = 64

    def load(slot):
        return pltpu.make_async_copy(tiles.at[slot], tile_buf.at[slot], sem.at[slot])

    for slot in range(slots):

        @pl.when(slot < count)
        def _():
            load(slot).start()

    token[...] = jnp.zeros_like(token)

    def one_tile(slot, carry):
        load(slot).wait()

        def one_chunk(n, carry):
            rows = pl.ds(pl.multiple_of(n * chunk, chunk), chunk)
            counts = tile_buf[slot, rows, :].astype(f32)
            level = jnp.maximum(counts, 1.0)
            logs[slot, rows, :] = jnp.log(level)
            weight = 0.1 + 0.25 * (level * lax.rsqrt(level))
            weights[slot, rows, :] = jnp.where(counts > 0.0, weight, 0.0).astype(bf16)
            return carry

        lax.fori_loop(0, size // chunk, one_chunk, 0)
        return carry

    lax.fori_loop(0, count, one_tile, 0)


def levels(used, tiles):
    return pl.pallas_call(
        levels_kernel,
        out_shape=[shape(tiles.shape, f32), shape(tiles.shape, bf16), shape((8, 128), f32)],
        in_specs=[SMEM, HBM],
        out_specs=[VMEM] * 3,
        scratch_shapes=[
            pltpu.VMEM(tiles.shape, jnp.int32),
            pltpu.SemaphoreType.DMA((tiles.shape[0],)),
        ],
        compiler_params=pltpu.CompilerParams(vmem_limit_bytes=LEVELS),
        cost_estimate=cost(0, 12 << 20),
    )(used, tiles)


def join_kernel(sizes, *refs):
    parts, outs = list(refs[: sum(sizes)]), refs[-len(sizes) :]
    for out in outs:
        for n in range(out.shape[0]):
            part = parts.pop(0)
            out[n] = part[0] if len(part.shape) == 3 else part[...]


def join(parts, sizes, afters):
    piece = parts[0].shape[-2:]
    return list(
        pl.pallas_call(
            functools.partial(join_kernel, sizes),
            out_shape=[shape((size, *piece), bf16) for size in sizes],
            in_specs=[VMEM] * len(parts) + [ANY] * len(afters),
            out_specs=[VMEM] * len(sizes),
            compiler_params=pltpu.CompilerParams(vmem_limit_bytes=SMALL),
            cost_estimate=cost(0, 1 << 20),
        )(*parts, *afters)
    )


def marg_table(pieces, owners, part, size):
    table = jnp.zeros((MARG_ROWS, size), f32)
    for piece, owner in zip(pieces, owners):
        tail = piece[piece.shape[0] - MARG_ROWS :, :MARG_LANES]
        k = lax.broadcasted_iota(jnp.int32, (MARG_LANES, size), 0)
        at = lax.broadcasted_iota(jnp.int32, (MARG_LANES, size), 1)
        place = ((at == k + owner * part) & (k < part)).astype(bf16)
        table += jnp.dot(tail, place, preferred_element_type=f32)
    return table


def work_kernel(first, n_sides, n_row, n_col, row_owner, col_owner, *refs):
    refs = list(refs)

    def take(n):
        return [refs.pop(0) for _ in range(n)]

    listing, used, logs, weights = take(4)
    sides, col_in = take(n_sides), take(n_col)
    row_in = [side.at[n] for side in sides for n in range(side.shape[0])]
    if not first:
        left, right = take(2)
    keep, swap = take(2)
    col_out = take(n_col)
    if first:
        left, right = take(2)
    row_panel, row_turned, col_panel, grad_row, grad_turned, grad_col, even, odd = take(8)

    row_blocks, size, width = row_panel.shape
    col_blocks = col_panel.shape[0]
    row_part, col_part = size // n_row, size // n_col
    half = n_row // 2
    me_row, me_col = lax.axis_index("row"), lax.axis_index("col")
    row_owners = [me_col ^ k for k in row_owner]
    col_owners = [me_row ^ k for k in col_owner]
    row_zero, col_zero = me_row * row_blocks, me_col * col_blocks
    count = used[0]

    for pieces, owners, panel, part in (
        (row_in, row_owners, row_panel, row_part),
        (col_in, col_owners, col_panel, col_part),
    ):
        for piece, owner in zip(pieces, owners):
            start = pl.multiple_of(owner * part, part)
            for b in range(panel.shape[0]):
                panel[b, pl.ds(start, part), :] = piece[b * part : (b + 1) * part, :]

    if first:
        row_table = marg_table(row_in, row_owners, row_part, size).astype(bf16)
        for b in range(row_blocks):
            pick = (lax.broadcasted_iota(jnp.int32, (MARG_ROWS, 128), 0) == b).astype(bf16)
            left[b] = lax.dot_general(
                row_table, pick, (((0,), (0,)), ((), ())), preferred_element_type=f32
            )
        col_table = marg_table(col_in, col_owners, col_part, size)
        for b in range(col_blocks):
            right[b] = jnp.broadcast_to(col_table[b : b + 1, :], right.shape[1:])

    chunks = [slice(at, at + 256) for at in range(0, size, 256)]

    def place(slot):
        return listing[0, slot] - row_zero, listing[1, slot] - col_zero

    def make_signal(slot, rows, signal):
        i, j = place(slot)
        scores = lax.dot_general(
            row_panel[i, rows, :], col_panel[j], (((1,), (1,)), ((), ())), preferred_element_type=f32
        )
        marg_left = jnp.concatenate([left[i, rows, :]] * (size // 128), axis=1)
        diff = (scores + marg_left + right[j, 0:1, :] - logs[slot, rows, :]).astype(bf16)
        weight = weights[slot, rows, :]
        half_one = jnp.asarray(0.5, bf16)
        flat = half_one * jnp.tanh(half_one * diff) + half_one
        signal[rows, :] = jnp.where(weight > 0, weight * diff, flat)

    def add_row(slot, rows, signal):
        i, j = place(slot)
        grad_row[i, rows, :] += jnp.dot(signal[rows, :], col_panel[j], preferred_element_type=f32)

    def add_col(slot, signal):
        i, j = place(slot)
        grad_turned[j] += jnp.dot(row_turned[i], signal[...], preferred_element_type=f32)

    def step(slot, before, now):
        for rows in chunks:
            make_signal(slot, rows, now)
            add_row(slot - 1, rows, before)
        add_col(slot - 1, before)

    pairs = (count - 1) // 2

    def pair(n, carry):
        step(2 * n + 1, even, odd)
        step(2 * n + 2, odd, even)
        return carry

    for rows in chunks:
        make_signal(0, rows, even)
    for b in range(row_blocks):
        row_turned[b] = row_panel[b].T
    grad_row[...] = jnp.zeros_like(grad_row)
    grad_turned[...] = jnp.zeros_like(grad_turned)
    lax.fori_loop(0, pairs, pair, 0)

    @pl.when(2 * pairs + 1 < count)
    def _():
        step(2 * pairs + 1, even, odd)

    for parity, signal in enumerate((even, odd)):

        @pl.when(lax.rem(count - 1, 2) == parity)
        def _():
            for rows in chunks:
                add_row(count - 1, rows, signal)
            add_col(count - 1, signal)

    for n in range(n_row):
        place, sibling = row_owner[n] >> 1, row_owner[n] & 1
        start = pl.multiple_of(row_owners[n] * row_part, row_part)
        piece = grad_row[:, pl.ds(start, row_part), :]
        if sibling:
            swap[place] = piece.astype(bf16)
        else:
            keep[place] = piece
    aligned = col_part % 128 == 0
    if not aligned:
        for b in range(col_blocks):
            grad_col[b] = grad_turned[b].astype(bf16).T
    for n in range(n_col):
        start = pl.multiple_of(col_owners[n] * col_part, col_part)
        if aligned:
            for b in range(col_blocks):
                col_out[n][b] = grad_turned[b, :, pl.ds(start, col_part)].astype(bf16).T
        else:
            col_out[n][...] = grad_col[:, pl.ds(start, col_part), :]


def work(listing, used, tabs, row_in, col_in, tables, row_owner, col_owner, dims):
    row_blocks, col_blocks, size, width = dims
    first = tables is None
    n_row, n_col = len(row_owner), len(col_owner)
    row_part, col_part = size // n_row, size // n_col
    half = n_row // 2
    outs = [
        shape((half, row_blocks, row_part, width), f32),
        shape((half, row_blocks, row_part, width), bf16),
    ] + [shape((col_blocks, col_part, width), bf16)] * n_col
    if first:
        outs += [shape((row_blocks, size, 128), f32), shape((col_blocks, 8, size), f32)]
    args = [listing, used, *tabs, *row_in, *col_in] + ([] if first else list(tables))
    res = pl.pallas_call(
        functools.partial(work_kernel, first, len(row_in), n_row, n_col, row_owner, col_owner),
        out_shape=outs,
        in_specs=[SMEM, SMEM] + [VMEM] * (len(args) - 2),
        out_specs=[VMEM] * len(outs),
        scratch_shapes=[
            pltpu.VMEM((row_blocks, size, width), bf16),
            pltpu.VMEM((row_blocks, width, size), bf16),
            pltpu.VMEM((col_blocks, size, width), bf16),
            pltpu.VMEM((row_blocks, size, width), f32),
            pltpu.VMEM((col_blocks, width, size), f32),
            pltpu.VMEM((col_blocks, size, width), bf16),
            pltpu.VMEM((size, size), bf16),
            pltpu.VMEM((size, size), bf16),
        ],
        compiler_params=pltpu.CompilerParams(vmem_limit_bytes=LARGE),
        cost_estimate=cost(8 * 6 * size * size * width, 16 << 20),
    )(*args)
    return res[0], res[1], res[2 : 2 + n_col], res[2 + n_col :]


def merge_kernel(n_held, keep, got, *refs):
    held, outs = refs[:n_held], refs[n_held:]
    for n in range(keep.shape[0]):
        outs[n][...] = (keep[n] + got[n].astype(f32)).astype(outs[n].dtype)
    for src, out in zip(held, outs[keep.shape[0] :]):
        out[...] = src[...]


def merge(keep, got, kept, held):
    n, *piece = keep.shape
    outs = [shape(tuple(piece), f32 if k in kept else bf16) for k in range(n)]
    outs += [shape(x.shape, x.dtype) for x in held]
    return pl.pallas_call(
        functools.partial(merge_kernel, len(held)),
        out_shape=outs,
        in_specs=[VMEM] * (2 + len(held)),
        out_specs=[VMEM] * len(outs),
        compiler_params=pltpu.CompilerParams(vmem_limit_bytes=SMALL),
        cost_estimate=cost(0, 2 << 20),
    )(keep, got, *held)


def add_kernel(n_parts, n_held, own, *refs):
    parts, held, outs = refs[:n_parts], refs[n_parts : n_parts + n_held], refs[n_parts + n_held :]
    total = own[...]
    for part in parts:
        total += part[...].astype(f32)
    outs[0][...] = total.astype(bf16)
    for src, out in zip(held, outs[1:]):
        out[...] = src[...]


def add(own, parts, held):
    return pl.pallas_call(
        functools.partial(add_kernel, len(parts), len(held)),
        out_shape=[shape(own.shape, bf16)] + [shape(x.shape, x.dtype) for x in held],
        in_specs=[VMEM] * (1 + len(parts) + len(held)),
        out_specs=[VMEM] * (1 + len(held)),
        compiler_params=pltpu.CompilerParams(vmem_limit_bytes=SMALL),
        cost_estimate=cost(0, 1 << 20),
    )(own, *parts, *held)


def update_kernel(n_parts, n_outs, emb, *refs):
    parts, outs = refs[:n_parts], refs[-n_outs:]
    total = parts[0][...].astype(f32)
    for part in parts[1:]:
        total += part[...].astype(f32)
    new = emb[...] - RATE * total
    outs[0][...] = new
    if len(outs) > 1:
        outs[1][...] = new.astype(bf16).reshape(outs[1].shape)


def update(emb, parts, afters, last):
    blocks, part, width = emb.shape
    outs = [shape(emb.shape, f32)]
    if not last:
        outs.append(shape((blocks * part, width), bf16))
    res = pl.pallas_call(
        functools.partial(update_kernel, len(parts), len(outs)),
        out_shape=outs,
        in_specs=[VMEM] * (1 + len(parts)) + [ANY] * len(afters),
        out_specs=[VMEM] * len(outs),
        compiler_params=pltpu.CompilerParams(vmem_limit_bytes=SMALL),
        cost_estimate=cost(0, 1 << 20),
    )(emb, *parts, *afters)
    return res if not last else (res[0], None)


def send(x, axis, count, mask):
    return lax.ppermute(x, axis, [(k, k ^ mask) for k in range(count)])


def shards(n_row_dev, n_col_dev, row_emb, col_emb, row_marg, col_marg, tile_list, tile_count, tile_data):
    listing = tile_list[0, 0].T
    used = tile_count[0]
    tiles = tile_data[0, 0]
    dims = (row_emb.shape[0], col_emb.shape[0], tiles.shape[-1], row_emb.shape[-1])
    half = n_col_dev // 2
    far = half // 2
    near = range(1, far)
    row_owner = [2 * k for k in range(half)] + [2 * k + 1 for k in range(half)]
    col_owner = list(range(n_row_dev))

    def hop(x, distance):
        return send(x, "col", n_col_dev, 2 * distance)

    row_pay, col_pay = pack(row_emb, row_marg, col_emb, col_marg)
    *tabs, tabs_made = levels(used, tiles)
    tables = None
    for substep in range(2):
        crossed = hop(row_pay, far)
        col_in = [col_pay] + [send(col_pay, "row", n_row_dev, k) for k in col_owner[1:]]
        if substep == 0:
            before_leg, before_swap, sizes = [tabs_made], col_in[1:-1], [1, far - 1, 1, far - 1]
        else:
            before_leg, before_swap, sizes = col_in[-1:], [], [far, 1, far - 1]
        (crossed,) = join([crossed], [1], before_leg)
        row_in = [row_pay] + [hop(row_pay, k) for k in near] + [crossed] + [hop(crossed, k) for k in near]
        row_in = join(row_in, sizes, before_swap)
        row_in += [send(piece, "col", n_col_dev, 1) for piece in row_in]
        keep, swap, col_out, made = work(
            listing, used, tabs, row_in, col_in, tables, row_owner, col_owner, dims
        )
        tables = tables or made
        held = col_out[-1:] if substep == 1 else []
        merged = merge(keep, send(swap, "col", n_col_dev, 1), (0, far), held)
        col_out = [*col_out[: len(col_out) - len(held)], *merged[half:]]
        relays = [hop(merged[far + k], k) for k in near]
        crossing, *straight = add(merged[far], relays, [merged[k] for k in near])
        col_parts = [col_out[0]] + [send(col_out[k], "row", n_row_dev, k) for k in col_owner[1:]]
        row_parts = [merged[0]] + [hop(x, k) for x, k in zip(straight, near)] + [hop(crossing, far)]
        col_emb, col_pay = update(col_emb, col_parts, [straight[0]], substep == 1)
        row_emb, row_pay = update(row_emb, row_parts, [col_pay if substep == 0 else straight[0]], substep == 1)
    return (row_emb, col_emb)


def solution(mesh):
    placed = (
        P("row", "col", None),
        P("col", "row", None),
        P("row", "col"),
        P("col", "row"),
        P("row", "col", None, None),
        P("row", "col"),
        P("row", "col", None, None, None),
    )
    return jax.shard_map(
        functools.partial(shards, mesh.shape["row"], mesh.shape["col"]),
        mesh=mesh,
        in_specs=placed,
        out_specs=(P("row", "col", None), P("col", "row", None)),
        check_vma=False,
    )
```

```python
import functools

import jax
import jax.numpy as jnp
from jax import lax
from jax.experimental import pallas as pl
from jax.experimental.pallas import tpu as pltpu
from jax.sharding import PartitionSpec as P

RATE = 0.0004
MARG_ROWS = 16
MARG_LANES = 128
ANY = pl.BlockSpec(memory_space=pl.ANY)
HBM = pl.BlockSpec(memory_space=pltpu.HBM)
VMEM = pl.BlockSpec(memory_space=pltpu.VMEM)
SMEM = pl.BlockSpec(memory_space=pltpu.SMEM)
SMALL = 12 << 20
LARGE = 16 << 20
LEVELS = 35 << 20
PACK = 62 << 20
f32, bf16 = jnp.float32, jnp.bfloat16
shape = jax.ShapeDtypeStruct


def cost(flops, moved):
    return pl.CostEstimate(flops=flops, bytes_accessed=moved, transcendentals=0)


def pack_kernel(row_emb, row_marg, col_emb, col_marg, row_out, col_out, *scratch):
    bufs, sem = scratch[:4], scratch[4]
    copies = [
        pltpu.make_async_copy(src, dst, sem.at[n])
        for n, (src, dst) in enumerate(zip((row_emb, row_marg, col_emb, col_marg), bufs))
    ]
    for copy in copies:
        copy.start()
    for n, out in enumerate((row_out, col_out)):
        copies[2 * n].wait()
        copies[2 * n + 1].wait()
        emb, marg = bufs[2 * n], bufs[2 * n + 1]
        blocks, part, width = emb.shape
        out[: blocks * part, :] = emb[...].astype(bf16).reshape(blocks * part, width)
        out[blocks * part :, :] = jnp.zeros((MARG_ROWS, width), bf16)
        for b in range(blocks):
            out[blocks * part + b : blocks * part + b + 1, :part] = marg[b : b + 1, :]


def pack(row_emb, row_marg, col_emb, col_marg):
    args = (row_emb, row_marg, col_emb, col_marg)
    return pl.pallas_call(
        pack_kernel,
        out_shape=[
            shape((e.shape[0] * e.shape[1] + MARG_ROWS, e.shape[2]), bf16) for e in args[::2]
        ],
        in_specs=[ANY] * 4,
        out_specs=[VMEM] * 2,
        scratch_shapes=[pltpu.VMEM(x.shape, x.dtype) for x in args]
        + [pltpu.SemaphoreType.DMA((4,))],
        compiler_params=pltpu.CompilerParams(vmem_limit_bytes=PACK),
        cost_estimate=cost(0, 1 << 20),
    )(*args)


def levels_kernel(used, tiles, logs, weights, token, tile_buf, sem):
    slots, size, _ = tile_buf.shape
    count = used[0]
    chunk = 64

    def load(slot):
        return pltpu.make_async_copy(tiles.at[slot], tile_buf.at[slot], sem.at[slot])

    for slot in range(slots):

        @pl.when(slot < count)
        def _():
            load(slot).start()

    token[...] = jnp.zeros_like(token)

    def one_tile(slot, carry):
        load(slot).wait()

        def one_chunk(n, carry):
            rows = pl.ds(pl.multiple_of(n * chunk, chunk), chunk)
            counts = tile_buf[slot, rows, :].astype(f32)
            level = jnp.maximum(counts, 1.0)
            logs[slot, rows, :] = jnp.log(level)
            weight = 0.1 + 0.25 * (level * lax.rsqrt(level))
            weights[slot, rows, :] = jnp.where(counts > 0.0, weight, 0.0).astype(bf16)
            return carry

        lax.fori_loop(0, size // chunk, one_chunk, 0)
        return carry

    lax.fori_loop(0, count, one_tile, 0)


def levels(used, tiles):
    return pl.pallas_call(
        levels_kernel,
        out_shape=[shape(tiles.shape, f32), shape(tiles.shape, bf16), shape((8, 128), f32)],
        in_specs=[SMEM, HBM],
        out_specs=[VMEM] * 3,
        scratch_shapes=[
            pltpu.VMEM(tiles.shape, jnp.int32),
            pltpu.SemaphoreType.DMA((tiles.shape[0],)),
        ],
        compiler_params=pltpu.CompilerParams(vmem_limit_bytes=LEVELS),
        cost_estimate=cost(0, 12 << 20),
    )(used, tiles)


def join_kernel(sizes, *refs):
    parts, outs = list(refs[: sum(sizes)]), refs[-len(sizes) :]
    for out in outs:
        for n in range(out.shape[0]):
            part = parts.pop(0)
            out[n] = part[0] if len(part.shape) == 3 else part[...]


def join(parts, sizes, afters):
    piece = parts[0].shape[-2:]
    return list(
        pl.pallas_call(
            functools.partial(join_kernel, sizes),
            out_shape=[shape((size, *piece), bf16) for size in sizes],
            in_specs=[VMEM] * len(parts) + [ANY] * len(afters),
            out_specs=[VMEM] * len(sizes),
            compiler_params=pltpu.CompilerParams(vmem_limit_bytes=SMALL),
            cost_estimate=cost(0, 1 << 20),
        )(*parts, *afters)
    )


def marg_table(pieces, owners, part, size):
    table = jnp.zeros((MARG_ROWS, size), f32)
    for piece, owner in zip(pieces, owners):
        tail = piece[piece.shape[0] - MARG_ROWS :, :MARG_LANES]
        k = lax.broadcasted_iota(jnp.int32, (MARG_LANES, size), 0)
        at = lax.broadcasted_iota(jnp.int32, (MARG_LANES, size), 1)
        place = ((at == k + owner * part) & (k < part)).astype(bf16)
        table += jnp.dot(tail, place, preferred_element_type=f32)
    return table


def work_kernel(first, n_sides, n_row, n_col, row_owner, col_owner, *refs):
    refs = list(refs)

    def take(n):
        return [refs.pop(0) for _ in range(n)]

    listing, used, logs, weights = take(4)
    sides, col_in = take(n_sides), take(n_col)
    row_in = [side.at[n] for side in sides for n in range(side.shape[0])]
    if not first:
        left, right = take(2)
    keep, swap = take(2)
    col_out = take(n_col)
    if first:
        left, right = take(2)
    row_panel, row_turned, col_panel, grad_row, grad_turned, grad_col, even, odd = take(8)

    row_blocks, size, width = row_panel.shape
    col_blocks = col_panel.shape[0]
    row_part, col_part = size // n_row, size // n_col
    half = n_row // 2
    me_row, me_col = lax.axis_index("row"), lax.axis_index("col")
    row_owners = [me_col ^ k for k in row_owner]
    col_owners = [me_row ^ k for k in col_owner]
    row_zero, col_zero = me_row * row_blocks, me_col * col_blocks
    count = used[0]

    for pieces, owners, panel, part in (
        (row_in, row_owners, row_panel, row_part),
        (col_in, col_owners, col_panel, col_part),
    ):
        for piece, owner in zip(pieces, owners):
            start = pl.multiple_of(owner * part, part)
            for b in range(panel.shape[0]):
                panel[b, pl.ds(start, part), :] = piece[b * part : (b + 1) * part, :]

    if first:
        row_table = marg_table(row_in, row_owners, row_part, size).astype(bf16)
        for b in range(row_blocks):
            pick = (lax.broadcasted_iota(jnp.int32, (MARG_ROWS, 128), 0) == b).astype(bf16)
            left[b] = lax.dot_general(
                row_table, pick, (((0,), (0,)), ((), ())), preferred_element_type=f32
            )
        col_table = marg_table(col_in, col_owners, col_part, size)
        for b in range(col_blocks):
            right[b] = jnp.broadcast_to(col_table[b : b + 1, :], right.shape[1:])

    chunks = [slice(at, at + 256) for at in range(0, size, 256)]

    def place(slot):
        return listing[0, slot] - row_zero, listing[1, slot] - col_zero

    def make_signal(slot, rows, signal):
        i, j = place(slot)
        scores = lax.dot_general(
            row_panel[i, rows, :], col_panel[j], (((1,), (1,)), ((), ())), preferred_element_type=f32
        )
        marg_left = jnp.concatenate([left[i, rows, :]] * (size // 128), axis=1)
        shift = marg_left + right[j, 0:1, :] - logs[slot, rows, :]
        diff = (scores + shift).astype(bf16)
        weight = weights[slot, rows, :]
        half_one = jnp.asarray(0.5, bf16)
        flat = half_one * jnp.tanh(half_one * diff) + half_one
        signal[rows, :] = jnp.where(weight > 0, weight * diff, flat)

    def add_row(slot, rows, signal):
        i, j = place(slot)
        grad_row[i, rows, :] += jnp.dot(signal[rows, :], col_panel[j], preferred_element_type=f32)

    def add_col(slot, signal):
        i, j = place(slot)
        grad_turned[j] += jnp.dot(row_turned[i], signal[...], preferred_element_type=f32)

    def step(slot, before, now):
        for rows in chunks:
            make_signal(slot, rows, now)
            add_row(slot - 1, rows, before)
        add_col(slot - 1, before)

    pairs = (count - 1) // 2

    def pair(n, carry):
        step(2 * n + 1, even, odd)
        step(2 * n + 2, odd, even)
        return carry

    for rows in chunks:
        make_signal(0, rows, even)
    for b in range(row_blocks):
        row_turned[b] = row_panel[b].T
    grad_row[...] = jnp.zeros_like(grad_row)
    grad_turned[...] = jnp.zeros_like(grad_turned)
    lax.fori_loop(0, pairs, pair, 0)

    @pl.when(2 * pairs + 1 < count)
    def _():
        step(2 * pairs + 1, even, odd)

    for parity, signal in enumerate((even, odd)):

        @pl.when(lax.rem(count - 1, 2) == parity)
        def _():
            for rows in chunks:
                add_row(count - 1, rows, signal)
            add_col(count - 1, signal)

    for n in range(n_row):
        place, sibling = row_owner[n] >> 1, row_owner[n] & 1
        start = pl.multiple_of(row_owners[n] * row_part, row_part)
        piece = grad_row[:, pl.ds(start, row_part), :]
        if sibling:
            swap[place] = piece.astype(bf16)
        else:
            keep[place] = piece
    aligned = col_part % 128 == 0
    if not aligned:
        for b in range(col_blocks):
            grad_col[b] = grad_turned[b].astype(bf16).T
    for n in range(n_col):
        start = pl.multiple_of(col_owners[n] * col_part, col_part)
        if aligned:
            for b in range(col_blocks):
                col_out[n][b] = grad_turned[b, :, pl.ds(start, col_part)].astype(bf16).T
        else:
            col_out[n][...] = grad_col[:, pl.ds(start, col_part), :]


def work(listing, used, tabs, row_in, col_in, tables, row_owner, col_owner, dims):
    row_blocks, col_blocks, size, width = dims
    first = tables is None
    n_row, n_col = len(row_owner), len(col_owner)
    row_part, col_part = size // n_row, size // n_col
    half = n_row // 2
    outs = [
        shape((half, row_blocks, row_part, width), f32),
        shape((half, row_blocks, row_part, width), bf16),
    ] + [shape((col_blocks, col_part, width), bf16)] * n_col
    if first:
        outs += [shape((row_blocks, size, 128), f32), shape((col_blocks, 8, size), f32)]
    args = [listing, used, *tabs, *row_in, *col_in] + ([] if first else list(tables))
    res = pl.pallas_call(
        functools.partial(work_kernel, first, len(row_in), n_row, n_col, row_owner, col_owner),
        out_shape=outs,
        in_specs=[SMEM, SMEM] + [VMEM] * (len(args) - 2),
        out_specs=[VMEM] * len(outs),
        scratch_shapes=[
            pltpu.VMEM((row_blocks, size, width), bf16),
            pltpu.VMEM((row_blocks, width, size), bf16),
            pltpu.VMEM((col_blocks, size, width), bf16),
            pltpu.VMEM((row_blocks, size, width), f32),
            pltpu.VMEM((col_blocks, width, size), f32),
            pltpu.VMEM((col_blocks, size, width), bf16),
            pltpu.VMEM((size, size), bf16),
            pltpu.VMEM((size, size), bf16),
        ],
        compiler_params=pltpu.CompilerParams(vmem_limit_bytes=LARGE),
        cost_estimate=cost(8 * 6 * size * size * width, 16 << 20),
    )(*args)
    return res[0], res[1], res[2 : 2 + n_col], res[2 + n_col :]


def merge_kernel(n_held, keep, got, *refs):
    held, outs = refs[:n_held], refs[n_held:]
    for n in range(keep.shape[0]):
        outs[n][...] = (keep[n] + got[n].astype(f32)).astype(outs[n].dtype)
    for src, out in zip(held, outs[keep.shape[0] :]):
        out[...] = src[...]


def merge(keep, got, kept, held):
    n, *piece = keep.shape
    outs = [shape(tuple(piece), f32 if k in kept else bf16) for k in range(n)]
    outs += [shape(x.shape, x.dtype) for x in held]
    return pl.pallas_call(
        functools.partial(merge_kernel, len(held)),
        out_shape=outs,
        in_specs=[VMEM] * (2 + len(held)),
        out_specs=[VMEM] * len(outs),
        compiler_params=pltpu.CompilerParams(vmem_limit_bytes=SMALL),
        cost_estimate=cost(0, 2 << 20),
    )(keep, got, *held)


def add_kernel(n_parts, n_held, own, *refs):
    parts, held, outs = refs[:n_parts], refs[n_parts : n_parts + n_held], refs[n_parts + n_held :]
    total = own[...]
    for part in parts:
        total += part[...].astype(f32)
    outs[0][...] = total.astype(bf16)
    for src, out in zip(held, outs[1:]):
        out[...] = src[...]


def add(own, parts, held):
    return pl.pallas_call(
        functools.partial(add_kernel, len(parts), len(held)),
        out_shape=[shape(own.shape, bf16)] + [shape(x.shape, x.dtype) for x in held],
        in_specs=[VMEM] * (1 + len(parts) + len(held)),
        out_specs=[VMEM] * (1 + len(held)),
        compiler_params=pltpu.CompilerParams(vmem_limit_bytes=SMALL),
        cost_estimate=cost(0, 1 << 20),
    )(own, *parts, *held)


def update_kernel(n_parts, n_outs, emb, *refs):
    parts, outs = refs[:n_parts], refs[-n_outs:]
    total = parts[0][...].astype(f32)
    for part in parts[1:]:
        total += part[...].astype(f32)
    new = emb[...] - RATE * total
    outs[0][...] = new
    if len(outs) > 1:
        outs[1][...] = new.astype(bf16).reshape(outs[1].shape)


def update(emb, parts, afters, last):
    blocks, part, width = emb.shape
    outs = [shape(emb.shape, f32)]
    if not last:
        outs.append(shape((blocks * part, width), bf16))
    res = pl.pallas_call(
        functools.partial(update_kernel, len(parts), len(outs)),
        out_shape=outs,
        in_specs=[VMEM] * (1 + len(parts)) + [ANY] * len(afters),
        out_specs=[VMEM] * len(outs),
        compiler_params=pltpu.CompilerParams(vmem_limit_bytes=SMALL),
        cost_estimate=cost(0, 1 << 20),
    )(emb, *parts, *afters)
    return res if not last else (res[0], None)


def send(x, axis, count, mask):
    return lax.ppermute(x, axis, [(k, k ^ mask) for k in range(count)])


def shards(n_row_dev, n_col_dev, row_emb, col_emb, row_marg, col_marg, tile_list, tile_count, tile_data):
    listing = tile_list[0, 0].T
    used = tile_count[0]
    tiles = tile_data[0, 0]
    dims = (row_emb.shape[0], col_emb.shape[0], tiles.shape[-1], row_emb.shape[-1])
    half = n_col_dev // 2
    far = half // 2
    near = range(1, far)
    row_owner = [2 * k for k in range(half)] + [2 * k + 1 for k in range(half)]
    col_owner = list(range(n_row_dev))

    def hop(x, distance):
        return send(x, "col", n_col_dev, 2 * distance)

    row_pay, col_pay = pack(row_emb, row_marg, col_emb, col_marg)
    *tabs, tabs_made = levels(used, tiles)
    tables = None
    for substep in range(2):
        crossed = hop(row_pay, far)
        col_in = [col_pay] + [send(col_pay, "row", n_row_dev, k) for k in col_owner[1:]]
        if substep == 0:
            before_leg, before_swap, sizes = [tabs_made], col_in[1:-1], [1, far - 1, 1, far - 1]
        else:
            before_leg, before_swap, sizes = col_in[-1:], [], [far, 1, far - 1]
        (crossed,) = join([crossed], [1], before_leg)
        row_in = [row_pay] + [hop(row_pay, k) for k in near] + [crossed] + [hop(crossed, k) for k in near]
        row_in = join(row_in, sizes, before_swap)
        row_in += [send(piece, "col", n_col_dev, 1) for piece in row_in]
        keep, swap, col_out, made = work(
            listing, used, tabs, row_in, col_in, tables, row_owner, col_owner, dims
        )
        tables = tables or made
        held = col_out[-1:] if substep == 1 else []
        merged = merge(keep, send(swap, "col", n_col_dev, 1), (0, far), held)
        col_out = [*col_out[: len(col_out) - len(held)], *merged[half:]]
        relays = [hop(merged[far + k], k) for k in near]
        crossing, *straight = add(merged[far], relays, [merged[k] for k in near])
        col_parts = [col_out[0]] + [send(col_out[k], "row", n_row_dev, k) for k in col_owner[1:]]
        row_parts = [merged[0]] + [hop(x, k) for x, k in zip(straight, near)] + [hop(crossing, far)]
        col_emb, col_pay = update(col_emb, col_parts, [straight[0]], substep == 1)
        row_emb, row_pay = update(row_emb, row_parts, [col_pay if substep == 0 else straight[0]], substep == 1)
    return (row_emb, col_emb)


def solution(mesh):
    placed = (
        P("row", "col", None),
        P("col", "row", None),
        P("row", "col"),
        P("col", "row"),
        P("row", "col", None, None),
        P("row", "col"),
        P("row", "col", None, None, None),
    )
    return jax.shard_map(
        functools.partial(shards, mesh.shape["row"], mesh.shape["col"]),
        mesh=mesh,
        in_specs=placed,
        out_specs=(P("row", "col", None), P("col", "row", None)),
        check_vma=False,
    )
```
